32 devices in a mesh: section: 2 (over core), dp: 4 (over y, x), tensor: 4 (over z).
Axes of the slice: x: 2, y: 2, z: 4, core: 2. Of those that a mesh axis runs over, the one named last changes fastest.
Arguments:
- tokens: bfloat16 [8, 2048, 1024], P('dp', 'tensor'), may hold values from -6 to 6
- segment_ids: int32 [8, 2048], P('dp'), may hold values from 0 to 3, as said below
- cotangent: bfloat16 [8, 2048, 1024], P('dp', 'tensor'), may hold values from -6 to 6
- query_weight: bfloat16 [2, 1024, 1024], P('section', None, 'tensor'), may hold values from -0.1875 to 0.1875
- key_weight: bfloat16 [2, 1024, 1024], P('section', None, 'tensor'), may hold values from -0.1875 to 0.1875
- value_weight: bfloat16 [2, 1024, 1024], P('section', None, 'tensor'), may hold values from -0.1875 to 0.1875
- output_weight: bfloat16 [2, 1024, 1024], P('section', 'tensor'), may hold values from -0.75 to 0.75
- gate_weight: bfloat16 [2, 1024, 2816], P('section', None, 'tensor'), may hold values from -0.1875 to 0.1875
- up_weight: bfloat16 [2, 1024, 2816], P('section', None, 'tensor'), may hold values from -0.1875 to 0.1875
- down_weight: bfloat16 [2, 2816, 1024], P('section', 'tensor'), may hold values from -0.109375 to 0.109375
- attn_gain: float32 [2, 1024], P('section'), may hold values from 0.5 to 1.5
- mlp_gain: float32 [2, 1024], P('section'), may hold values from 0.5 to 1.5
Outputs:
- activations: bfloat16 [8, 2048, 1024], P('dp', 'tensor')
- input_grad: float32 [8, 2048, 1024], P('dp', 'tensor', 'section')
- grad_query: float32 [2, 1024, 1024], P('section', 'dp', 'tensor')
- grad_key: float32 [2, 1024, 1024], P('section', 'dp', 'tensor')
- grad_value: float32 [2, 1024, 1024], P('section', 'dp', 'tensor')
- grad_output: float32 [2, 1024, 1024], P('section', 'tensor', 'dp')
- grad_gate: float32 [2, 1024, 2816], P('section', 'dp', 'tensor')
- grad_up: float32 [2, 1024, 2816], P('section', 'dp', 'tensor')
- grad_down: float32 [2, 2816, 1024], P('section', 'tensor', 'dp')
- grad_attn_gain: float32 [2, 1024], P('section', ('dp', 'tensor'))
- grad_mlp_gain: float32 [2, 1024], P('section', ('dp', 'tensor'))
- grad_norm: float32 [2], P('section')
The draws below stay inside these ranges and needn't reach their ends.
Inputs may be any that keep to these rules, and one draw needn't show every extreme that they name: `segment_ids`: segment numbers never fall along a row; they are 0 at the first position and 3 at the last. In each group of 2 rows that one index of dp holds, one row drawn from the seed has a document that starts within the first sixteenth of 2048 positions and ends within the last sixteenth.
All inputs are finite; a program needn't handle non-finite values.
Results may differ from the reference program's by a relative error of at most 0.025.
Values may be sent and summed in bfloat16 or wider, within the bound.
No kernel may reach another device: no remote copies, remote signals or barrier semaphores. Data moves between devices by JAX's collectives and lax.ppermute only.
A program may use at most 320 MiB of HBM per device.

```python
import jax
import jax.numpy as jnp
from jax import lax

D = 1024
HEADS = 16
HEAD_DIM = 64
FF = 2816
SEQ = 2048
MB = 2
ROWS = 8


def draw_segment_ids(key, part):
    first_key, second_key, third_key, fourth_key = jax.random.split(key, 4)
    edge = max(SEQ // 16, 2)
    spread_cuts = jax.random.randint(first_key, (ROWS, 3), 1, SEQ)
    head_cut = jax.random.randint(second_key, (ROWS, 1), 1, edge)
    tail_cuts = jax.random.randint(third_key, (ROWS, 2), SEQ - edge, SEQ)
    long_cuts = jnp.concatenate([head_cut, tail_cuts], axis=1)
    chosen = jax.random.randint(fourth_key, (ROWS // MB,), 0, MB)
    row_slot = jnp.arange(ROWS, dtype=jnp.int32) % MB
    is_long = row_slot == jnp.repeat(chosen, MB)
    cuts = jnp.where(is_long[:, None], long_cuts, spread_cuts)
    positions = jnp.arange(SEQ, dtype=jnp.int32)
    return jnp.sum((cuts[:, None, :] <= positions[None, :, None]).astype(jnp.int32), axis=-1).astype(jnp.int32)


def level_of(rng, shape, cuts, low, top_value):
    loudness, own = 1.0, jax.random.fold_in(rng, 6)
    for dim, blocks in cuts:
        heights = jnp.exp(jax.random.uniform(jax.random.fold_in(own, dim), (blocks,), jnp.float32, low / len(cuts), top_value / len(cuts)))
        loudness = loudness * jnp.repeat(heights, shape[dim] // blocks).reshape([-1 if axis == dim else 1 for axis in range(len(shape))])
    return loudness


def normal_values(key, shape, scale, most, cuts=(), kind=jnp.bfloat16):
    entries = scale * jax.random.normal(key, shape, jnp.float32)
    if cuts:
        entries = entries * level_of(key, shape, cuts, -0.22, 0.18)
    return jnp.clip(entries, -most, most).astype(kind)


def setup_inputs(seed: int = 0) -> dict:
    keys = jax.random.split(jax.random.key(seed), 13)
    tokens = normal_values(keys[0], (ROWS, SEQ, D), 1.0, 6.0, ((0, 4), (1, 4)))
    segment_ids = draw_segment_ids(jax.random.fold_in(keys[12], 71), 0)
    cotangent = normal_values(keys[2], (ROWS, SEQ, D), 1.0, 6.0, ((0, 4), (1, 4)))
    query_weight = normal_values(keys[3], (2, D, D), D ** -0.5, 0.1875, ((0, 2), (2, 4)))
    key_weight = normal_values(keys[4], (2, D, D), D ** -0.5, 0.1875, ((0, 2), (2, 4)))
    value_weight = normal_values(keys[5], (2, D, D), D ** -0.5, 0.1875, ((0, 2), (2, 4)))
    output_weight = normal_values(keys[6], (2, D, D), (D // 16) ** -0.5, 0.75, ((0, 2), (1, 4)))
    gate_weight = normal_values(keys[7], (2, D, FF), D ** -0.5, 0.1875, ((0, 2), (2, 4)))
    up_weight = normal_values(keys[8], (2, D, FF), D ** -0.5, 0.1875, ((0, 2), (2, 4)))
    down_weight = normal_values(keys[9], (2, FF, D), FF ** -0.5, 0.109375, ((0, 2), (1, 4)))
    attn_gain = jnp.clip(1.0 + 0.1 * jax.random.normal(keys[10], (2, D), jnp.float32), 0.5, 1.5)
    mlp_gain = jnp.clip(1.0 + 0.1 * jax.random.normal(keys[11], (2, D), jnp.float32), 0.5, 1.5)
    return dict(tokens=tokens, segment_ids=segment_ids, cotangent=cotangent, query_weight=query_weight, key_weight=key_weight, value_weight=value_weight, output_weight=output_weight, gate_weight=gate_weight, up_weight=up_weight, down_weight=down_weight, attn_gain=attn_gain, mlp_gain=mlp_gain)


epsilon = 1e-05
rope_base = 10000.0
masked_score = -1e+30

@jax.custom_vjp
def low(v):
    return lax.optimization_barrier(v.astype(jnp.bfloat16)).astype(jnp.float32)

@jax.custom_vjp
def low_back(v):
    return v

def low_keep(v):
    return (low(v), None)

def low_pass(kept, grad):
    return (grad,)

def back_keep(v):
    return (v, None)

def back_low(kept, grad):
    return (low(grad),)
low.defvjp(low_keep, low_pass)
low_back.defvjp(back_keep, back_low)

def matmul(left, right):
    return jnp.dot(left, right, precision=lax.Precision.HIGHEST, preferred_element_type=jnp.float32)

def rms_norm(inputs, gain):
    return inputs * lax.rsqrt(lax.optimization_barrier(jnp.mean(inputs * inputs, axis=-1, keepdims=True)) + epsilon) * gain

def rope_tables(length, width):
    half_width = width // 2
    frequency = rope_base ** (-jnp.arange(half_width, dtype=jnp.float32) / half_width)
    angles = jnp.arange(length, dtype=jnp.float32)[:, None] * frequency[None, :]
    return (jnp.cos(angles), jnp.sin(angles))

def rotate(tensor, cosine_table, sine_table, direction):
    half_width = tensor.shape[-1] // 2
    first_half = tensor[..., :half_width]
    second_half = tensor[..., half_width:]
    cosine = cosine_table[:, None, :]
    sine_part = sine_table[:, None, :] * direction
    return jnp.concatenate([first_half * cosine - second_half * sine_part, second_half * cosine + first_half * sine_part], axis=-1)

def attend(query_rows, key_rows, value_rows, segments):
    length = query_rows.shape[0]
    block_rows = min(512, length)
    score_scale = query_rows.shape[-1] ** (-0.5)
    key_places = jnp.arange(length, dtype=jnp.int32)

    def one_block(block_index):
        row_start = (block_index * block_rows).astype(jnp.int32)
        query_block = lax.dynamic_slice_in_dim(query_rows, row_start, block_rows, 0)
        query_segments = lax.dynamic_slice_in_dim(segments, row_start, block_rows, 0)
        query_places = row_start + jnp.arange(block_rows, dtype=jnp.int32)
        allowed = (query_segments[:, None] == segments[None, :]) & (key_places[None, :] <= query_places[:, None])
        scores = jnp.einsum('qhd,khd->hqk', query_block, key_rows, precision=lax.Precision.HIGHEST) * score_scale
        scores = low_back(scores)
        scores = jnp.where(allowed[None], scores, masked_score)
        row_max = lax.optimization_barrier(jnp.max(scores, axis=-1, keepdims=True))
        exponent = jnp.exp(scores - row_max)
        weights_low = low(exponent / lax.optimization_barrier(jnp.sum(exponent, axis=-1, keepdims=True)))
        return jnp.einsum('hqk,khd->qhd', weights_low, value_rows, precision=lax.Precision.HIGHEST)
    blocks = lax.map(jax.checkpoint(one_block), jnp.arange(length // block_rows, dtype=jnp.int32))
    return blocks.reshape(query_rows.shape)

def layer(inputs, segments, weights, first_values, mix_weight):
    w_query, w_key, w_value, w_output, w_gate, w_up, w_down, gain_attn, gain_mlp = weights
    length = inputs.shape[0]
    cosine_table, sine_table = rope_tables(length, HEAD_DIM)
    shape_heads = (length, HEADS, HEAD_DIM)
    normed = low(rms_norm(inputs, gain_attn))
    query_rows = low(rotate(low_back(matmul(normed, w_query)).reshape(shape_heads), cosine_table, sine_table, 1.0))
    key_rows = low(rotate(low_back(matmul(normed, w_key)).reshape(shape_heads), cosine_table, sine_table, 1.0))
    raw_values = low_back(matmul(normed, w_value))
    mixed_values = low((1.0 - mix_weight) * raw_values + mix_weight * first_values)
    attended = attend(query_rows, key_rows, mixed_values.reshape(shape_heads), segments)
    attended = low_back(low(attended.reshape(length, HEADS * HEAD_DIM)))
    hidden_state = inputs + low_back(matmul(attended, w_output))
    normed_mlp = low(rms_norm(hidden_state, gain_mlp))
    gate_pre = low_back(matmul(normed_mlp, w_gate))
    up_pre = low_back(matmul(normed_mlp, w_up))
    product = low(jax.nn.silu(gate_pre) * up_pre)
    layer_out = hidden_state + low_back(matmul(product, w_down))
    return (layer_out, mixed_values)

def row_forward(params, inputs, segments):
    first_layer = tuple((param[0] for param in params))
    later_layer = tuple((param[1] for param in params))
    empty_values = jnp.zeros((inputs.shape[0], HEADS * HEAD_DIM), inputs.dtype)
    first_out, first_values = layer(inputs, segments, first_layer, empty_values, 0.0)
    later_out, unused = layer(low(first_out), segments, later_layer, first_values, 0.5)
    return later_out

def reference(tokens, segment_ids, cotangent, query_weight, key_weight, value_weight, output_weight, gate_weight, up_weight, down_weight, attn_gain, mlp_gain):
    params = (query_weight.astype(jnp.float32), key_weight.astype(jnp.float32), value_weight.astype(jnp.float32), output_weight.astype(jnp.float32), gate_weight.astype(jnp.float32), up_weight.astype(jnp.float32), down_weight.astype(jnp.float32), attn_gain.astype(jnp.float32), mlp_gain.astype(jnp.float32))
    inputs = tokens.astype(jnp.float32)
    row_step = jax.checkpoint(row_forward)

    def forward(all_inputs, weights):
        return lax.map(lambda row_pair: row_step(weights, row_pair[0], row_pair[1]), (all_inputs, segment_ids))
    outputs, pullback = jax.vjp(forward, inputs, params)
    input_grad, weight_grads = pullback(cotangent.astype(jnp.float32))
    squares = jnp.stack([lax.optimization_barrier(jnp.sum((gradient * gradient).reshape(2, -1), axis=1)) for gradient in weight_grads])
    grad_norm = jnp.sqrt(lax.optimization_barrier(jnp.sum(squares, axis=0)))
    return (outputs.astype(jnp.bfloat16), input_grad, weight_grads[0], weight_grads[1], weight_grads[2], weight_grads[3], weight_grads[4], weight_grads[5], weight_grads[6], weight_grads[7], weight_grads[8], grad_norm)
```

```python
import functools
import math

import jax
import jax.numpy as jnp
from jax import lax
from jax.experimental import pallas as pl
from jax.experimental.pallas import tpu as pltpu
from jax.sharding import PartitionSpec as P

HEAD = 64
EPS = 1e-05
ROPE_BASE = 10000.0
BIG = 1e30
LOG2E = math.log2(math.e)
BF = jnp.bfloat16
F32 = jnp.float32
ALL = ("section", "dp", "tensor")
VMEM_LIMIT = 60 * 1024 * 1024

COL_OF_REL, ABS_OF_REL, REL_OF_ABS, REL_OF_RING, REL_OF_COL, REL_OF_DP = 0, 8, 16, 24, 32, 40


def nn(a, b):
    return jnp.dot(a, b, preferred_element_type=F32)


def nt(a, b):
    return lax.dot_general(a, b, (((1,), (1,)), ((), ())), preferred_element_type=F32)


def tn(a, b):
    return lax.dot_general(a, b, (((0,), (0,)), ((), ())), preferred_element_type=F32)


def vmem_spec():
    return pl.BlockSpec(memory_space=pltpu.VMEM)


def any_spec():
    return pl.BlockSpec(memory_space=pl.ANY)


def smem_spec():
    return pl.BlockSpec(memory_space=pltpu.SMEM)


def sds(shape, dtype):
    return jax.ShapeDtypeStruct(shape, dtype)


def cost(flops, moved):
    return pl.CostEstimate(flops=int(flops), bytes_accessed=int(moved), transcendentals=0)


def params(**more):
    return pltpu.CompilerParams(vmem_limit_bytes=VMEM_LIMIT, **more)


def piece_plan(sources, rows_from, rows):
    plan = []
    if len(sources) == 1:
        return [(0, rows_from, 0, rows, None)]
    half = sources[3].shape[0]
    for side in range(2):
        for place in range(3):
            plan.append((side * 5 + place, rows_from, 0, rows, side * 4 + place))
        top = max(0, min(half, rows_from + rows) - rows_from)
        if top > 0:
            plan.append((side * 5 + 3, rows_from, 0, top, side * 4 + 3))
        if rows - top > 0:
            start = max(rows_from, half)
            plan.append((side * 5 + 4, start - half, start - rows_from, rows - top, side * 4 + 3))
    return plan


def weight_copies(meta, plan, refs, buffer, sems, first_sem):
    copies = []
    for number, (operand, src_row, dst_row, count, rel) in enumerate(plan):
        src = refs[operand].at[pl.ds(src_row, count), :]
        if rel is None:
            dst = buffer.at[pl.ds(dst_row, count), :]
        else:
            offset = pl.multiple_of(meta[COL_OF_REL + rel] * 128, 128)
            dst = buffer.at[pl.ds(dst_row, count), pl.ds(offset, 128)]
        copies.append(pltpu.make_async_copy(src, dst, sems.at[first_sem + number]))
    return copies


def swap_halves(tile):
    lane = lax.broadcasted_iota(jnp.int32, tile.shape, 1)
    return jnp.where(lane % HEAD < HEAD // 2, pltpu.roll(tile, 128 - HEAD // 2, 1), pltpu.roll(tile, HEAD // 2, 1))


def qkv_kernel(blocks, later, meta, *refs):
    a_refs = refs[:blocks]
    w_ref, cos_ref, sin_ref, extq_ref, extk_ref = refs[blocks : blocks + 5]
    rest = refs[blocks + 5 :]
    if later:
        first_ref, rest = rest[0], rest[1:]
    q_ref, k_ref, v_ref = rest
    length = a_refs[0].shape[0]
    cols = w_ref.shape[1] // 3
    lane = lax.broadcasted_iota(jnp.int32, (length, 128), 1)
    low = lane < HEAD
    ones_even = ((lane >= HEAD + 4) & (lane < HEAD + 7)).astype(F32)
    ones_odd = ((lane >= 4) & (lane < 7)).astype(F32)
    for i in range(blocks):
        start = pl.multiple_of(meta[ABS_OF_REL + i] * length, length)
        rows = pl.ds(start, length)
        a = a_refs[i][...]
        cosine, sine = cos_ref[rows, :], sin_ref[rows, :]
        for part, out in ((0, q_ref), (1, k_ref), (2, v_ref)):
            whole = nn(a, w_ref[:, part * cols : (part + 1) * cols])
            for pair in range(cols // 128):
                tile = whole[:, pair * 128 : (pair + 1) * 128]
                if part < 2:
                    tile = tile * cosine + swap_halves(tile) * sine
                    ext = extq_ref if part == 0 else extk_ref
                    if part == 0:
                        tile = tile * (LOG2E * HEAD**-0.5)
                    even_ext = ext[rows, :128].astype(F32)
                    odd_ext = ext[rows, 128:].astype(F32)
                else:
                    if later:
                        first = jnp.where(
                            low,
                            first_ref[2 * pair, rows, :].astype(F32),
                            first_ref[2 * pair + 1, rows, :].astype(F32),
                        )
                        tile = 0.5 * tile + 0.5 * first
                    even_ext, odd_ext = ones_even, ones_odd
                out[2 * pair, rows, :] = jnp.where(low, tile, even_ext).astype(BF)
                out[2 * pair + 1, rows, :] = jnp.where(low, odd_ext, tile).astype(BF)


def project(meta, a_blocks, w, tables, exts, first):
    blocks, (length, width) = len(a_blocks), a_blocks[0].shape
    cols = w.shape[1] // 3
    heads = cols // HEAD
    seq = blocks * length
    out = sds((heads, seq, 128), BF)
    later = first is not None
    operands = [meta, *a_blocks, w, *tables, *exts] + ([first] if later else [])
    return pl.pallas_call(
        functools.partial(qkv_kernel, blocks, later),
        out_shape=(out, out, out),
        in_specs=[smem_spec()] + [vmem_spec()] * (len(operands) - 1),
        out_specs=(vmem_spec(),) * 3,
        compiler_params=params(),
        cost_estimate=cost(2 * seq * width * cols * 3, seq * width * 2 + 8e6),
        name="project",
    )(*operands)


def project_back_kernel(blocks, dp_blocks, meta, *refs):
    a_refs = refs[:blocks]
    dq_ref, dk_ref, dv_ref, w_ref = refs[blocks : blocks + 4]
    da_refs = refs[blocks + 4 : 2 * blocks + 4]
    dw_ref, acc_ref = refs[2 * blocks + 4 :]
    length, width = a_refs[0].shape
    cols = dq_ref.shape[1]
    for i in range(blocks):
        start = pl.multiple_of(meta[ABS_OF_REL + i] * length, length)
        rows = pl.ds(start, length)
        grads = jnp.concatenate([dq_ref[rows, :], dk_ref[rows, :], dv_ref[rows, :]], axis=1)
        da_refs[i][...] = nt(grads, w_ref[...]).astype(BF)
        term = tn(a_refs[i][...], grads)
        if i == 0:
            acc_ref[...] = term
        else:
            acc_ref[...] += term
    size = width // dp_blocks
    for j in range(dp_blocks):
        dw_ref[meta[REL_OF_DP + j]] = acc_ref[j * size : (j + 1) * size, :].astype(BF)


def project_back(meta, a_blocks, grads, w, dp_blocks):
    blocks, (length, width) = len(a_blocks), a_blocks[0].shape
    cols = w.shape[1]
    seq = blocks * length
    results = pl.pallas_call(
        functools.partial(project_back_kernel, blocks, dp_blocks),
        out_shape=tuple(sds((length, width), BF) for _ in range(blocks))
        + (sds((dp_blocks, width // dp_blocks, cols), BF),),
        in_specs=[smem_spec()] + [vmem_spec()] * (blocks + 4),
        out_specs=(vmem_spec(),) * (blocks + 1),
        scratch_shapes=[pltpu.VMEM((width, cols), F32)],
        compiler_params=params(),
        cost_estimate=cost(4 * seq * width * cols, seq * width * 4 + 8e6),
        name="project_back",
    )(meta, *a_blocks, *grads, w)
    return results[:blocks], results[blocks]


def three_parts(value):
    high = value.astype(BF).astype(F32)
    middle = (value - high).astype(BF).astype(F32)
    return high, middle, value - high - middle


def with_parts(base, value, odd):
    lane = lax.broadcasted_iota(jnp.int32, base.shape, 1)
    offset = 4 if odd else HEAD + 4
    high, middle, rest = three_parts(value)
    out = jnp.where(lane == offset, high, base)
    out = jnp.where(lane == offset + 1, middle, out)
    return jnp.where(lane == offset + 2, rest, out)


def attend_kernel(block, meta, q_ref, k_ref, v_ref, o_ref, ql_ref):
    seq = q_ref.shape[1]
    length = o_ref.shape[1]
    lane = lax.broadcasted_iota(jnp.int32, (block, 128), 1)
    low = lane < HEAD
    row = lax.broadcasted_iota(jnp.int32, (block, block), 0)
    col = lax.broadcasted_iota(jnp.int32, (block, block), 1)
    causal = col <= row
    for i in range(seq // block):
        rows = slice(i * block, (i + 1) * block)
        results = []
        for e in range(2):
            q = q_ref[e, rows, :]
            scores = []
            if i > 0:
                scores.append(nt(q, k_ref[e, : i * block, :]))
            scores.append(jnp.where(causal, nt(q, k_ref[e, rows, :]), -BIG))
            top = scores[-1].max(axis=1, keepdims=True)
            if i > 0:
                top = jnp.maximum(top, scores[0].max(axis=1, keepdims=True))
            total = nn(jnp.exp2(scores[-1] - top).astype(BF), v_ref[e, rows, :])
            if i > 0:
                total += nn(jnp.exp2(scores[0] - top).astype(BF), v_ref[e, : i * block, :])
            place = 4 if e else HEAD + 4
            weight = total[:, place : place + 1]
            results.append(total / weight)
            ql_ref[e, rows, :] = with_parts(q.astype(F32), -(top + jnp.log2(weight)), e == 1).astype(BF)
        offset = (i * block) % length
        o_ref[meta[REL_OF_ABS + (i * block) // length], offset : offset + block, :] = jnp.where(
            low, results[0], results[1]
        ).astype(BF)


def attend(meta, q, k, v, blocks):
    heads, seq, _ = q.shape
    pairs = heads // 2
    length = seq // blocks
    head_spec = pl.BlockSpec((2, seq, 128), lambda p: (p, 0, 0))
    return pl.pallas_call(
        functools.partial(attend_kernel, min(256, length)),
        grid=(pairs,),
        out_shape=(sds((blocks, length, pairs * 128), BF), sds(q.shape, BF)),
        in_specs=[smem_spec(), head_spec, head_spec, head_spec],
        out_specs=(pl.BlockSpec((blocks, length, 128), lambda p: (0, 0, p)), head_spec),
        compiler_params=params(),
        cost_estimate=cost(heads * seq * seq * 8 * HEAD, 8e6),
        name="attend",
    )(meta, q, k, v)


def attend_back_kernel(block, blocks, later, meta, q_ref, k_ref, v_ref, o_ref, *refs):
    do_refs = refs[:blocks]
    cos_ref, sin_ref = refs[blocks : blocks + 2]
    rest = refs[blocks + 2 :]
    if not later:
        first_ref, rest = rest[0], rest[1:]
    dq_ref, dk_ref, dv_ref = rest[:3]
    rest = rest[3:]
    if later:
        first_out, rest = rest[0], rest[1:]
    do_scr, dq_scr, dk_scr, dv_scr = rest
    seq = q_ref.shape[1]
    length = o_ref.shape[1]
    lane = lax.broadcasted_iota(jnp.int32, (length, 128), 1)
    low = lane < HEAD
    for i in range(blocks):
        start = pl.multiple_of(meta[ABS_OF_REL + i] * length, length)
        rows = pl.ds(start, length)
        do = do_refs[i][...].astype(F32)
        product = do * o_ref[i].astype(F32)
        for e in range(2):
            mine = low if e == 0 else jnp.logical_not(low)
            delta = jnp.sum(jnp.where(mine, product, 0.0), axis=1, keepdims=True)
            do_scr[e, rows, :] = with_parts(jnp.where(mine, do, 0.0), -delta, e == 1).astype(BF)
    dk_scr[...] = jnp.zeros_like(dk_scr)
    dv_scr[...] = jnp.zeros_like(dv_scr)
    key_row = lax.broadcasted_iota(jnp.int32, (block, block), 0)
    query_col = lax.broadcasted_iota(jnp.int32, (block, block), 1)
    causal = key_row <= query_col
    for e in range(2):
        for i in range(seq // block):
            rows = slice(i * block, (i + 1) * block)
            q = q_ref[e, rows, :]
            do = do_scr[e, rows, :]
            spans = [(i * block, (i + 1) * block, True)]
            spans += [(j, min(j + 512, i * block), False) for j in range(0, i * block, 512)]
            dq = None
            for lo, hi, diagonal in spans:
                keys = k_ref[e, lo:hi, :]
                scores = nt(keys, q)
                if diagonal:
                    scores = jnp.where(causal, scores, -BIG)
                prob = jnp.exp2(scores)
                ds = (prob * nt(v_ref[e, lo:hi, :], do)).astype(BF)
                dv_scr[e, lo:hi, :] += nn(prob.astype(BF), do)
                dk_scr[e, lo:hi, :] += nn(ds, q)
                term = tn(ds, keys)
                dq = term if dq is None else dq + term
            dq_scr[e, rows, :] = dq
    for i in range(blocks):
        rows = slice(i * length, (i + 1) * length)
        cosine, sine = cos_ref[rows, :], sin_ref[rows, :]
        dq = jnp.where(low, dq_scr[0, rows, :], dq_scr[1, rows, :]) * (HEAD**-0.5)
        dk = jnp.where(low, dk_scr[0, rows, :], dk_scr[1, rows, :]) * (1.0 / LOG2E)
        dv = jnp.where(low, dv_scr[0, rows, :], dv_scr[1, rows, :])
        dq_ref[rows, :] = (dq * cosine - swap_halves(dq) * sine).astype(BF)
        dk_ref[rows, :] = (dk * cosine - swap_halves(dk) * sine).astype(BF)
        if later:
            dv_ref[rows, :] = (0.5 * dv).astype(BF)
            first_out[rows, :] = 0.5 * dv
        else:
            dv_ref[rows, :] = (dv + first_ref[rows, :]).astype(BF)


def attend_back(meta, q, k, v, o, do_blocks, tables, first):
    heads, seq, _ = q.shape
    pairs = heads // 2
    blocks, length, cols = o.shape
    later = first is None
    head_spec = pl.BlockSpec((2, seq, 128), lambda p: (p, 0, 0))
    col_spec = pl.BlockSpec((seq, 128), lambda p: (0, p))
    table_spec = pl.BlockSpec((seq, 128), lambda p: (0, 0))
    out = sds((seq, cols), BF)
    return pl.pallas_call(
        functools.partial(attend_back_kernel, min(256, length), blocks, later),
        grid=(pairs,),
        out_shape=(out, out, out) + ((sds((seq, cols), F32),) if later else ()),
        in_specs=[smem_spec(), head_spec, head_spec, head_spec]
        + [pl.BlockSpec((blocks, length, 128), lambda p: (0, 0, p))]
        + [pl.BlockSpec((length, 128), lambda p: (0, p))] * blocks
        + [table_spec] * 2
        + ([] if later else [col_spec]),
        out_specs=(col_spec,) * (4 if later else 3),
        scratch_shapes=[
            pltpu.VMEM((2, seq, 128), BF),
            pltpu.VMEM((2, seq, 128), F32),
            pltpu.VMEM((2, seq, 128), F32),
            pltpu.VMEM((2, seq, 128), F32),
        ],
        compiler_params=params(),
        cost_estimate=cost(heads * seq * seq * 20 * HEAD, 12e6),
        name="attend_back",
    )(meta, q, k, v, o, *do_blocks, *tables, *([] if later else [first]))


def mlp_kernel(blocks, counts, plans, meta, x_ref, gain_ref, *refs):
    o_refs, refs = refs[:blocks], refs[blocks:]
    sources = []
    for count in counts:
        sources.append(refs[:count])
        refs = refs[count:]
    y_ref, h_ref, b_ref, g_ref, u_ref, w_ref, o_scr, sems = refs
    copies, number = [], 0
    for k in range(blocks):
        group = weight_copies(meta, plans[k], sources[k], w_ref.at[k], sems, number)
        number += len(group)
        for copy in group:
            copy.start()
        copies.append(group)
    rows_o = o_refs[0].shape[1]
    hidden = g_ref.shape[2]
    for i in range(blocks):
        o_scr[i] = o_refs[i][...]
    h_ref[...] = x_ref[...].astype(F32)
    for k in range(blocks):
        for copy in copies[k]:
            copy.wait()
        h_ref[...] += nn(o_scr[meta[REL_OF_RING + k]], w_ref[k, :rows_o, :])
    h = h_ref[...]
    inverse = lax.rsqrt(jnp.mean(h * h, axis=1, keepdims=True) + EPS)
    b_ref[...] = (h * inverse * gain_ref[...]).astype(BF)
    total = None
    for k in range(blocks):
        b = b_ref[...]
        g = nt(b, w_ref[k, rows_o : rows_o + hidden, :])
        u = nt(b, w_ref[k, rows_o + hidden : rows_o + 2 * hidden, :])
        g_ref[k] = g.astype(BF)
        u_ref[k] = u.astype(BF)
        m = (g * jax.nn.sigmoid(g) * u).astype(BF)
        term = nn(m, w_ref[k, rows_o + 2 * hidden :, :])
        total = term if total is None else total + term
    y_ref[...] = (h_ref[...] + total).astype(BF)


def flatten(groups):
    return [item for group in groups for item in group]


def mlp_forward(meta, x, gain, o_blocks, weights, hidden):
    blocks, (length, cols) = len(o_blocks), o_blocks[0].shape
    width = x.shape[1]
    rows = cols + 3 * hidden
    plans = [piece_plan(source, 0, rows) for source in weights]
    saved = sds((blocks, length, hidden), BF)
    return pl.pallas_call(
        functools.partial(mlp_kernel, blocks, [len(w) for w in weights], plans),
        out_shape=(sds((length, width), BF), sds((length, width), F32), sds((length, width), BF), saved, saved),
        in_specs=[smem_spec()]
        + [vmem_spec()] * (2 + blocks)
        + [any_spec()] * sum(len(w) for w in weights),
        out_specs=(vmem_spec(),) * 5,
        scratch_shapes=[
            pltpu.VMEM((blocks, rows, width), BF),
            pltpu.VMEM((blocks, length, cols), BF),
            pltpu.SemaphoreType.DMA((sum(len(p) for p in plans),)),
        ],
        compiler_params=params(),
        cost_estimate=cost(2 * length * width * rows * blocks, rows * width * 2 * blocks + 12e6),
        name="mlp",
    )(meta, x, gain, *o_blocks, *flatten(weights))


def mlp_back_kernel(quarters, counts, plans, first, meta, dy_ref, b_ref, g_ref, u_ref, *refs):
    if not first:
        db_in, refs = refs[0], refs[1:]
    sources = []
    for count in counts:
        sources.append(refs[:count])
        refs = refs[count:]
    number = len(quarters)
    outs, refs = refs[: 2 * number], refs[2 * number :]
    db_ref, w_ref, grad_scr, sems, out_sems = refs
    copies, placed = [], 0
    for n in range(number):
        group = weight_copies(meta, plans[n], sources[n], w_ref.at[n], sems, placed)
        placed += len(group)
        for copy in group:
            copy.start()
        copies.append(group)
    hidden = g_ref.shape[2]
    if first:
        db_ref[...] = jnp.zeros_like(db_ref)
    else:
        db_ref[...] = db_in[...]
    sends = []
    for n, k in enumerate(quarters):
        for copy in copies[n]:
            copy.wait()
        dy = dy_ref[...]
        b = b_ref[...]
        dm = nt(dy, w_ref[n, 2 * hidden :, :])
        g = g_ref[k].astype(F32)
        u = u_ref[k].astype(F32)
        gate = jax.nn.sigmoid(g)
        active = g * gate
        m = (active * u).astype(BF)
        dg = (dm * u * gate * (1.0 + g * (1.0 - gate))).astype(BF)
        du = (dm * active).astype(BF)
        db_ref[...] += nn(dg, w_ref[n, :hidden, :]) + nn(du, w_ref[n, hidden : 2 * hidden, :])
        for part, (left, right) in enumerate(((dg, b), (du, b), (m, dy))):
            grad = tn(left, right).astype(BF)
            for j in range(grad.shape[1] // 128):
                grad_scr[n, meta[REL_OF_COL + j], part * hidden : (part + 1) * hidden, :] = grad[
                    :, j * 128 : (j + 1) * 128
                ]
        for side in range(2):
            copy = pltpu.make_async_copy(
                grad_scr.at[n, pl.ds(4 * side, 4)], outs[2 * n + side], out_sems.at[2 * n + side]
            )
            copy.start()
            sends.append(copy)
    for copy in sends:
        copy.wait()


def mlp_backward(meta, dy, b, g, u, db, weights, quarters, rows_from):
    blocks, length, hidden = g.shape
    width = b.shape[1]
    rows = 3 * hidden
    chosen = [weights[k] for k in quarters]
    plans = [piece_plan(source, rows_from, rows) for source in chosen]
    number = len(quarters)
    first = db is None
    results = pl.pallas_call(
        functools.partial(mlp_back_kernel, quarters, [len(w) for w in chosen], plans, first),
        out_shape=tuple(sds((4, rows, 128), BF) for _ in range(2 * number)) + (sds((length, width), F32),),
        in_specs=[smem_spec()]
        + [vmem_spec()] * (4 if first else 5)
        + [any_spec()] * sum(len(w) for w in chosen),
        out_specs=(any_spec(),) * (2 * number) + (vmem_spec(),),
        scratch_shapes=[
            pltpu.VMEM((number, rows, width), BF),
            pltpu.VMEM((number, 8, rows, 128), BF),
            pltpu.SemaphoreType.DMA((sum(len(p) for p in plans),)),
            pltpu.SemaphoreType.DMA((2 * number,)),
        ],
        compiler_params=params(),
        cost_estimate=cost(4 * length * width * rows * number, rows * width * 4 * number + 8e6),
        name="mlp_back",
    )(meta, dy, b, g, u, *([] if first else [db]), *flatten(chosen))
    return results[: 2 * number], results[2 * number]


def norm_back(values, gain, grads):
    inverse = lax.rsqrt(jnp.mean(values * values, axis=1, keepdims=True) + EPS)
    normed = values * inverse
    scaled = grads * gain
    gain_grad = jnp.sum(grads * normed, axis=0, keepdims=True)
    return inverse * (scaled - normed * jnp.mean(scaled * normed, axis=1, keepdims=True)), gain_grad


def middle_kernel(blocks, counts, plans, meta, dy_ref, db_ref, h_ref, gain_ref, *refs):
    o_refs, refs = refs[:blocks], refs[blocks:]
    sources = []
    for count in counts:
        sources.append(refs[:count])
        refs = refs[count:]
    dh_ref, gain_out, do_ref, own_ref, sib_ref, w_ref, o_scr, grad_scr, sems, out_sems = refs
    copies, number = [], 0
    for k in range(blocks):
        group = weight_copies(meta, plans[k], sources[k], w_ref.at[k], sems, number)
        number += len(group)
        for copy in group:
            copy.start()
        copies.append(group)
    cols = o_refs[0].shape[1]
    for i in range(blocks):
        o_scr[i] = o_refs[i][...]
    part, gain_grad = norm_back(h_ref[...], gain_ref[...], db_ref[...])
    dh = dy_ref[...].astype(F32) + part
    dh_ref[...] = dh
    gain_out[...] = gain_grad
    low = dh.astype(BF)
    for k in range(blocks):
        for copy in copies[k]:
            copy.wait()
        place = meta[REL_OF_RING + k]
        do_ref[place] = nt(low, w_ref[k]).astype(BF)
        grad = tn(o_scr[place], low).astype(BF)
        for j in range(grad.shape[1] // 128):
            grad_scr[meta[REL_OF_COL + j], k * cols : (k + 1) * cols, :] = grad[:, j * 128 : (j + 1) * 128]
    sends = []
    for side, out in enumerate((own_ref, sib_ref)):
        copy = pltpu.make_async_copy(grad_scr.at[pl.ds(4 * side, 4)], out, out_sems.at[side])
        copy.start()
        sends.append(copy)
    for copy in sends:
        copy.wait()


def middle(meta, dy, db, h, gain, o_blocks, weights):
    blocks, (length, cols) = len(o_blocks), o_blocks[0].shape
    width = h.shape[1]
    plans = [piece_plan(source, 0, cols) for source in weights]
    half = sds((4, blocks * cols, 128), BF)
    return pl.pallas_call(
        functools.partial(middle_kernel, blocks, [len(w) for w in weights], plans),
        out_shape=(sds((length, width), F32), sds((1, width), F32), sds((blocks, length, cols), BF), half, half),
        in_specs=[smem_spec()]
        + [vmem_spec()] * (4 + blocks)
        + [any_spec()] * sum(len(w) for w in weights),
        out_specs=(vmem_spec(),) * 3 + (any_spec(),) * 2,
        scratch_shapes=[
            pltpu.VMEM((blocks, cols, width), BF),
            pltpu.VMEM((blocks, length, cols), BF),
            pltpu.VMEM((8, blocks * cols, 128), BF),
            pltpu.SemaphoreType.DMA((sum(len(p) for p in plans),)),
            pltpu.SemaphoreType.DMA((2,)),
        ],
        compiler_params=params(),
        cost_estimate=cost(4 * length * width * cols * blocks, 16e6),
        name="middle",
    )(meta, dy, db, h, gain, *o_blocks, *flatten(weights))


def add_low(*terms):
    total = terms[0].astype(F32)
    for term in terms[1:]:
        total = total + term.astype(F32)
    return total.astype(BF)


class Links:
    def __init__(self):
        self.T = lax.axis_size("tensor")
        self.DP = lax.axis_size("dp")
        self.G = self.T // 2
        self.s = lax.axis_index("section")
        self.d = lax.axis_index("dp")
        self.z = lax.axis_index("tensor")
        self.r = self.z // self.G
        self.c = self.z % self.G
        self.home = self.s == self.r
        self.planar = self.DP == 4
        self.order = [0] + list(range(1, self.T, 2)) + list(range(self.T - 2, 0, -2))

    def sibling(self, x):
        return lax.ppermute(x, "section", [(0, 1), (1, 0)])

    def ring(self, x):
        order = self.order
        return lax.ppermute(x, "tensor", [(order[i], order[(i + 1) % self.T]) for i in range(self.T)])

    def along(self, x, bit):
        return lax.ppermute(x, "dp", [(i, i ^ bit) for i in range(self.DP)])

    def along_away(self, x, bit):
        pairs = []
        for d in range(self.DP):
            for z in range(self.T):
                s = 1 - z // self.G
                pairs.append(tuple((s * self.DP + e) * self.T + z for e in (d, d ^ bit)))
        return lax.ppermute(x, ALL, pairs)

    def partner(self, x, from_home):
        pairs = []
        for s in range(2):
            for z in range(self.T):
                if (z // self.G == s) == from_home:
                    pairs.append((s * self.T + z, s * self.T + (z + self.G) % self.T))
        return lax.ppermute(x, ("section", "tensor"), pairs)

    def shift(self, x, k):
        pairs = [(z, z // self.G * self.G + (z + k) % self.G) for z in range(self.T)]
        return lax.ppermute(x, "tensor", pairs)

    def spread(self, x):
        mine = [x] + [self.shift(x, -k) for k in range(1, self.G)]
        return mine + [self.sibling(item) for item in mine]

    def exchange(self, pieces):
        G = self.G
        near, far = [None] * G, [None] * G
        near[0], far[0] = pieces[0], pieces[G]
        for k in range(1, G):
            both = self.shift(jnp.stack([pieces[k], pieces[k + G]]), k)
            near[-k % G], far[-k % G] = both[0], both[1]
        return near + [self.sibling(item) for item in far]

    def combine(self, parts):
        G = self.G
        got = [self.sibling(parts[k + G]) for k in range(G)]
        total = parts[0].astype(F32) + got[0].astype(F32)
        for k in range(1, G):
            total = total + self.shift(add_low(parts[k], got[k]), k).astype(F32)
        return total

    def to_group(self, x):
        got = self.partner(lax.dynamic_index_in_dim(x, 1 - self.s, 0, keepdims=False), True)
        return jnp.where(self.home, lax.dynamic_index_in_dim(x, self.s, 0, keepdims=False), got)

    def from_group(self, x):
        got = self.partner(x, False)
        return jnp.stack([jnp.where(self.r == 0, x, got), jnp.where(self.r == 0, got, x)])

    def table(self):
        T, G, s, c, d = self.T, self.G, self.s, self.c, self.d
        out = [jnp.int32(0)] * 48
        position = jnp.array([self.order.index(z) for z in range(T)], jnp.int32)[self.z]
        order = jnp.array(self.order, jnp.int32)
        for rel in range(8):
            if self.planar:
                out[COL_OF_REL + rel] = ((d ^ (rel % 4)) * 2 + (s ^ (rel // 4))).astype(jnp.int32)
                out[REL_OF_COL + rel] = ((d ^ (rel // 2)) + 4 * (s ^ (rel % 2))).astype(jnp.int32)
            else:
                out[COL_OF_REL + rel] = jnp.int32(rel)
                out[REL_OF_COL + rel] = jnp.int32(rel)
        for i in range(T):
            out[ABS_OF_REL + i] = (c + i % G) % G + G * (s ^ (i // G))
            out[REL_OF_ABS + i] = (i % G - c) % G + G * ((i // G) ^ s)
            quarter = order[(position - i) % T]
            out[REL_OF_RING + i] = (quarter % G - c) % G + G * ((quarter // G) ^ s)
        for i in range(self.DP):
            out[REL_OF_DP + i] = (d ^ i) if self.planar else jnp.int32(i)
        return jnp.stack([jnp.asarray(item, jnp.int32) for item in out])


def gather_weights(links, stacked):
    rows = stacked.shape[0]
    s, d = links.s, links.d
    other = links.sibling(stacked)
    whole = [jnp.where(s == 0, stacked, other), jnp.where(s == 0, other, stacked)]
    weights = [[[item]] for item in whole]
    if not links.planar:
        for layer in range(2):
            current = whole[layer]
            for _ in range(1, links.T):
                current = links.ring(current)
                weights[layer].append([current])
        return weights
    mine = lax.dynamic_slice_in_dim(stacked, (2 * d + s) * 128, 128, 1)
    give = lax.dynamic_slice_in_dim(stacked, (2 * d + 1 - s) * 128, 128, 1)
    got = links.sibling(give)
    start = [jnp.where(s == 0, mine, got), jnp.where(s == 0, got, mine)]
    half = rows // 2
    for layer in range(2):
        current = start[layer]
        for _ in range(1, links.T):
            current = links.ring(current)
            by_x, by_y = links.along(current, 1), links.along(current, 2)
            top = links.along(by_y[:half], 1)
            bottom = links.along(by_x[half:], 2)
            mine = [current, by_x, by_y, top, bottom]
            weights[layer].append(mine + [links.sibling(item) for item in mine])
    return weights


def gather_projection(links, own):
    s, d = links.s, links.d
    other = links.sibling(own)
    whole = [jnp.where(s == 0, own, other), jnp.where(s == 0, other, own)]
    result = []
    for item in whole:
        if not links.planar:
            result.append(jnp.where(links.home, item, links.partner(item, True)))
            continue
        size = item.shape[0] // 4
        piece = links.partner(lax.dynamic_slice_in_dim(item, d * size, size, 0), True)
        by_x, by_y = links.along_away(piece, 1), links.along_away(piece, 2)
        across = jnp.concatenate(
            [links.along_away(by_y[: size // 2], 1), links.along_away(by_x[size // 2 :], 2)]
        )
        buffer = jnp.zeros_like(item)
        for place, part in enumerate((piece, by_x, by_y, across)):
            buffer = lax.dynamic_update_slice_in_dim(buffer, part, (d ^ place) * size, 0)
        result.append(jnp.where(links.home, item, buffer))
    return result


def plane_reduce(links, parts, along):
    half = parts.shape[1] // 2
    from_x = along(parts[3, :half], 1)
    from_y = along(parts[3, half:], 2)
    for_x = jnp.concatenate([parts[1, :half], add_low(parts[1, half:], from_y)])
    for_y = jnp.concatenate([add_low(parts[2, :half], from_x), parts[2, half:]])
    return add_low(parts[0], along(for_x, 1), along(for_y, 2))


def reduce_start(links, own, sib):
    if not links.planar:
        return jnp.concatenate([own, sib])
    return plane_reduce(links, add_low(own, links.sibling(sib)), links.along)


def reduce_end(links, total):
    if links.planar:
        return total
    total = add_low(total, links.sibling(total))
    return lax.psum_scatter(total, "dp", scatter_dimension=0, tiled=True)[0]


def ring_add(links, running, term):
    return term if running is None else add_low(links.ring(running), term)


def home_layers(links, per_layer):
    mine = jnp.where(links.s == 0, per_layer[0], per_layer[1])
    if not links.planar:
        return mine
    got = links.sibling(jnp.where(links.s == 0, per_layer[1], per_layer[0]))
    return jnp.where(
        links.s == 0, jnp.concatenate([mine, got], axis=1), jnp.concatenate([got, mine], axis=1)
    )


def sum_everywhere(links, x):
    x = x + links.sibling(x)
    if links.planar:
        x = x + links.along(x, 1)
        x = x + links.along(x, 2)
    else:
        x = lax.psum(x, "dp")
    step = 1
    while step < links.T:
        x = x + lax.ppermute(x, "tensor", [(z, z ^ step) for z in range(links.T)])
        step *= 2
    return x


def norm_low(x, gain):
    inverse = lax.rsqrt(jnp.mean(x * x, axis=-1, keepdims=True) + EPS)
    return (x * inverse * gain).astype(BF)


def per_device(
    tokens,
    segment_ids,
    cotangent,
    query_weight,
    key_weight,
    value_weight,
    output_weight,
    gate_weight,
    up_weight,
    down_weight,
    attn_gain,
    mlp_gain,
):
    links = Links()
    T, DP, s = links.T, links.DP, links.s
    seq = segment_ids.shape[1]
    width = tokens.shape[2]
    cols = query_weight.shape[2]
    hidden = gate_weight.shape[2]
    meta = links.table()

    half = HEAD // 2
    frequency = ROPE_BASE ** (-jnp.arange(half, dtype=F32) / half)
    angles = jnp.arange(seq, dtype=F32)[:, None] * frequency[None, :]
    cosine, sine = jnp.cos(angles), jnp.sin(angles)
    tables = (
        jnp.concatenate([cosine] * 4, axis=1),
        jnp.concatenate([-sine, sine, -sine, sine], axis=1),
    )
    segments = lax.dynamic_index_in_dim(segment_ids, links.r, 0, keepdims=False)
    lane = jnp.arange(256, dtype=jnp.int32)[None, :]
    place = jnp.where(lane < 128, lane - HEAD, lane - 128)
    same = segments[:, None] == place
    in_seg = (place >= 0) & (place < 4)
    ext_q = jnp.where(in_seg & ~same, -BIG, 0.0).astype(BF)
    ext_k = jnp.where((in_seg & same) | ((place >= 4) & (place < 7)), 1.0, 0.0).astype(BF)

    projection = jnp.concatenate([query_weight[0], key_weight[0], value_weight[0]], axis=1)
    stacked = jnp.concatenate([output_weight[0], gate_weight[0].T, up_weight[0].T, down_weight[0]], axis=0)
    own_gains = jnp.concatenate([attn_gain, mlp_gain])
    other_gains = links.sibling(own_gains)
    gains = [
        jnp.where(s == layer, own_gains, other_gains) for layer in range(2)
    ]
    w_proj = gather_projection(links, projection)
    weights = gather_weights(links, stacked)

    x = links.to_group(tokens)
    kept = []
    first_values = None
    for layer in range(2):
        gain_attn, gain_mlp = gains[layer][0:1], gains[layer][1:2]
        a = norm_low(x.astype(F32), gain_attn)
        a_blocks = links.spread(a)
        q, k, v = project(meta, a_blocks, w_proj[layer], tables, (ext_q, ext_k), first_values)
        if layer == 0:
            first_values = v
        o_rel, q = attend(meta, q, k, v, T)
        o_blocks = links.exchange([o_rel[i] for i in range(T)])
        y, h, b, g, u = mlp_forward(meta, x, gain_mlp, o_blocks, weights[layer], hidden)
        kept.append((x, a_blocks, q, k, v, o_rel, o_blocks, h, b, g, u))
        x = y
    grouped = links.from_group(x)
    activations = jnp.where(links.home, grouped, links.sibling(grouped))

    dy = links.to_group(cotangent)
    first_grad = None
    mlp_sums, out_sums, proj_sums, gain_sums = [None] * 2, [None] * 2, [None] * 2, [None] * 2
    for layer in (1, 0):
        gain_attn, gain_mlp = gains[layer][0:1], gains[layer][1:2]
        x, a_blocks, q, k, v, o_rel, o_blocks, h, b, g, u = kept[layer]
        dy_low = dy.astype(BF)
        running, db = None, None
        for quarter in list(range(1, T)) + [0]:
            (own, sib), db = mlp_backward(meta, dy_low, b, g, u, db, weights[layer], [quarter], cols)
            running = ring_add(links, running, reduce_start(links, own, sib))
        mlp_sums[layer] = running
        dh, mlp_gain_grad, do_rel, own, sib = middle(meta, dy, db, h, gain_mlp, o_blocks, weights[layer])
        do_blocks = links.exchange([do_rel[i] for i in range(T)])
        out_part = reduce_start(links, own, sib)
        running = None
        for quarter in list(range(1, T)) + [0]:
            term = out_part[..., quarter * cols : (quarter + 1) * cols, :]
            running = ring_add(links, running, term)
        out_sums[layer] = running
        back = attend_back(meta, q, k, v, o_rel, do_blocks, tables, first_grad)
        if layer == 1:
            first_grad = back[3]
        da_parts, dw = project_back(meta, a_blocks, back[:3], w_proj[layer], DP)
        if links.planar:
            proj_sums[layer] = plane_reduce(links, dw, links.along)
        else:
            proj_sums[layer] = lax.psum_scatter(dw, "dp", scatter_dimension=0, tiled=True)[0]
        da = links.combine(list(da_parts))
        part, attn_gain_grad = norm_back(x.astype(F32), gain_attn, da)
        gain_sums[layer] = jnp.concatenate([attn_gain_grad, mlp_gain_grad])
        dy = dh + part
    grouped = links.from_group(dy.astype(BF))
    half_width = width // 2
    keep = lax.dynamic_slice_in_dim(grouped, s * half_width, half_width, 2)
    send = lax.dynamic_slice_in_dim(grouped, (1 - s) * half_width, half_width, 2)
    input_grad = jnp.where(links.home, keep, links.sibling(send)).astype(F32)

    own_mlp = home_layers(links, [reduce_end(links, item) for item in mlp_sums]).astype(F32)
    own_out = home_layers(links, [reduce_end(links, item) for item in out_sums]).astype(F32)
    joined = [item.astype(F32) + links.partner(item, False).astype(F32) for item in proj_sums]
    mine = jnp.where(s == 0, joined[0], joined[1])
    got = links.sibling(jnp.where(s == 0, joined[1], joined[0]))
    own_proj = jnp.where(links.home, mine, got)
    squares = jnp.sum(own_mlp * own_mlp) + jnp.sum(own_out * own_out) + jnp.sum(own_proj * own_proj)
    line = jnp.where(jnp.arange(width)[None, :] == s, squares, 0.0)
    summed = sum_everywhere(links, jnp.concatenate([gain_sums[0], gain_sums[1], line]))
    gain_total = jnp.where(s == 0, summed[0:2], summed[2:4])
    weight_total = jnp.where(s == 0, summed[4, 0], summed[4, 1])
    grad_norm = jnp.sqrt(weight_total + jnp.sum(gain_total * gain_total)).reshape(1)
    shard = width // (DP * T)
    gain_out = lax.dynamic_slice_in_dim(gain_total, (links.d * T + links.z) * shard, shard, 1)
    return (
        activations,
        input_grad,
        own_proj[None, :, :cols],
        own_proj[None, :, cols : 2 * cols],
        own_proj[None, :, 2 * cols :],
        own_out[None],
        own_mlp[:hidden].T[None],
        own_mlp[hidden : 2 * hidden].T[None],
        own_mlp[2 * hidden :][None],
        gain_out[0:1],
        gain_out[1:2],
        grad_norm,
    )


def solution(mesh):
    return jax.shard_map(
        per_device,
        mesh=mesh,
        in_specs=(
            P("dp", "tensor", None),
            P("dp", None),
            P("dp", "tensor", None),
            P("section", None, "tensor"),
            P("section", None, "tensor"),
            P("section", None, "tensor"),
            P("section", "tensor", None),
            P("section", None, "tensor"),
            P("section", None, "tensor"),
            P("section", "tensor", None),
            P("section", None),
            P("section", None),
        ),
        out_specs=(
            P("dp", "tensor", None),
            P("dp", "tensor", "section"),
            P("section", "dp", "tensor"),
            P("section", "dp", "tensor"),
            P("section", "dp", "tensor"),
            P("section", "tensor", "dp"),
            P("section", "dp", "tensor"),
            P("section", "dp", "tensor"),
            P("section", "tensor", "dp"),
            P("section", ("dp", "tensor")),
            P("section", ("dp", "tensor")),
            P("section"),
        ),
        check_vma=False,
    )
```

```python
import functools
import math

import jax
import jax.numpy as jnp
import numpy as np
from jax import lax
from jax.experimental import pallas as pl
from jax.experimental.pallas import tpu as pltpu
from jax.sharding import PartitionSpec as P

HEAD = 64
EPS = 1e-05
ROPE_BASE = 10000.0
BIG = 1e30
LOG2E = math.log2(math.e)
BF = jnp.bfloat16
F32 = jnp.float32
ALL = ("section", "dp", "tensor")
VMEM_LIMIT = 60 * 1024 * 1024
STEP = 256
CHUNK = 32
STRIP = 256

COL_OF_REL, ABS_OF_REL, OUT_OF_ABS, ABS_OF_OUT, CHIP_OF_RING, SIDE_OF_RING, REL_OF_DP, SECTION = 0, 8, 16, 24, 32, 40, 48, 56
PLACES = 64


def nn(a, b):
    return jnp.dot(a, b, preferred_element_type=F32)


def nt(a, b):
    return lax.dot_general(a, b, (((1,), (1,)), ((), ())), preferred_element_type=F32)


def tn(a, b):
    return lax.dot_general(a, b, (((0,), (0,)), ((), ())), preferred_element_type=F32)


def vmem_spec():
    return pl.BlockSpec(memory_space=pltpu.VMEM)


def any_spec():
    return pl.BlockSpec(memory_space=pl.ANY)


def smem_spec():
    return pl.BlockSpec(memory_space=pltpu.SMEM)


def sds(shape, dtype):
    return jax.ShapeDtypeStruct(shape, dtype)


def cost(micros):
    return pl.CostEstimate(flops=int(micros * 1.15e9), bytes_accessed=0, transcendentals=0)


def params(**more):
    return pltpu.CompilerParams(vmem_limit_bytes=VMEM_LIMIT, **more)


def call(kernel, deps, operands, *, in_specs, **rest):
    count, extra = len(operands), len(deps)

    def body(*refs):
        kernel(*refs[:count], *refs[count + extra :])

    return pl.pallas_call(body, in_specs=in_specs + [any_spec()] * extra, **rest)(*operands, *deps)


class Weights:
    def __init__(self, arrays, offset=0):
        self.arrays, self.offset = arrays, offset

    def copies(self, meta, refs, parts, sems, first):
        found = []
        for n, ref in enumerate(refs):
            for row, rows, target in parts:
                dst = target
                if len(refs) > 1:
                    width = ref.shape[1]
                    dst = target.at[:, pl.ds(pl.multiple_of(meta[COL_OF_REL + n] * width, width), width)]
                src = ref.at[pl.ds(self.offset + row, rows), :]
                found.append(pltpu.make_async_copy(src, dst, sems.at[first + len(found)]))
        return found


class Blocks:
    def __init__(self, arrays, places, by_section=()):
        self.arrays, self.places, self.by_section = arrays, places, by_section

    def copies(self, meta, refs, target, sems, first):
        found = []
        for i, (n, place) in enumerate(self.places):
            place = meta[SECTION] ^ place if i in self.by_section else place
            found.append(pltpu.make_async_copy(refs[n].at[place], target(i), sems.at[first + i]))
        return found


def unique(weights):
    operands, places = [], []
    for item in weights:
        mine = []
        for array in item.arrays:
            for n, other in enumerate(operands):
                if other is array:
                    mine.append(n)
                    break
            else:
                mine.append(len(operands))
                operands.append(array)
        places.append(mine)
    return operands, places


def start_all(copies):
    for copy in copies:
        copy.start()
    return copies


def wait_all(copies):
    for copy in copies:
        copy.wait()


def swap_halves(tile):
    lane = lax.broadcasted_iota(jnp.int32, tile.shape, 1)
    return jnp.where(lane % HEAD < HEAD // 2, pltpu.roll(tile, 128 - HEAD // 2, 1), pltpu.roll(tile, HEAD // 2, 1))


def column_of(part, pair, cols):
    side = cols // 2
    if side % 128:
        return part * cols + pair * 128
    per_side = side // 128
    return (pair // per_side * 3 + part) * side + pair % per_side * 128


def qkv_kernel(a_blocks, later, meta, *refs):
    blocks, held = len(a_blocks.places), len(a_blocks.arrays)
    a_refs = refs[:held]
    w_ref, cos_ref, sin_ref, extq_ref, extk_ref = refs[held : held + 5]
    rest = refs[held + 5 :]
    if later:
        first_ref, rest = rest[0], rest[1:]
    outs, (a_scr, w_scr, q_scr, k_scr, v_scr, cos_scr, sin_scr, extq_scr, extk_scr), rest = rest[:3], rest[3:12], rest[12:]
    if later:
        first_scr, rest = rest[0], rest[1:]
    sems, out_sems = rest
    length = a_scr.shape[1]
    cols = w_ref.shape[1] // 3
    loads = [
        pltpu.make_async_copy(w_ref, w_scr, sems.at[0]),
        pltpu.make_async_copy(cos_ref, cos_scr, sems.at[2]),
        pltpu.make_async_copy(sin_ref, sin_scr, sems.at[3]),
        pltpu.make_async_copy(extq_ref, extq_scr, sems.at[4]),
        pltpu.make_async_copy(extk_ref, extk_scr, sems.at[5]),
    ]
    if later:
        loads.append(pltpu.make_async_copy(first_ref, first_scr, sems.at[6]))
    more = a_blocks.copies(meta, a_refs, lambda i: a_scr.at[i], sems, 7)
    start_all(loads)
    start_all(more)
    lane = lax.broadcasted_iota(jnp.int32, (length, 128), 1)
    low = lane < HEAD
    ones_even = ((lane >= HEAD + 4) & (lane < HEAD + 7)).astype(F32)
    ones_odd = ((lane >= 4) & (lane < 7)).astype(F32)
    stores = []
    for i in range(blocks):
        start = pl.multiple_of(meta[ABS_OF_REL + i] * length, length)
        rows = pl.ds(start, length)
        if i == 0:
            wait_all(loads)
        more[i].wait()
        a = a_scr[i]
        cosine, sine = cos_scr[rows, :], sin_scr[rows, :]
        whole = nn(a, w_scr[...])
        for part, out in ((0, q_scr), (1, k_scr), (2, v_scr)):
            for pair in range(cols // 128):
                column = column_of(part, pair, cols)
                tile = whole[:, column : column + 128]
                if part < 2:
                    tile = tile * cosine + swap_halves(tile) * sine
                    ext = extq_scr if part == 0 else extk_scr
                    if part == 0:
                        tile = tile * (LOG2E * HEAD**-0.5)
                    even_ext = ext[rows, :128].astype(F32)
                    odd_ext = ext[rows, 128:].astype(F32)
                else:
                    if later:
                        first = jnp.where(
                            low,
                            first_scr[2 * pair, rows, :].astype(F32),
                            first_scr[2 * pair + 1, rows, :].astype(F32),
                        )
                        tile = 0.5 * tile + 0.5 * first
                    even_ext, odd_ext = ones_even, ones_odd
                out[i, 2 * pair] = jnp.where(low, tile, even_ext).astype(BF)
                out[i, 2 * pair + 1] = jnp.where(low, odd_ext, tile).astype(BF)
        for n, (scr, out) in enumerate(zip((q_scr, k_scr, v_scr), outs)):
            stores += start_all([pltpu.make_async_copy(scr.at[i], out.at[:, rows, :], out_sems.at[3 * i + n])])
    wait_all(stores)


def project(meta, a_blocks, w, tables, exts, first, deps):
    blocks, (_, length, width) = len(a_blocks.places), a_blocks.arrays[0].shape
    cols = w.shape[1] // 3
    heads = cols // HEAD
    seq = blocks * length
    out = sds((heads, seq, 128), BF)
    later = first is not None
    operands = [meta, *a_blocks.arrays, w, *tables, *exts] + ([first] if later else [])
    block = pltpu.VMEM((blocks, heads, length, 128), BF)
    return call(
        functools.partial(qkv_kernel, a_blocks, later),
        deps,
        operands,
        out_shape=(out, out, out),
        in_specs=[smem_spec()] + [any_spec()] * (len(operands) - 1),
        out_specs=(any_spec(),) * 3,
        scratch_shapes=[
            pltpu.VMEM((blocks, length, width), BF),
            pltpu.VMEM(w.shape, BF),
            block,
            block,
            block,
            pltpu.VMEM((seq, 128), F32),
            pltpu.VMEM((seq, 128), F32),
            pltpu.VMEM((seq, 256), BF),
            pltpu.VMEM((seq, 256), BF),
        ]
        + ([pltpu.VMEM(out.shape, BF)] if later else [])
        + [pltpu.SemaphoreType.DMA((blocks + 7,)), pltpu.SemaphoreType.DMA((3 * blocks,))],
        compiler_params=params(),
        cost_estimate=cost(10),
        name="project",
    )


def project_back_kernel(a_blocks, dp_blocks, meta, *refs):
    blocks, held = len(a_blocks.places), len(a_blocks.arrays)
    a_refs = refs[:held]
    dq_ref, dk_ref, dv_ref, w_ref, near_ref, far_ref, dw_ref = refs[held : held + 7]
    a_scr, d_scr, w_scr, da_scr, dw_scr, sems, out_sems = refs[held + 7 :]
    _, length, width = da_scr.shape
    cols = dq_ref.shape[1]
    loads = [pltpu.make_async_copy(w_ref, w_scr, sems.at[0])]
    for part, ref in enumerate((dq_ref, dk_ref, dv_ref)):
        for pair in range(cols // 128):
            target = d_scr.at[:, pl.ds(column_of(part, pair, cols), 128)]
            source = ref.at[:, pl.ds(pair * 128, 128)]
            loads.append(pltpu.make_async_copy(source, target, sems.at[len(loads)]))

    def place(i):
        start = pl.multiple_of(meta[ABS_OF_REL + i] * length, length)
        return a_scr.at[pl.ds(start, length)]

    more = a_blocks.copies(meta, a_refs, place, sems, len(loads))
    start_all(loads)
    start_all(more)
    wait_all(loads)
    order = list(range(1, blocks, 2)) + list(range(2, blocks, 2)) + [0]
    stores = []
    for i in order:
        start = pl.multiple_of(meta[ABS_OF_REL + i] * length, length)
        da_scr[i] = nt(d_scr[pl.ds(start, length), :], w_scr[...]).astype(BF)
        out = far_ref if i % 2 else near_ref
        stores += start_all([pltpu.make_async_copy(da_scr.at[i], out.at[i // 2], out_sems.at[i])])
    wait_all(more)
    size = width // dp_blocks
    for j in range(dp_blocks):
        dw_scr[meta[REL_OF_DP + j]] = tn(a_scr[:, j * size : (j + 1) * size], d_scr[...]).astype(BF)
    stores += start_all([pltpu.make_async_copy(dw_scr, dw_ref, out_sems.at[blocks])])
    wait_all(stores)


def project_back(meta, a_blocks, grads, w, dp_blocks, deps):
    blocks, (_, length, width) = len(a_blocks.places), a_blocks.arrays[0].shape
    cols = w.shape[1]
    seq = blocks * length
    half = sds((blocks // 2, length, width), BF)
    dw = (dp_blocks, width // dp_blocks, cols)
    return call(
        functools.partial(project_back_kernel, a_blocks, dp_blocks),
        deps,
        [meta, *a_blocks.arrays, *grads, w],
        out_shape=(half, half, sds(dw, BF)),
        in_specs=[smem_spec()] + [any_spec()] * (len(a_blocks.arrays) + 4),
        out_specs=(any_spec(),) * 3,
        scratch_shapes=[
            pltpu.VMEM((seq, width), BF),
            pltpu.VMEM((seq, cols), BF),
            pltpu.VMEM(w.shape, BF),
            pltpu.VMEM((blocks, length, width), BF),
            pltpu.VMEM(dw, BF),
            pltpu.SemaphoreType.DMA((blocks + 1 + cols // 128,)),
            pltpu.SemaphoreType.DMA((blocks + 1,)),
        ],
        compiler_params=params(),
        cost_estimate=cost(12),
        name="project_back",
    )


def three_parts(value):
    high = value.astype(BF).astype(F32)
    middle = (value - high).astype(BF).astype(F32)
    return high, middle, value - high - middle


def with_parts(base, value, odd):
    lane = lax.broadcasted_iota(jnp.int32, base.shape, 1)
    offset = 4 if odd else HEAD + 4
    high, middle, rest = three_parts(value)
    out = jnp.where(lane == offset, high, base)
    out = jnp.where(lane == offset + 1, middle, out)
    return jnp.where(lane == offset + 2, rest, out)


def attend_kernel(block, meta, q_ref, k_ref, v_ref, o_ref, ql_ref, vt_scr, tot_scr, top_scr, s_scr, p_scr):
    seq = q_ref.shape[1]
    length = o_ref.shape[1]
    key_row = lax.broadcasted_iota(jnp.int32, (STEP, block), 0)
    query_col = lax.broadcasted_iota(jnp.int32, (STEP, block), 1)
    for e in range(2):
        vt_scr[e] = v_ref[e].T

    def score(i, e):
        q = q_ref[e, i * block : (i + 1) * block, :]
        best = None
        for lo in range(0, (i + 1) * block, STEP):
            tile = nt(k_ref[e, lo : lo + STEP, :], q)
            if lo >= i * block:
                tile = jnp.where(key_row + (lo - i * block) <= query_col, tile, -BIG)
            s_scr[e, i % 2, lo : lo + STEP, :] = tile
            best = tile if best is None else jnp.maximum(best, tile)
        top_scr[e, :, i * block : (i + 1) * block] = best.max(axis=0, keepdims=True)

    def weigh(i, e):
        cols = slice(i * block, (i + 1) * block)
        top = top_scr[e, :, cols]
        for lo in range(0, (i + 1) * block, STEP):
            p_scr[e, lo : lo + STEP, :] = jnp.exp2(s_scr[e, i % 2, lo : lo + STEP, :] - top).astype(BF)
        tot_scr[e, :, cols] = nn(vt_scr[e, :, : (i + 1) * block], p_scr[e, : (i + 1) * block, :])

    count = seq // block
    for i in range(count + 1):
        for e in range(2):
            if i < count:
                score(i, e)
            if i > 0:
                weigh(i - 1, e)
    low = lax.broadcasted_iota(jnp.int32, (length, 128), 1) < HEAD
    lane = lax.broadcasted_iota(jnp.int32, (length, 128), 1)
    row = lax.broadcasted_iota(jnp.int32, (128, length), 0)
    for i in range(seq // length):
        rows = slice(i * length, (i + 1) * length)
        results = []
        for e in range(2):
            place = 4 if e else HEAD + 4
            total = tot_scr[e, :, rows]
            weight = total[place : place + 1, :]
            total = total * (1.0 / weight)
            for n, value in enumerate(three_parts(-(top_scr[e, :, rows] + jnp.log2(weight)))):
                total = jnp.where(row == place + n, value, total)
            turned = total.T
            results.append(turned)
            parts = (lane >= place) & (lane < place + 3)
            ql_ref[e, rows, :] = jnp.where(parts, turned, q_ref[e, rows, :].astype(F32)).astype(BF)
        o_ref[meta[OUT_OF_ABS + i]] = jnp.where(low, results[0], results[1]).astype(BF)


def attend(meta, q, k, v, blocks, deps):
    heads, seq, _ = q.shape
    pairs = heads // 2
    length = seq // blocks
    head_spec = pl.BlockSpec((2, seq, 128), lambda p: (p, 0, 0))
    return call(
        functools.partial(attend_kernel, min(256, length)),
        deps,
        [meta, q, k, v],
        grid=(pairs,),
        out_shape=(sds((blocks, length, pairs * 128), BF), sds(q.shape, BF)),
        in_specs=[smem_spec(), head_spec, head_spec, head_spec],
        out_specs=(pl.BlockSpec((blocks, length, 128), lambda p: (0, 0, p)), head_spec),
        scratch_shapes=[
            pltpu.VMEM((2, 128, seq), BF),
            pltpu.VMEM((2, 128, seq), F32),
            pltpu.VMEM((2, 1, seq), F32),
            pltpu.VMEM((2, 2, seq, min(256, length)), F32),
            pltpu.VMEM((2, seq, min(256, length)), BF),
        ],
        compiler_params=params(),
        cost_estimate=cost(14.5),
        name="attend",
    )


def attend_back_kernel(block, blocks, later, meta, q_ref, k_ref, v_ref, o_ref, *refs):
    do_refs = refs[:blocks]
    cos_ref, sin_ref = refs[blocks : blocks + 2]
    rest = refs[blocks + 2 :]
    if not later:
        first_ref, rest = rest[0], rest[1:]
    dq_ref, dk_ref, dv_ref = rest[:3]
    rest = rest[3:]
    if later:
        first_out, rest = rest[0], rest[1:]
    do_scr, dq_scr, dk_scr, dv_scr, kt_scr, p_scr, ds_scr = rest
    seq = q_ref.shape[1]
    length = o_ref.shape[1]
    lane = lax.broadcasted_iota(jnp.int32, (length, 128), 1)
    low = lane < HEAD
    for i in range(blocks):
        start = pl.multiple_of(meta[ABS_OF_OUT + i] * length, length)
        rows = pl.ds(start, length)
        do = do_refs[i][...].astype(F32)
        product = do * o_ref[i].astype(F32)
        for e in range(2):
            mine = low if e == 0 else jnp.logical_not(low)
            delta = jnp.sum(jnp.where(mine, product, 0.0), axis=1, keepdims=True)
            do_scr[e, rows, :] = with_parts(jnp.where(mine, do, 0.0), -delta, e == 1).astype(BF)
    key_row = lax.broadcasted_iota(jnp.int32, (STEP, block), 0)
    query_col = lax.broadcasted_iota(jnp.int32, (STEP, block), 1)
    for e in range(2):
        kt_scr[e] = k_ref[e].T
    count = seq // block

    def weigh(i, e):
        cols = slice(i * block, (i + 1) * block)
        q = q_ref[e, cols, :]
        do = do_scr[e, cols, :]
        for lo in range(0, (i + 1) * block, STEP):
            rows = slice(lo, lo + STEP)
            scores = nt(k_ref[e, rows, :], q)
            if lo >= i * block:
                scores = jnp.where(key_row + (lo - i * block) <= query_col, scores, -BIG)
            prob = jnp.exp2(scores)
            p_scr[e, rows, cols] = prob.astype(BF)
            ds_scr[e, rows, cols] = (prob * nt(v_ref[e, rows, :], do)).astype(BF)

    def query_grad(i, e):
        cols = slice(i * block, (i + 1) * block)
        dq_scr[e, :, cols] = nn(kt_scr[e, :, : (i + 1) * block], ds_scr[e, : (i + 1) * block, cols])

    def key_grads(i, e):
        rows, cols = slice(i * block, (i + 1) * block), slice(i * block, seq)
        dv_scr[e, rows, :] = nn(p_scr[e, rows, cols], do_scr[e, cols, :])
        dk_scr[e, rows, :] = nn(ds_scr[e, rows, cols], q_ref[e, cols, :])

    for i in range(count + 1):
        for e in range(2):
            if i < count:
                weigh(i, e)
            if i > 0:
                query_grad(i - 1, e)
    for i in range(count):
        for e in range(2):
            key_grads(i, e)
    for i in range(blocks):
        rows = slice(i * length, (i + 1) * length)
        cosine, sine = cos_ref[rows, :], sin_ref[rows, :]
        dq = jnp.where(low, dq_scr[0, :, rows].T, dq_scr[1, :, rows].T) * (HEAD**-0.5)
        dk = jnp.where(low, dk_scr[0, rows, :], dk_scr[1, rows, :]) * (1.0 / LOG2E)
        dv = jnp.where(low, dv_scr[0, rows, :], dv_scr[1, rows, :])
        dq_ref[rows, :] = (dq * cosine - swap_halves(dq) * sine).astype(BF)
        dk_ref[rows, :] = (dk * cosine - swap_halves(dk) * sine).astype(BF)
        if later:
            dv_ref[rows, :] = (0.5 * dv).astype(BF)
            first_out[rows, :] = 0.5 * dv
        else:
            dv_ref[rows, :] = (dv + first_ref[rows, :]).astype(BF)


def attend_back(meta, q, k, v, o, do_blocks, tables, first, deps):
    heads, seq, _ = q.shape
    pairs = heads // 2
    blocks, length, cols = o.shape
    later = first is None
    head_spec = pl.BlockSpec((2, seq, 128), lambda p: (p, 0, 0))
    col_spec = pl.BlockSpec((seq, 128), lambda p: (0, p))
    table_spec = pl.BlockSpec((seq, 128), lambda p: (0, 0))
    out = sds((seq, cols), BF)
    return call(
        functools.partial(attend_back_kernel, min(256, length), blocks, later),
        deps,
        [meta, q, k, v, o, *[do_blocks.arrays[n] for n, _ in do_blocks.places], *tables, *([] if later else [first])],
        grid=(pairs,),
        out_shape=(out, out, out) + ((sds((seq, cols), F32),) if later else ()),
        in_specs=[smem_spec(), head_spec, head_spec, head_spec]
        + [pl.BlockSpec((blocks, length, 128), lambda p: (0, 0, p))]
        + [pl.BlockSpec((None, length, 128), functools.partial(lambda n, p: (n, 0, p), n)) for _, n in do_blocks.places]
        + [table_spec] * 2
        + ([] if later else [col_spec]),
        out_specs=(col_spec,) * (4 if later else 3),
        scratch_shapes=[
            pltpu.VMEM((2, seq, 128), BF),
            pltpu.VMEM((2, 128, seq), F32),
            pltpu.VMEM((2, seq, 128), F32),
            pltpu.VMEM((2, seq, 128), F32),
            pltpu.VMEM((2, 128, seq), BF),
            pltpu.VMEM((2, seq, seq), BF),
            pltpu.VMEM((2, seq, seq), BF),
        ],
        compiler_params=params(),
        cost_estimate=cost(29.5),
        name="attend_back",
    )


def place_output(weights, places, meta, refs, target, sems, first):
    found = []
    rows = target.shape[1] // 2
    for k, item in enumerate(weights):
        side = pl.multiple_of(meta[SIDE_OF_RING + k] * rows, rows)
        part = (0, rows, target.at[meta[CHIP_OF_RING + k], pl.ds(side, rows)])
        found += item.copies(meta, [refs[n] for n in places[k]], [part], sems, first + 4 * k)
    return found


def output_kernel(o_blocks, weights, places, meta, *refs):
    o_refs, refs = refs[: len(o_blocks.arrays)], refs[len(o_blocks.arrays) :]
    number = len({n for place in places for n in place})
    w_refs, (p_ref, o_scr, w_scr, sems) = refs[:number], refs[number:]
    count = len(o_blocks.places)
    length = o_scr.shape[1] // 2
    loads = o_blocks.copies(meta, o_refs, lambda i: o_scr.at[i // 2, pl.ds(i % 2 * length, length)], sems, 0)
    loads += place_output(weights, places, meta, w_refs, w_scr, sems, count)
    wait_all(start_all(loads))
    for f in range(2):
        rows = slice(f * length, (f + 1) * length)
        total = nn(o_scr[0, rows, :], w_scr[0])
        for n in range(1, count // 2):
            total += nn(o_scr[n, rows, :], w_scr[n])
        p_ref[rows, :] = total.astype(BF)


def output_forward(meta, o_blocks, weights, width, deps):
    count = len(o_blocks.places)
    _, length, cols = o_blocks.arrays[0].shape
    operands, places = unique(weights)
    return call(
        functools.partial(output_kernel, o_blocks, weights, places),
        deps,
        [meta, *o_blocks.arrays, *operands],
        out_shape=sds((2 * length, width), BF),
        in_specs=[smem_spec()] + [any_spec()] * (len(o_blocks.arrays) + len(operands)),
        out_specs=vmem_spec(),
        scratch_shapes=[
            pltpu.VMEM((count // 2, 2 * length, cols), BF),
            pltpu.VMEM((count // 2, cols, width), BF),
            pltpu.SemaphoreType.DMA((5 * count,)),
        ],
        compiler_params=params(),
        cost_estimate=cost(5),
        name="output",
    )


def place_hidden(batch, weights, places, meta, refs, target, sems, first, row):
    hidden = target.shape[1] // len(batch)
    found = []
    for n, k in enumerate(batch):
        parts = [(row + m * hidden, hidden, target.at[m, pl.ds(n * hidden, hidden)]) for m in range(3)]
        found += weights[k].copies(meta, [refs[i] for i in places[k]], parts, sems, first + 12 * n)
    return found


def mlp_kernel(batches, weights, places, row, meta, x_ref, p_ref, other_ref, gain_ref, *refs):
    number = len({n for place in places for n in place})
    w_refs, refs = refs[:number], refs[number:]
    count = len(batches)
    y_ref, h_ref, b_ref = refs[:3]
    g_refs, u_refs, refs = refs[3 : 3 + count], refs[3 + count : 3 + 2 * count], refs[3 + 2 * count :]
    w_scr, sems = refs
    first = [12 * sum(len(other) for other in batches[:n]) for n in range(count)]

    def loads(n):
        return place_hidden(batches[n], weights, places, meta, w_refs, w_scr.at[n], sems, first[n], row)

    @pl.when(pl.program_id(0) == 0)
    def _():
        for n in range(count):
            start_all(loads(n))

    gain = gain_ref[...]
    for start in range(0, x_ref.shape[0], CHUNK):
        rows = slice(start, start + CHUNK)
        h = x_ref[rows, :].astype(F32) + (p_ref[rows, :].astype(F32) + other_ref[rows, :].astype(F32))
        h_ref[rows, :] = h
        inverse = lax.rsqrt(jnp.mean(h * h, axis=1, keepdims=True) + EPS)
        b_ref[rows, :] = (h * inverse * gain).astype(BF)

    @pl.when(pl.program_id(0) == 0)
    def _():
        for n in range(count):
            wait_all(loads(n))

    for start in range(0, x_ref.shape[0], STRIP):
        rows = slice(start, start + STRIP)
        b = b_ref[rows, :]
        total = None
        for n in range(count):
            g = nt(b, w_scr[n, 0])
            u = nt(b, w_scr[n, 1])
            g_refs[n][rows, :] = g.astype(BF)
            u_refs[n][rows, :] = u.astype(BF)
            m = (g * jax.nn.sigmoid(g) * u).astype(BF)
            term = nn(m, w_scr[n, 2])
            total = term if total is None else total + term
        y_ref[rows, :] = total.astype(BF)


def mlp_forward(meta, x, p, other, gain, weights, batches, hidden, row, deps):
    rows, width = x.shape
    operands, places = unique(weights)
    size = [len(batch) * hidden for batch in batches]
    quarters = sum(len(batch) for batch in batches)
    low = sds((rows, width), BF)
    saved = tuple(sds((rows, n), BF) for n in size)
    block = min(256, rows)

    def by_rows(n):
        return pl.BlockSpec((block, n), lambda i: (i, 0))

    return call(
        functools.partial(mlp_kernel, batches, weights, places, row),
        deps,
        [meta, x, p, other, gain, *operands],
        grid=(rows // block,),
        out_shape=(low, sds((rows, width), F32), low) + saved + saved,
        in_specs=[smem_spec()]
        + [by_rows(width)] * 3
        + [pl.BlockSpec((1, width), lambda i: (0, 0))]
        + [any_spec()] * len(operands),
        out_specs=(by_rows(width),) * 3 + tuple(by_rows(n) for n in size) * 2,
        scratch_shapes=[
            pltpu.VMEM((len(batches), 3, size[0], width), BF),
            pltpu.SemaphoreType.DMA((12 * quarters,)),
        ],
        compiler_params=params(),
        cost_estimate=cost(19),
        name="mlp",
    )


def mlp_back_kernel(batches, weights, places, row, meta, dy_ref, b_ref, *refs):
    count = len(batches)
    g_refs, u_refs, refs = refs[:count], refs[count : 2 * count], refs[2 * count :]
    number = len({n for place in places for n in place})
    w_refs, refs = refs[:number], refs[number:]
    out_refs, refs = refs[:count], refs[count:]
    db_ref, dy_scr, b_scr, g_scr, u_scr, w_scr, low_scr, grad_scr, sems, out_sems = refs
    dy_load = pltpu.make_async_copy(dy_ref, dy_scr, sems.at[0])
    b_load = pltpu.make_async_copy(b_ref, b_scr, sems.at[1])
    dy_load.start()
    loads, used = [], 2
    for n, batch in enumerate(batches):
        group = place_hidden(batch, weights, places, meta, w_refs, w_scr.at[n], sems, used, row)
        used += 12 * len(batch)
        for source, target in ((g_refs[n], g_scr.at[n]), (u_refs[n], u_scr.at[n])):
            group.append(pltpu.make_async_copy(source, target, sems.at[used]))
            used += 1
        loads.append(start_all(group))
    b_load.start()
    total_rows, width = dy_scr.shape
    hidden = w_scr.shape[2] // len(batches[0])
    columns, _, size = out_refs[0].shape
    stores = []
    dy_load.wait()
    for n, batch in enumerate(batches):
        wait_all(loads[n])
        for start in range(0, total_rows, STRIP):
            rows = slice(start, start + STRIP)
            dm = nt(dy_scr[rows, :], w_scr[n, 2])
            g = g_scr[n, rows, :].astype(F32)
            u = u_scr[n, rows, :].astype(F32)
            gate = jax.nn.sigmoid(g)
            active = g * gate
            low_scr[n, 0, rows, :] = (dm * u * (gate + active * (1.0 - gate))).astype(BF)
            low_scr[n, 1, rows, :] = (dm * active).astype(BF)
            low_scr[n, 2, rows, :] = (active * u).astype(BF)
    b_load.wait()
    for n, batch in enumerate(batches):
        for m in range(3):
            grad_scr[n, m] = tn(low_scr[n, m], dy_scr[...] if m == 2 else b_scr[...]).astype(BF)
            for q in range(len(batch)):
                for j in range(columns):
                    copy = pltpu.make_async_copy(
                        grad_scr.at[n, m, pl.ds(q * hidden, hidden), pl.ds(j * size, size)],
                        out_refs[n].at[meta[REL_OF_DP + j], pl.ds((q * 3 + m) * hidden, hidden), :],
                        out_sems.at[((n * 3 + m) * len(batch) + q) * columns + j],
                    )
                    copy.start()
                    stores.append(copy)
    for start in range(0, total_rows, 256):
        rows = slice(start, start + 256)
        db = None
        for n in range(count):
            term = nn(low_scr[n, 0, rows, :], w_scr[n, 0]) + nn(low_scr[n, 1, rows, :], w_scr[n, 1])
            db = term if db is None else db + term
        db_ref[rows, :] = db.astype(BF)
    wait_all(stores)


def mlp_backward(meta, dy, b, saved, weights, batches, row, dp_blocks, deps):
    rows, width = b.shape
    count = len(batches)
    size = saved[0].shape[1]
    operands, places = unique(weights)
    copies = sum(12 * len(batch) + 2 for batch in batches)
    return call(
        functools.partial(mlp_back_kernel, batches, weights, places, row),
        deps,
        [meta, dy, b, *saved, *operands],
        out_shape=(sds((dp_blocks, 3 * size, width // dp_blocks), BF),) * count + (sds((rows, width), BF),),
        in_specs=[smem_spec()] + [any_spec()] * (2 + 2 * count + len(operands)),
        out_specs=(any_spec(),) * count + (vmem_spec(),),
        scratch_shapes=[
            pltpu.VMEM((rows, width), BF),
            pltpu.VMEM((rows, width), BF),
            pltpu.VMEM((count, rows, size), BF),
            pltpu.VMEM((count, rows, size), BF),
            pltpu.VMEM((count, 3, size, width), BF),
            pltpu.VMEM((count, 3, rows, size), BF),
            pltpu.VMEM((count, 3, size, width), BF),
            pltpu.SemaphoreType.DMA((2 + copies,)),
            pltpu.SemaphoreType.DMA((3 * dp_blocks * sum(len(batch) for batch in batches),)),
        ],
        compiler_params=params(),
        cost_estimate=cost(28),
        name="mlp_back",
    )


def norm_back(values, gain, grads):
    inverse = lax.rsqrt(jnp.mean(values * values, axis=1, keepdims=True) + EPS)
    normed = values * inverse
    scaled = grads * gain
    gain_grad = jnp.sum(grads * normed, axis=0, keepdims=True)
    return inverse * (scaled - normed * jnp.mean(scaled * normed, axis=1, keepdims=True)), gain_grad


def middle_kernel(o_blocks, weights, places, meta, dy_ref, db_ref, other_ref, h_ref, gain_ref, *refs):
    o_refs, refs = refs[: len(o_blocks.arrays)], refs[len(o_blocks.arrays) :]
    number = len({n for place in places for n in place})
    w_refs, refs = refs[:number], refs[number:]
    dh_ref, gain_out, do_ref, grad_ref, w_scr, o_scr, low_scr, grad_scr, sems, out_sems = refs
    count = len(o_blocks.places)
    length = o_scr.shape[1] // 2
    step, steps = pl.program_id(0), pl.num_programs(0)

    def loads():
        found = o_blocks.copies(meta, o_refs, lambda i: o_scr.at[i // 2, pl.ds(i % 2 * length, length)], sems, 0)
        return found + place_output(weights, places, meta, w_refs, w_scr, sems, count)

    @pl.when(step == 0)
    def _():
        start_all(loads())
        gain_out[...] = jnp.zeros_like(gain_out)

    gain = gain_ref[...]
    block = dy_ref.shape[0]
    first = pl.multiple_of(step * block, block)
    total = None
    for start in range(0, block, CHUNK):
        rows = slice(start, start + CHUNK)
        db = db_ref[rows, :].astype(F32) + other_ref[rows, :].astype(F32)
        part, gain_grad = norm_back(h_ref[rows, :], gain, db)
        dh = dy_ref[rows, :].astype(F32) + part
        dh_ref[rows, :] = dh
        low_scr[pl.ds(first + start, CHUNK), :] = dh.astype(BF)
        total = gain_grad if total is None else total + gain_grad
    gain_out[...] += total

    @pl.when(step == 0)
    def _():
        wait_all(loads())

    low = low_scr[pl.ds(first, block), :]
    for n in range(count // 2):
        do_ref[n] = nt(low, w_scr[n]).astype(BF)

    @pl.when(step == steps - 1)
    def _():
        for n in range(count // 2):
            grad_scr[n] = tn(o_scr[n], low_scr[...]).astype(BF)
        stores = []
        columns = grad_ref.shape[0]
        size = grad_ref.shape[2]
        rows = o_scr.shape[2] // 2
        for k in range(count):
            side = pl.multiple_of(meta[SIDE_OF_RING + k] * rows, rows)
            for j in range(columns):
                stores.append(
                    pltpu.make_async_copy(
                        grad_scr.at[meta[CHIP_OF_RING + k], pl.ds(side, rows), pl.ds(j * size, size)],
                        grad_ref.at[meta[REL_OF_DP + j], pl.ds(k * rows, rows), :],
                        out_sems.at[k * columns + j],
                    )
                )
        wait_all(start_all(stores))


def middle(meta, dy, db, other, h, gain, o_blocks, weights, dp_blocks, deps):
    count = len(o_blocks.places)
    _, length, cols = o_blocks.arrays[0].shape
    width = h.shape[1]
    operands, places = unique(weights)
    block = 256
    by_rows = pl.BlockSpec((block, width), lambda i: (i, 0))
    fixed = pl.BlockSpec((1, width), lambda i: (0, 0))
    return call(
        functools.partial(middle_kernel, o_blocks, weights, places),
        deps,
        [meta, dy, db, other, h, gain, *o_blocks.arrays, *operands],
        grid=(2 * length // block,),
        out_shape=(
            sds((2 * length, width), F32),
            sds((1, width), F32),
            sds((count // 2, 2 * length, cols), BF),
            sds((dp_blocks, count * cols // 2, width // dp_blocks), BF),
        ),
        in_specs=[smem_spec()]
        + [by_rows] * 4
        + [fixed]
        + [any_spec()] * (len(o_blocks.arrays) + len(operands)),
        out_specs=(by_rows, fixed, pl.BlockSpec((count // 2, block, cols), lambda i: (0, i, 0)), any_spec()),
        scratch_shapes=[
            pltpu.VMEM((count // 2, cols, width), BF),
            pltpu.VMEM((count // 2, 2 * length, cols), BF),
            pltpu.VMEM((2 * length, width), BF),
            pltpu.VMEM((count // 2, cols, width), BF),
            pltpu.SemaphoreType.DMA((5 * count,)),
            pltpu.SemaphoreType.DMA((count * dp_blocks,)),
        ],
        compiler_params=params(),
        cost_estimate=cost(13),
        name="middle",
    )


def add_low(*terms):
    total = terms[0].astype(F32)
    for term in terms[1:]:
        total = total + term.astype(F32)
    return total.astype(BF)


def hold(x, *after):
    return lax.optimization_barrier((x, *after))[0] if after else x


class Links:
    def __init__(self):
        self.T = lax.axis_size("tensor")
        self.DP = lax.axis_size("dp")
        self.G = self.T // 2
        self.s = lax.axis_index("section")
        self.d = lax.axis_index("dp")
        self.z = lax.axis_index("tensor")
        self.r = self.z // self.G
        self.home = self.s == self.r
        self.planar = self.DP == 4 and self.T == 4
        self.order = [0] + list(range(1, self.T, 2)) + list(range(self.T - 2, 0, -2))

    def sibling(self, x):
        return lax.ppermute(x, "section", [(0, 1), (1, 0)])

    def ring(self, x):
        order = self.order
        return lax.ppermute(x, "tensor", [(order[i], order[(i + 1) % self.T]) for i in range(self.T)])

    def along(self, x, bit):
        return lax.ppermute(x, "dp", [(i, i ^ bit) for i in range(self.DP)])

    def across(self, x):
        return lax.ppermute(x, "tensor", [(z, (z + self.G) % self.T) for z in range(self.T)])

    def shift(self, x, k):
        pairs = [(z, z // self.G * self.G + (z + k) % self.G) for z in range(self.T)]
        return lax.ppermute(x, "tensor", pairs)

    def swap_blocks(self, x):
        pairs = []
        for s in range(2):
            z0 = s * self.G
            for z in range(z0, z0 + self.G):
                pairs.append((s * self.T + z, s * self.T + (z + self.G) % self.T))
        give = lax.dynamic_index_in_dim(x, 1 - self.r, 0, keepdims=False)
        got = lax.ppermute(give, ("section", "tensor"), pairs)
        got = jnp.where(self.home, self.sibling(got), got)
        mine = (jnp.arange(2) == self.r)[:, None, None]
        return jnp.where(mine, x, got[None])

    def spread(self, x):
        give = lax.dynamic_index_in_dim(x, self.s, 0)
        arrays, places = [x], [(0, 0), (0, 1)]
        for k in range(1, self.G):
            got = self.shift(give, -k)
            arrays += [got, self.sibling(got)]
            places += [(len(arrays) - 2, 0), (len(arrays) - 1, 0)]
        return Blocks(arrays, places, (0, 1))

    def exchange(self, x, length):
        cols = x.shape[-1]
        arrays, places = [x.reshape(self.T, length, cols)], [(0, 0), (0, 1)] + [None] * (self.T - 2)
        for k in range(1, self.G):
            got = self.shift(x.reshape(self.G, 2 * length, cols)[k], k)
            chip = -k % self.G
            places[2 * chip], places[2 * chip + 1] = (len(arrays), 0), (len(arrays), 1)
            arrays.append(got.reshape(2, length, cols))
        return Blocks(arrays, places)

    def combine(self, near, far):
        got = self.sibling(far)
        terms = [near[0], got[0]]
        for k in range(1, self.G):
            terms.append(self.shift(add_low(near[k], got[k]), k))
        mine = add_low(*terms)
        both = (jnp.arange(2) == self.s)[:, None, None]
        return jnp.where(both, mine[None], self.sibling(mine)[None])

    def table(self):
        T, G, DP, order = self.T, self.G, self.DP, self.order
        table = np.zeros((2, DP, T, PLACES), np.int32)
        for s in range(2):
            for d in range(DP):
                for z in range(T):
                    out, c, r, position = table[s, d, z], z % G, z // G, order.index(z)
                    for rel in range(4):
                        out[COL_OF_REL + rel] = d ^ rel if self.planar else rel
                    for i in range(T):
                        quarter = order[(position - i) % T]
                        out[ABS_OF_REL + i] = (c + i // 2) % G + G * (s ^ (i % 2))
                        out[OUT_OF_ABS + i] = 2 * ((i % G - c) % G) + i // G
                        out[ABS_OF_OUT + i] = (c + i // 2) % G + G * (i % 2)
                        out[CHIP_OF_RING + i] = (quarter % G - c) % G
                        out[SIDE_OF_RING + i] = (quarter // G) ^ r
                    for i in range(DP):
                        out[REL_OF_DP + i] = (d ^ i) if self.planar else i
                    out[SECTION] = s
        index = (self.s * DP + self.d) * T + self.z
        return lax.dynamic_index_in_dim(jnp.asarray(table.reshape(-1, PLACES)), index, 0, keepdims=False)


def gather_weights(links, output_weight, gate_weight, up_weight, down_weight, after):
    s, d = links.s, links.d
    width = output_weight.shape[1]

    def half(which):
        def cut(x, dim):
            size = x.shape[dim] // 2
            return lax.dynamic_slice_in_dim(x, which * size, size, dim)

        return jnp.concatenate(
            [cut(output_weight, 0), cut(gate_weight, 1).T, cut(up_weight, 1).T, cut(down_weight, 0)]
        )

    mine = half(s)
    got = links.sibling(half(1 - s))
    weights, rings = [[], []], [[], []]
    for layer in range(2):
        own = jnp.where(s == layer, mine, got)
        weights[layer].append(Weights([own]))
        if not links.planar:
            for _ in range(1, links.T):
                own = links.ring(own)
                weights[layer].append(Weights([own]))
            continue
        size = width // 4
        current = lax.dynamic_slice_in_dim(own, d * size, size, 1)
        current = hold(current, *after)
        steps = []
        for _ in range(1, links.T):
            current = links.ring(current)
            steps.append(current)
        rings[layer] = steps
        rows = current.shape[0]
        for batch in ([0], [1], [2]) if layer == 0 else ([0], [1, 2]):
            part = steps[batch[0]] if len(batch) == 1 else jnp.concatenate([steps[n] for n in batch])
            pieces = [part] + [links.along(part, bit) for bit in (1, 2, 3)]
            for n in range(len(batch)):
                weights[layer].append(Weights(pieces, n * rows))
    return weights, rings


def gather_projection(links, query_weight, key_weight, value_weight):
    s, d = links.s, links.d
    depth, cols = query_weight.shape

    def half(which):
        return jnp.concatenate(
            [lax.dynamic_slice_in_dim(w, which * (cols // 2), cols // 2, 1) for w in (query_weight, key_weight, value_weight)],
            axis=1,
        )

    mine = half(s)
    got = links.sibling(half(1 - s))
    result, early = [], []
    for layer in range(2):
        own = jnp.where(s == layer, mine, got)
        if links.planar:
            other = links.across(lax.dynamic_slice_in_dim(own, d * (depth // 4), depth // 4, 0))
            early.append(other)
            for bit in (1, 2):
                far = links.along(other, bit)
                other = jnp.where(
                    d & bit == 0, jnp.concatenate([other, far]), jnp.concatenate([far, other])
                )
        else:
            other = links.across(own)
        if cols // 2 % 128:
            both = jnp.stack([own.reshape(depth, 3, cols // 2), other.reshape(depth, 3, cols // 2)], axis=2)
            result.append(both.reshape(depth, 3 * cols))
        else:
            result.append(jnp.concatenate([own, other], axis=1))
    return result, early


class PlaneSum:
    def __init__(self, links, part):
        self.links, self.part, self.half = links, part, part.shape[1] // 2

    def begin(self, *after):
        part = hold(self.part, *after)
        self.x = self.links.along(part[1::2, : self.half], 1)
        self.y = self.links.along(part[2:4, self.half :], 2)
        return [self.x, self.y]

    def finish(self, *after):
        part = hold(self.part, *after)
        self.x_end = self.links.along(add_low(part[1, self.half :], self.y[1]), 1)
        self.y_end = self.links.along(add_low(part[2, : self.half], self.x[1]), 2)
        return [self.x_end, self.y_end]

    def total(self, first, rows, more, after):
        part = hold(self.part, *after)
        here = slice(first, first + rows)
        if first + rows <= self.half:
            terms = [part[0, here], self.x[0, here], self.y_end[here]]
        else:
            there = slice(first - self.half, first - self.half + rows)
            terms = [part[0, here], self.y[0, there], self.x_end[there]]
        return add_low(*terms, *more)


class RingSum:
    def __init__(self, links, part_of):
        self.links, self.part_of, self.count, self.passed = links, part_of, 0, []

    def step(self, *after):
        self.total = self.part_of(self.count, self.passed, after)
        self.count += 1
        if self.count < self.links.T:
            self.passed = [self.links.ring(self.total)]
        return [self.passed[0] if self.count < self.links.T else self.total]


class LayerSums:
    def __init__(self, links, parts, out_part, rows, out_rows, order):
        first, second = PlaneSum(links, parts[0]), PlaneSum(links, parts[1])
        out = PlaneSum(links, out_part)
        self.links, self.first, self.second, self.out = links, first, second, out
        self.mlp_ring = RingSum(
            links, lambda n, more, after: (first, second)[n // 2].total(n % 2 * rows, rows, more, after)
        )
        self.out_ring = RingSum(
            links, lambda n, more, after: out.total(order[n] * out_rows, out_rows, more, after)
        )

    def stage(self, number, *after):
        if number == 0:
            return self.second.finish(*after) + self.out.begin(*after) + self.mlp_ring.step(*after)
        if number == 1:
            return self.out.finish(*after) + self.proj.begin(*after) + self.mlp_ring.step(*after)
        if number == 2:
            return self.mlp_ring.step(*after) + self.proj.finish(*after) + self.out_ring.step(*after)
        if number == 3:
            size = self.proj.part.shape[1] // 2
            self.proj_total = jnp.concatenate([self.proj.total(n * size, size, [], after) for n in range(2)])
            return self.mlp_ring.step(*after) + self.out_ring.step(*after) + [self.proj_total]
        return self.out_ring.step(*after)


def both_halves(links, per_layer):
    mine = jnp.where(links.s == 0, per_layer[0], per_layer[1])
    got = links.sibling(jnp.where(links.s == 0, per_layer[1], per_layer[0]))
    return jnp.where(links.s == 0, mine, got), jnp.where(links.s == 0, got, mine)


def sum_everywhere(links, x):
    if links.planar:
        x = x + links.along(x, 1)
        x = x + links.along(x, 2)
    else:
        x = lax.psum(x, "dp")
    step = 1
    while step < links.T:
        x = x + lax.ppermute(x, "tensor", [(z, z ^ step) for z in range(links.T)])
        step *= 2
    return x


def norm_low(x, gain):
    inverse = lax.rsqrt(jnp.mean(x * x, axis=-1, keepdims=True) + EPS)
    return (x * inverse * gain).astype(BF)


def per_device(
    tokens,
    segment_ids,
    cotangent,
    query_weight,
    key_weight,
    value_weight,
    output_weight,
    gate_weight,
    up_weight,
    down_weight,
    attn_gain,
    mlp_gain,
):
    links = Links()
    T, DP, s = links.T, links.DP, links.s
    seq = segment_ids.shape[1]
    length, width = tokens.shape[1:]
    cols = query_weight.shape[2]
    hidden = gate_weight.shape[2] // 2
    meta = links.table()

    half = HEAD // 2
    frequency = np.float32(ROPE_BASE) ** (-np.arange(half, dtype=np.float32) / np.float32(half))
    angles = np.arange(seq, dtype=np.float32)[:, None] * frequency[None, :].astype(np.float32)
    cosine, sine = np.cos(angles), np.sin(angles)
    tables = (
        jnp.asarray(np.concatenate([cosine] * 4, axis=1), F32),
        jnp.asarray(np.concatenate([-sine, sine, -sine, sine], axis=1), F32),
    )
    segments = lax.dynamic_index_in_dim(segment_ids, links.r, 0, keepdims=False)
    lane = jnp.arange(256, dtype=jnp.int32)[None, :]
    place = jnp.where(lane < 128, lane - HEAD, lane - 128)
    same = segments[:, None] == place
    in_seg = (place >= 0) & (place < 4)
    ext_q = jnp.where(in_seg & ~same, -BIG, 0.0).astype(BF)
    ext_k = jnp.where((in_seg & same) | ((place >= 4) & (place < 7)), 1.0, 0.0).astype(BF)

    own_gains = jnp.concatenate([attn_gain, mlp_gain])
    other_gains = links.sibling(own_gains)
    gains = [
        jnp.where(s == layer, own_gains, other_gains) for layer in range(2)
    ]
    w_proj, early = gather_projection(links, query_weight[0], key_weight[0], value_weight[0])
    def flat(item):
        return item.reshape(2 * length, width)

    def blocked(item):
        return item.reshape(2, length, width)

    x = flat(links.swap_blocks(tokens))
    weights, rings = gather_weights(links, output_weight[0], gate_weight[0], up_weight[0], down_weight[0], [x] + early[:1])
    planar = links.planar
    order = list(range(1, T)) + [0]
    batches = [order[: T // 2], order[T // 2 :]]
    out_rows = cols // 2
    rows = 3 * hidden

    a = norm_low(x.astype(F32), gains[0][0:1])
    kept = []
    first_values = None
    for layer in range(2):
        gain_mlp = gains[layer][1:2]
        a_blocks = links.spread(blocked(a))
        deps = [[], [], [], []]
        if planar and layer == 0:
            deps = [[], rings[0][:2] + w_proj[1:], rings[0][2:] + weights[0][1].arrays[1:], rings[1][:1]]
        elif planar:
            deps = [rings[1][1:] + weights[1][1].arrays[1:], [], [], []]
        q, k, v = project(meta, a_blocks, w_proj[layer], tables, (ext_q, ext_k), first_values, deps[0])
        o_rel, q = attend(meta, q, k, v, T, deps[1])
        o_blocks = links.exchange(o_rel, length)
        p = output_forward(meta, o_blocks, weights[layer], width, deps[2])
        if layer:
            dy = flat(links.swap_blocks(cotangent))
            deps[3] = [dy]
        y, h, b, *saved = mlp_forward(
            meta, x, p, links.sibling(p), gain_mlp, weights[layer], batches, hidden, out_rows, deps[3]
        )
        kept.append((x, a_blocks, q, k, v, o_rel, o_blocks, h, b, saved))
        x = (h + (y.astype(F32) + links.sibling(y).astype(F32))).astype(BF)
        if layer == 0:
            a, first_values = norm_low(x.astype(F32), gains[1][0:1]), v
    activations = links.swap_blocks(blocked(x))

    first_grad = None
    mlp_sums, out_sums, proj_sums, gain_sums, sums = [None] * 2, [None] * 2, [None] * 2, [None] * 2, [None] * 2
    for layer in (1, 0):
        gain_attn, gain_mlp = gains[layer][0:1], gains[layer][1:2]
        x, a_blocks, q, k, v, o_rel, o_blocks, h, b, saved = kept[layer]
        dy_low = dy.astype(BF)
        due = {name: [] for name in ("middle", "attend", "project")}
        before = sums[1] if planar and layer == 0 else None
        *parts, db = mlp_backward(meta, dy_low, b, saved, weights[layer], batches, out_rows, DP, [])
        if before:
            due["middle"] = passing
            due["attend"] = before.stage(2, parts[0])
        dh, mlp_gain_grad, do_rel, out_part = middle(
            meta, dy, db, links.sibling(db), h, gain_mlp, o_blocks, weights[layer], DP, due["middle"]
        )
        do_blocks = links.exchange(do_rel, length)
        if planar:
            mine = sums[layer] = LayerSums(links, parts, out_part, rows, out_rows, order)
            begun = mine.first.begin() + mine.second.begin()
            due["attend"] = due["attend"] + begun[:2]
            due["project"] = mine.first.finish(do_rel)
            if before:
                due["project"] = due["project"] + before.stage(3, do_rel)
            else:
                due["attend"] = due["attend"] + [activations]
        back = attend_back(meta, q, k, v, o_rel, do_blocks, tables, first_grad, due["attend"])
        if planar:
            passing = mine.stage(0, back[0])
            if before:
                before.stage(4, back[0])
        if layer == 1:
            first_grad = back[3]
        near, far, dw = project_back(meta, a_blocks, back[:3], w_proj[layer], DP, due["project"])
        if planar:
            mine.proj = PlaneSum(links, dw)
            passing = passing + mine.stage(1, near)
            if before:
                before.stage(4)
                for number in (2, 3, 4, 4):
                    mine.stage(number)
        else:
            running = None
            for part in parts:
                for n in range(T // 2):
                    term = part[:, n * rows : (n + 1) * rows]
                    running = term if running is None else add_low(term, links.ring(running))
            mlp_sums[layer] = lax.psum_scatter(running, "dp", scatter_dimension=0, tiled=True)[0]
            running = None
            for n in order:
                term = out_part[:, n * out_rows : (n + 1) * out_rows]
                running = term if running is None else add_low(term, links.ring(running))
            out_sums[layer] = lax.psum_scatter(running, "dp", scatter_dimension=0, tiled=True)[0]
            proj_sums[layer] = lax.psum_scatter(dw, "dp", scatter_dimension=0, tiled=True)[0]
        da = flat(links.combine(near, far)).astype(F32)
        part, attn_gain_grad = norm_back(x.astype(F32), gain_attn, da)
        gain_sums[layer] = jnp.concatenate([attn_gain_grad, mlp_gain_grad])
        dy = dh + part
    if planar:
        mlp_sums = [item.mlp_ring.total for item in sums]
        out_sums = [item.out_ring.total for item in sums]
        proj_sums = [item.proj_total for item in sums]
    half_width = width // 2
    mine = blocked(dy)
    mine = lax.dynamic_slice_in_dim(mine, s * half_width, half_width, 2)
    give = lax.dynamic_index_in_dim(mine, 1 - links.r, 0, keepdims=False).astype(BF)
    input_grad = jnp.where((jnp.arange(2) == links.r)[:, None, None], mine, links.across(give).astype(F32)[None])

    halves = both_halves(links, [jnp.concatenate([mlp_sums[n], out_sums[n]]) for n in range(2)])
    joined = []
    for item in proj_sums:
        if out_rows % 128:
            item = item.reshape(-1, 3, 2, out_rows)
            sides = [item[:, :, e].reshape(-1, 3 * out_rows) for e in range(2)]
        else:
            sides = [item[:, : 3 * out_rows], item[:, 3 * out_rows :]]
        joined.append(add_low(sides[0], links.across(sides[1])))
    proj = [item.astype(F32) for item in both_halves(links, joined)]
    halves = [item.astype(F32) for item in halves]
    squares = sum(jnp.sum(item * item) for item in halves + proj)
    gain_mine = jnp.where(s == 0, gain_sums[0], gain_sums[1])
    line = jnp.where(jnp.arange(width)[None, :] == 0, squares, 0.0)
    summed = sum_everywhere(links, jnp.concatenate([gain_mine, line]))
    gain_total = summed[0:2]
    grad_norm = jnp.sqrt(summed[2, 0] + jnp.sum(gain_total * gain_total)).reshape(1)
    shard = width // (DP * T)
    gain_out = lax.dynamic_slice_in_dim(gain_total, (links.d * T + links.z) * shard, shard, 1)
    grads = [
        jnp.concatenate([item[m * hidden : (m + 1) * hidden] for item in halves]) for m in range(3)
    ]
    own_out = jnp.concatenate([item[rows:] for item in halves])
    own_proj = [
        jnp.concatenate([item[:, m * out_rows : (m + 1) * out_rows] for item in proj], axis=1) for m in range(3)
    ]
    return (
        activations,
        input_grad,
        own_proj[0][None],
        own_proj[1][None],
        own_proj[2][None],
        own_out[None],
        grads[0].T[None],
        grads[1].T[None],
        grads[2][None],
        gain_out[0:1],
        gain_out[1:2],
        grad_norm,
    )


def solution(mesh):
    return jax.shard_map(
        per_device,
        mesh=mesh,
        in_specs=(
            P("dp", "tensor", None),
            P("dp", None),
            P("dp", "tensor", None),
            P("section", None, "tensor"),
            P("section", None, "tensor"),
            P("section", None, "tensor"),
            P("section", "tensor", None),
            P("section", None, "tensor"),
            P("section", None, "tensor"),
            P("section", "tensor", None),
            P("section", None),
            P("section", None),
        ),
        out_specs=(
            P("dp", "tensor", None),
            P("dp", "tensor", "section"),
            P("section", "dp", "tensor"),
            P("section", "dp", "tensor"),
            P("section", "dp", "tensor"),
            P("section", "tensor", "dp"),
            P("section", "dp", "tensor"),
            P("section", "dp", "tensor"),
            P("section", "tensor", "dp"),
            P("section", ("dp", "tensor")),
            P("section", ("dp", "tensor")),
            P("section"),
        ),
        check_vma=False,
    )
```

```python
import functools
import math

import jax
import jax.numpy as jnp
import numpy as np
from jax import lax
from jax.experimental import pallas as pl
from jax.experimental.pallas import tpu as pltpu
from jax.sharding import PartitionSpec as P

HEAD = 64
EPS = 1e-05
ROPE_BASE = 10000.0
BIG = 1e30
LOG2E = math.log2(math.e)
BF = jnp.bfloat16
F32 = jnp.float32
ALL = ("section", "dp", "tensor")
VMEM_LIMIT = 60 * 1024 * 1024
STEP = 256
CHUNK = 32
STRIP = 256

COL_OF_REL, ABS_OF_REL, OUT_OF_ABS, ABS_OF_OUT, CHIP_OF_RING, SIDE_OF_RING, REL_OF_DP, SECTION = 0, 8, 16, 24, 32, 40, 48, 56
PLACES = 64


def nn(a, b):
    return jnp.dot(a, b, preferred_element_type=F32)


def nt(a, b):
    return lax.dot_general(a, b, (((1,), (1,)), ((), ())), preferred_element_type=F32)


def tn(a, b):
    return lax.dot_general(a, b, (((0,), (0,)), ((), ())), preferred_element_type=F32)


def vmem_spec():
    return pl.BlockSpec(memory_space=pltpu.VMEM)


def any_spec():
    return pl.BlockSpec(memory_space=pl.ANY)


def smem_spec():
    return pl.BlockSpec(memory_space=pltpu.SMEM)


def sds(shape, dtype):
    return jax.ShapeDtypeStruct(shape, dtype)


def cost(micros):
    return pl.CostEstimate(flops=int(micros * 1.15e9), bytes_accessed=0, transcendentals=0)


def params(**more):
    return pltpu.CompilerParams(vmem_limit_bytes=VMEM_LIMIT, **more)


def call(kernel, deps, operands, *, in_specs, **rest):
    count, extra = len(operands), len(deps)

    def body(*refs):
        kernel(*refs[:count], *refs[count + extra :])

    return pl.pallas_call(body, in_specs=in_specs + [any_spec()] * extra, **rest)(*operands, *deps)


class Weights:
    def __init__(self, arrays, offset=0):
        self.arrays, self.offset = arrays, offset

    def copies(self, meta, refs, parts, sems, first):
        found = []
        for n, ref in enumerate(refs):
            for row, rows, target in parts:
                dst = target
                if len(refs) > 1:
                    width = ref.shape[1]
                    dst = target.at[:, pl.ds(pl.multiple_of(meta[COL_OF_REL + n] * width, width), width)]
                src = ref.at[pl.ds(self.offset + row, rows), :]
                found.append(pltpu.make_async_copy(src, dst, sems.at[first + len(found)]))
        return found


class Blocks:
    def __init__(self, arrays, places, by_section=()):
        self.arrays, self.places, self.by_section = arrays, places, by_section

    def copies(self, meta, refs, target, sems, first):
        found = []
        for i, (n, place) in enumerate(self.places):
            place = meta[SECTION] ^ place if i in self.by_section else place
            found.append(pltpu.make_async_copy(refs[n].at[place], target(i), sems.at[first + i]))
        return found


def unique(weights):
    operands, places = [], []
    for item in weights:
        mine = []
        for array in item.arrays:
            for n, other in enumerate(operands):
                if other is array:
                    mine.append(n)
                    break
            else:
                mine.append(len(operands))
                operands.append(array)
        places.append(mine)
    return operands, places


def start_all(copies):
    for copy in copies:
        copy.start()
    return copies


def wait_all(copies):
    for copy in copies:
        copy.wait()


def swap_halves(tile):
    lane = lax.broadcasted_iota(jnp.int32, tile.shape, 1)
    return jnp.where(lane % HEAD < HEAD // 2, pltpu.roll(tile, 128 - HEAD // 2, 1), pltpu.roll(tile, HEAD // 2, 1))


def column_of(part, pair, cols):
    side = cols // 2
    if side % 128:
        return part * cols + pair * 128
    per_side = side // 128
    return (pair // per_side * 3 + part) * side + pair % per_side * 128


def qkv_kernel(a_blocks, later, meta, *refs):
    blocks, held = len(a_blocks.places), len(a_blocks.arrays)
    a_refs = refs[:held]
    w_ref, cos_ref, sin_ref, extq_ref, extk_ref = refs[held : held + 5]
    rest = refs[held + 5 :]
    if later:
        first_ref, rest = rest[0], rest[1:]
    outs, (a_scr, w_scr, q_scr, k_scr, v_scr, cos_scr, sin_scr, extq_scr, extk_scr), rest = rest[:3], rest[3:12], rest[12:]
    if later:
        first_scr, rest = rest[0], rest[1:]
    sems, out_sems = rest
    length = a_scr.shape[1]
    cols = w_ref.shape[1] // 3
    loads = [
        pltpu.make_async_copy(w_ref, w_scr, sems.at[0]),
        pltpu.make_async_copy(cos_ref, cos_scr, sems.at[2]),
        pltpu.make_async_copy(sin_ref, sin_scr, sems.at[3]),
        pltpu.make_async_copy(extq_ref, extq_scr, sems.at[4]),
        pltpu.make_async_copy(extk_ref, extk_scr, sems.at[5]),
    ]
    if later:
        loads.append(pltpu.make_async_copy(first_ref, first_scr, sems.at[6]))
    more = a_blocks.copies(meta, a_refs, lambda i: a_scr.at[i], sems, 7)
    start_all(loads)
    start_all(more)
    lane = lax.broadcasted_iota(jnp.int32, (length, 128), 1)
    low = lane < HEAD
    ones_even = ((lane >= HEAD + 4) & (lane < HEAD + 7)).astype(F32)
    ones_odd = ((lane >= 4) & (lane < 7)).astype(F32)
    stores = []
    for i in range(blocks):
        start = pl.multiple_of(meta[ABS_OF_REL + i] * length, length)
        rows = pl.ds(start, length)
        if i == 0:
            wait_all(loads)
        more[i].wait()
        a = a_scr[i]
        cosine, sine = cos_scr[rows, :], sin_scr[rows, :]
        whole = nn(a, w_scr[...])
        for part, out in ((0, q_scr), (1, k_scr), (2, v_scr)):
            for pair in range(cols // 128):
                column = column_of(part, pair, cols)
                tile = whole[:, column : column + 128]
                if part < 2:
                    tile = tile * cosine + swap_halves(tile) * sine
                    ext = extq_scr if part == 0 else extk_scr
                    if part == 0:
                        tile = tile * (LOG2E * HEAD**-0.5)
                    even_ext = ext[rows, :128].astype(F32)
                    odd_ext = ext[rows, 128:].astype(F32)
                else:
                    if later:
                        first = jnp.where(
                            low,
                            first_scr[2 * pair, rows, :].astype(F32),
                            first_scr[2 * pair + 1, rows, :].astype(F32),
                        )
                        tile = 0.5 * tile + 0.5 * first
                    even_ext, odd_ext = ones_even, ones_odd
                out[i, 2 * pair] = jnp.where(low, tile, even_ext).astype(BF)
                out[i, 2 * pair + 1] = jnp.where(low, odd_ext, tile).astype(BF)
        for n, (scr, out) in enumerate(zip((q_scr, k_scr, v_scr), outs)):
            stores += start_all([pltpu.make_async_copy(scr.at[i], out.at[:, rows, :], out_sems.at[3 * i + n])])
    wait_all(stores)


def project(meta, a_blocks, w, tables, exts, first, deps):
    blocks, (_, length, width) = len(a_blocks.places), a_blocks.arrays[0].shape
    cols = w.shape[1] // 3
    heads = cols // HEAD
    seq = blocks * length
    out = sds((heads, seq, 128), BF)
    later = first is not None
    operands = [meta, *a_blocks.arrays, w, *tables, *exts] + ([first] if later else [])
    block = pltpu.VMEM((blocks, heads, length, 128), BF)
    return call(
        functools.partial(qkv_kernel, a_blocks, later),
        deps,
        operands,
        out_shape=(out, out, out),
        in_specs=[smem_spec()] + [any_spec()] * (len(operands) - 1),
        out_specs=(any_spec(),) * 3,
        scratch_shapes=[
            pltpu.VMEM((blocks, length, width), BF),
            pltpu.VMEM(w.shape, BF),
            block,
            block,
            block,
            pltpu.VMEM((seq, 128), F32),
            pltpu.VMEM((seq, 128), F32),
            pltpu.VMEM((seq, 256), BF),
            pltpu.VMEM((seq, 256), BF),
        ]
        + ([pltpu.VMEM(out.shape, BF)] if later else [])
        + [pltpu.SemaphoreType.DMA((blocks + 7,)), pltpu.SemaphoreType.DMA((3 * blocks,))],
        compiler_params=params(),
        cost_estimate=cost(10),
        name="project",
    )


def project_back_kernel(a_blocks, dp_blocks, meta, *refs):
    blocks, held = len(a_blocks.places), len(a_blocks.arrays)
    a_refs = refs[:held]
    dq_ref, dk_ref, dv_ref, w_ref, near_ref, far_ref, dw_ref = refs[held : held + 7]
    a_scr, d_scr, w_scr, da_scr, dw_scr, sems, out_sems = refs[held + 7 :]
    _, length, width = da_scr.shape
    cols = dq_ref.shape[1]
    loads = [pltpu.make_async_copy(w_ref, w_scr, sems.at[0])]
    for part, ref in enumerate((dq_ref, dk_ref, dv_ref)):
        for pair in range(cols // 128):
            target = d_scr.at[:, pl.ds(column_of(part, pair, cols), 128)]
            source = ref.at[:, pl.ds(pair * 128, 128)]
            loads.append(pltpu.make_async_copy(source, target, sems.at[len(loads)]))

    def place(i):
        start = pl.multiple_of(meta[ABS_OF_REL + i] * length, length)
        return a_scr.at[pl.ds(start, length)]

    more = a_blocks.copies(meta, a_refs, place, sems, len(loads))
    start_all(loads)
    start_all(more)
    wait_all(loads)
    order = list(range(1, blocks, 2)) + list(range(2, blocks, 2)) + [0]
    stores = []
    for i in order:
        start = pl.multiple_of(meta[ABS_OF_REL + i] * length, length)
        da_scr[i] = nt(d_scr[pl.ds(start, length), :], w_scr[...]).astype(BF)
        out = far_ref if i % 2 else near_ref
        stores += start_all([pltpu.make_async_copy(da_scr.at[i], out.at[i // 2], out_sems.at[i])])
    wait_all(more)
    size = width // dp_blocks
    for j in range(dp_blocks):
        dw_scr[meta[REL_OF_DP + j]] = tn(a_scr[:, j * size : (j + 1) * size], d_scr[...]).astype(BF)
    stores += start_all([pltpu.make_async_copy(dw_scr, dw_ref, out_sems.at[blocks])])
    wait_all(stores)


def project_back(meta, a_blocks, grads, w, dp_blocks, deps):
    blocks, (_, length, width) = len(a_blocks.places), a_blocks.arrays[0].shape
    cols = w.shape[1]
    seq = blocks * length
    half = sds((blocks // 2, length, width), BF)
    dw = (dp_blocks, width // dp_blocks, cols)
    return call(
        functools.partial(project_back_kernel, a_blocks, dp_blocks),
        deps,
        [meta, *a_blocks.arrays, *grads, w],
        out_shape=(half, half, sds(dw, BF)),
        in_specs=[smem_spec()] + [any_spec()] * (len(a_blocks.arrays) + 4),
        out_specs=(any_spec(),) * 3,
        scratch_shapes=[
            pltpu.VMEM((seq, width), BF),
            pltpu.VMEM((seq, cols), BF),
            pltpu.VMEM(w.shape, BF),
            pltpu.VMEM((blocks, length, width), BF),
            pltpu.VMEM(dw, BF),
            pltpu.SemaphoreType.DMA((blocks + 1 + cols // 128,)),
            pltpu.SemaphoreType.DMA((blocks + 1,)),
        ],
        compiler_params=params(),
        cost_estimate=cost(12),
        name="project_back",
    )


def three_parts(value):
    high = value.astype(BF).astype(F32)
    middle = (value - high).astype(BF).astype(F32)
    return high, middle, value - high - middle


def with_parts(base, value, odd):
    lane = lax.broadcasted_iota(jnp.int32, base.shape, 1)
    offset = 4 if odd else HEAD + 4
    high, middle, rest = three_parts(value)
    out = jnp.where(lane == offset, high, base)
    out = jnp.where(lane == offset + 1, middle, out)
    return jnp.where(lane == offset + 2, rest, out)


def attend_kernel(block, meta, q_ref, k_ref, v_ref, o_ref, ql_ref, vt_scr, tot_scr, top_scr, s_scr, p_scr):
    seq = q_ref.shape[1]
    length = o_ref.shape[1]
    key_row = lax.broadcasted_iota(jnp.int32, (STEP, block), 0)
    query_col = lax.broadcasted_iota(jnp.int32, (STEP, block), 1)
    for e in range(2):
        vt_scr[e] = v_ref[e].T

    def score(i, e):
        q = q_ref[e, i * block : (i + 1) * block, :]
        best = None
        for lo in range(0, (i + 1) * block, STEP):
            tile = nt(k_ref[e, lo : lo + STEP, :], q)
            if lo >= i * block:
                tile = jnp.where(key_row + (lo - i * block) <= query_col, tile, -BIG)
            s_scr[e, i % 2, lo : lo + STEP, :] = tile
            best = tile if best is None else jnp.maximum(best, tile)
        top_scr[e, :, i * block : (i + 1) * block] = best.max(axis=0, keepdims=True)

    def weigh(i, e):
        cols = slice(i * block, (i + 1) * block)
        top = top_scr[e, :, cols]
        for lo in range(0, (i + 1) * block, STEP):
            p_scr[e, lo : lo + STEP, :] = jnp.exp2(s_scr[e, i % 2, lo : lo + STEP, :] - top).astype(BF)
        tot_scr[e, :, cols] = nn(vt_scr[e, :, : (i + 1) * block], p_scr[e, : (i + 1) * block, :])

    count = seq // block
    for i in range(count + 1):
        for e in range(2):
            if i < count:
                score(i, e)
            if i > 0:
                weigh(i - 1, e)
    low = lax.broadcasted_iota(jnp.int32, (length, 128), 1) < HEAD
    lane = lax.broadcasted_iota(jnp.int32, (length, 128), 1)
    row = lax.broadcasted_iota(jnp.int32, (128, length), 0)
    for i in range(seq // length):
        rows = slice(i * length, (i + 1) * length)
        results = []
        for e in range(2):
            place = 4 if e else HEAD + 4
            total = tot_scr[e, :, rows]
            weight = total[place : place + 1, :]
            total = total * (1.0 / weight)
            for n, value in enumerate(three_parts(-(top_scr[e, :, rows] + jnp.log2(weight)))):
                total = jnp.where(row == place + n, value, total)
            turned = total.T
            results.append(turned)
            parts = (lane >= place) & (lane < place + 3)
            ql_ref[e, rows, :] = jnp.where(parts, turned, q_ref[e, rows, :].astype(F32)).astype(BF)
        o_ref[meta[OUT_OF_ABS + i]] = jnp.where(low, results[0], results[1]).astype(BF)


def attend(meta, q, k, v, blocks, deps):
    heads, seq, _ = q.shape
    pairs = heads // 2
    length = seq // blocks
    head_spec = pl.BlockSpec((2, seq, 128), lambda p: (p, 0, 0))
    return call(
        functools.partial(attend_kernel, min(256, length)),
        deps,
        [meta, q, k, v],
        grid=(pairs,),
        out_shape=(sds((blocks, length, pairs * 128), BF), sds(q.shape, BF)),
        in_specs=[smem_spec(), head_spec, head_spec, head_spec],
        out_specs=(pl.BlockSpec((blocks, length, 128), lambda p: (0, 0, p)), head_spec),
        scratch_shapes=[
            pltpu.VMEM((2, 128, seq), BF),
            pltpu.VMEM((2, 128, seq), F32),
            pltpu.VMEM((2, 1, seq), F32),
            pltpu.VMEM((2, 2, seq, min(256, length)), F32),
            pltpu.VMEM((2, seq, min(256, length)), BF),
        ],
        compiler_params=params(),
        cost_estimate=cost(14.5),
        name="attend",
    )


def attend_back_kernel(block, blocks, later, meta, q_ref, k_ref, v_ref, o_ref, *refs):
    do_refs = refs[:blocks]
    cos_ref, sin_ref = refs[blocks : blocks + 2]
    rest = refs[blocks + 2 :]
    if not later:
        first_ref, rest = rest[0], rest[1:]
    dq_ref, dk_ref, dv_ref = rest[:3]
    rest = rest[3:]
    if later:
        first_out, rest = rest[0], rest[1:]
    do_scr, dq_scr, dk_scr, dv_scr, kt_scr, p_scr, ds_scr = rest
    seq = q_ref.shape[1]
    length = o_ref.shape[1]
    lane = lax.broadcasted_iota(jnp.int32, (length, 128), 1)
    low = lane < HEAD
    for i in range(blocks):
        start = pl.multiple_of(meta[ABS_OF_OUT + i] * length, length)
        rows = pl.ds(start, length)
        do = do_refs[i][...].astype(F32)
        product = do * o_ref[i].astype(F32)
        for e in range(2):
            mine = low if e == 0 else jnp.logical_not(low)
            delta = jnp.sum(jnp.where(mine, product, 0.0), axis=1, keepdims=True)
            do_scr[e, rows, :] = with_parts(jnp.where(mine, do, 0.0), -delta, e == 1).astype(BF)
    key_row = lax.broadcasted_iota(jnp.int32, (STEP, block), 0)
    query_col = lax.broadcasted_iota(jnp.int32, (STEP, block), 1)
    for e in range(2):
        kt_scr[e] = k_ref[e].T
    count = seq // block

    def weigh(i, e):
        cols = slice(i * block, (i + 1) * block)
        q = q_ref[e, cols, :]
        do = do_scr[e, cols, :]
        for lo in range(0, (i + 1) * block, STEP):
            rows = slice(lo, lo + STEP)
            scores = nt(k_ref[e, rows, :], q)
            if lo >= i * block:
                scores = jnp.where(key_row + (lo - i * block) <= query_col, scores, -BIG)
            prob = jnp.exp2(scores)
            p_scr[e, rows, cols] = prob.astype(BF)
            ds_scr[e, rows, cols] = (prob * nt(v_ref[e, rows, :], do)).astype(BF)

    def query_grad(i, e):
        cols = slice(i * block, (i + 1) * block)
        dq_scr[e, :, cols] = nn(kt_scr[e, :, : (i + 1) * block], ds_scr[e, : (i + 1) * block, cols])

    def key_grads(i, e):
        rows, cols = slice(i * block, (i + 1) * block), slice(i * block, seq)
        dv_scr[e, rows, :] = nn(p_scr[e, rows, cols], do_scr[e, cols, :])
        dk_scr[e, rows, :] = nn(ds_scr[e, rows, cols], q_ref[e, cols, :])

    for i in range(count + 1):
        for e in range(2):
            if i < count:
                weigh(i, e)
            if i > 0:
                query_grad(i - 1, e)
    for i in range(count):
        for e in range(2):
            key_grads(i, e)
    for i in range(blocks):
        rows = slice(i * length, (i + 1) * length)
        cosine, sine = cos_ref[rows, :], sin_ref[rows, :]
        dq = jnp.where(low, dq_scr[0, :, rows].T, dq_scr[1, :, rows].T) * (HEAD**-0.5)
        dk = jnp.where(low, dk_scr[0, rows, :], dk_scr[1, rows, :]) * (1.0 / LOG2E)
        dv = jnp.where(low, dv_scr[0, rows, :], dv_scr[1, rows, :])
        dq_ref[rows, :] = (dq * cosine - swap_halves(dq) * sine).astype(BF)
        dk_ref[rows, :] = (dk * cosine - swap_halves(dk) * sine).astype(BF)
        if later:
            dv_ref[rows, :] = (0.5 * dv).astype(BF)
            first_out[rows, :] = 0.5 * dv
        else:
            dv_ref[rows, :] = (dv + first_ref[rows, :]).astype(BF)


def attend_back(meta, q, k, v, o, do_blocks, tables, first, deps):
    heads, seq, _ = q.shape
    pairs = heads // 2
    blocks, length, cols = o.shape
    later = first is None
    head_spec = pl.BlockSpec((2, seq, 128), lambda p: (p, 0, 0))
    col_spec = pl.BlockSpec((seq, 128), lambda p: (0, p))
    table_spec = pl.BlockSpec((seq, 128), lambda p: (0, 0))
    out = sds((seq, cols), BF)
    return call(
        functools.partial(attend_back_kernel, min(256, length), blocks, later),
        deps,
        [meta, q, k, v, o, *[do_blocks.arrays[n] for n, _ in do_blocks.places], *tables, *([] if later else [first])],
        grid=(pairs,),
        out_shape=(out, out, out) + ((sds((seq, cols), F32),) if later else ()),
        in_specs=[smem_spec(), head_spec, head_spec, head_spec]
        + [pl.BlockSpec((blocks, length, 128), lambda p: (0, 0, p))]
        + [pl.BlockSpec((None, length, 128), functools.partial(lambda n, p: (n, 0, p), n)) for _, n in do_blocks.places]
        + [table_spec] * 2
        + ([] if later else [col_spec]),
        out_specs=(col_spec,) * (4 if later else 3),
        scratch_shapes=[
            pltpu.VMEM((2, seq, 128), BF),
            pltpu.VMEM((2, 128, seq), F32),
            pltpu.VMEM((2, seq, 128), F32),
            pltpu.VMEM((2, seq, 128), F32),
            pltpu.VMEM((2, 128, seq), BF),
            pltpu.VMEM((2, seq, seq), BF),
            pltpu.VMEM((2, seq, seq), BF),
        ],
        compiler_params=params(),
        cost_estimate=cost(29.5),
        name="attend_back",
    )


def place_output(weights, places, meta, refs, target, sems, first):
    found = []
    rows = target.shape[1] // 2
    for k, item in enumerate(weights):
        side = pl.multiple_of(meta[SIDE_OF_RING + k] * rows, rows)
        part = (0, rows, target.at[meta[CHIP_OF_RING + k], pl.ds(side, rows)])
        found += item.copies(meta, [refs[n] for n in places[k]], [part], sems, first + 4 * k)
    return found


def output_kernel(o_blocks, weights, places, meta, *refs):
    o_refs, refs = refs[: len(o_blocks.arrays)], refs[len(o_blocks.arrays) :]
    number = len({n for place in places for n in place})
    w_refs, (p_ref, o_scr, w_scr, sems) = refs[:number], refs[number:]
    count = len(o_blocks.places)
    length = o_scr.shape[1] // 2
    loads = o_blocks.copies(meta, o_refs, lambda i: o_scr.at[i // 2, pl.ds(i % 2 * length, length)], sems, 0)
    loads += place_output(weights, places, meta, w_refs, w_scr, sems, count)
    wait_all(start_all(loads))
    for f in range(2):
        rows = slice(f * length, (f + 1) * length)
        total = nn(o_scr[0, rows, :], w_scr[0])
        for n in range(1, count // 2):
            total += nn(o_scr[n, rows, :], w_scr[n])
        p_ref[rows, :] = total.astype(BF)


def output_forward(meta, o_blocks, weights, width, deps):
    count = len(o_blocks.places)
    _, length, cols = o_blocks.arrays[0].shape
    operands, places = unique(weights)
    return call(
        functools.partial(output_kernel, o_blocks, weights, places),
        deps,
        [meta, *o_blocks.arrays, *operands],
        out_shape=sds((2 * length, width), BF),
        in_specs=[smem_spec()] + [any_spec()] * (len(o_blocks.arrays) + len(operands)),
        out_specs=vmem_spec(),
        scratch_shapes=[
            pltpu.VMEM((count // 2, 2 * length, cols), BF),
            pltpu.VMEM((count // 2, cols, width), BF),
            pltpu.SemaphoreType.DMA((5 * count,)),
        ],
        compiler_params=params(),
        cost_estimate=cost(5),
        name="output",
    )


def place_hidden(batch, weights, places, meta, refs, target, sems, first, row):
    hidden = target.shape[1] // len(batch)
    found = []
    for n, k in enumerate(batch):
        parts = [(row + m * hidden, hidden, target.at[m, pl.ds(n * hidden, hidden)]) for m in range(3)]
        found += weights[k].copies(meta, [refs[i] for i in places[k]], parts, sems, first + 12 * n)
    return found


def mlp_kernel(batches, weights, places, row, meta, x_ref, p_ref, other_ref, gain_ref, *refs):
    number = len({n for place in places for n in place})
    w_refs, refs = refs[:number], refs[number:]
    count = len(batches)
    y_ref, h_ref, b_ref = refs[:3]
    g_refs, u_refs, refs = refs[3 : 3 + count], refs[3 + count : 3 + 2 * count], refs[3 + 2 * count :]
    w_scr, sems = refs
    first = [12 * sum(len(other) for other in batches[:n]) for n in range(count)]

    def loads(n):
        return place_hidden(batches[n], weights, places, meta, w_refs, w_scr.at[n], sems, first[n], row)

    @pl.when(pl.program_id(0) == 0)
    def _():
        for n in range(count):
            start_all(loads(n))

    gain = gain_ref[...]
    for start in range(0, x_ref.shape[0], CHUNK):
        rows = slice(start, start + CHUNK)
        h = x_ref[rows, :].astype(F32) + (p_ref[rows, :].astype(F32) + other_ref[rows, :].astype(F32))
        h_ref[rows, :] = h
        inverse = lax.rsqrt(jnp.mean(h * h, axis=1, keepdims=True) + EPS)
        b_ref[rows, :] = (h * inverse * gain).astype(BF)

    @pl.when(pl.program_id(0) == 0)
    def _():
        for n in range(count):
            wait_all(loads(n))

    for start in range(0, x_ref.shape[0], STRIP):
        rows = slice(start, start + STRIP)
        b = b_ref[rows, :]
        total = None
        for n in range(count):
            g = nt(b, w_scr[n, 0])
            u = nt(b, w_scr[n, 1])
            g_refs[n][rows, :] = g.astype(BF)
            u_refs[n][rows, :] = u.astype(BF)
            m = (g * jax.nn.sigmoid(g) * u).astype(BF)
            term = nn(m, w_scr[n, 2])
            total = term if total is None else total + term
        y_ref[rows, :] = total.astype(BF)


def mlp_forward(meta, x, p, other, gain, weights, batches, hidden, row, deps):
    rows, width = x.shape
    operands, places = unique(weights)
    size = [len(batch) * hidden for batch in batches]
    quarters = sum(len(batch) for batch in batches)
    low = sds((rows, width), BF)
    saved = tuple(sds((rows, n), BF) for n in size)
    block = min(256, rows)

    def by_rows(n):
        return pl.BlockSpec((block, n), lambda i: (i, 0))

    return call(
        functools.partial(mlp_kernel, batches, weights, places, row),
        deps,
        [meta, x, p, other, gain, *operands],
        grid=(rows // block,),
        out_shape=(low, sds((rows, width), F32), low) + saved + saved,
        in_specs=[smem_spec()]
        + [by_rows(width)] * 3
        + [pl.BlockSpec((1, width), lambda i: (0, 0))]
        + [any_spec()] * len(operands),
        out_specs=(by_rows(width),) * 3 + tuple(by_rows(n) for n in size) * 2,
        scratch_shapes=[
            pltpu.VMEM((len(batches), 3, size[0], width), BF),
            pltpu.SemaphoreType.DMA((12 * quarters,)),
        ],
        compiler_params=params(),
        cost_estimate=cost(19),
        name="mlp",
    )


def mlp_back_kernel(batches, weights, places, row, meta, dy_ref, b_ref, *refs):
    count = len(batches)
    g_refs, u_refs, refs = refs[:count], refs[count : 2 * count], refs[2 * count :]
    number = len({n for place in places for n in place})
    w_refs, refs = refs[:number], refs[number:]
    out_refs, refs = refs[:count], refs[count:]
    db_ref, dy_scr, b_scr, g_scr, u_scr, w_scr, low_scr, grad_scr, sems, out_sems = refs
    dy_load = pltpu.make_async_copy(dy_ref, dy_scr, sems.at[0])
    b_load = pltpu.make_async_copy(b_ref, b_scr, sems.at[1])
    dy_load.start()
    loads, used = [], 2
    for n, batch in enumerate(batches):
        group = place_hidden(batch, weights, places, meta, w_refs, w_scr.at[n], sems, used, row)
        used += 12 * len(batch)
        for source, target in ((g_refs[n], g_scr.at[n]), (u_refs[n], u_scr.at[n])):
            group.append(pltpu.make_async_copy(source, target, sems.at[used]))
            used += 1
        loads.append(start_all(group))
    b_load.start()
    total_rows, width = dy_scr.shape
    hidden = w_scr.shape[2] // len(batches[0])
    columns, _, size = out_refs[0].shape
    stores = []
    dy_load.wait()
    for n, batch in enumerate(batches):
        wait_all(loads[n])
        for start in range(0, total_rows, STRIP):
            rows = slice(start, start + STRIP)
            dm = nt(dy_scr[rows, :], w_scr[n, 2])
            g = g_scr[n, rows, :].astype(F32)
            u = u_scr[n, rows, :].astype(F32)
            gate = jax.nn.sigmoid(g)
            active = g * gate
            low_scr[n, 0, rows, :] = (dm * u * (gate + active * (1.0 - gate))).astype(BF)
            low_scr[n, 1, rows, :] = (dm * active).astype(BF)
            low_scr[n, 2, rows, :] = (active * u).astype(BF)
    b_load.wait()
    for n, batch in enumerate(batches):
        for m in range(3):
            grad_scr[n, m] = tn(low_scr[n, m], dy_scr[...] if m == 2 else b_scr[...]).astype(BF)
            for q in range(len(batch)):
                for j in range(columns):
                    copy = pltpu.make_async_copy(
                        grad_scr.at[n, m, pl.ds(q * hidden, hidden), pl.ds(j * size, size)],
                        out_refs[n].at[meta[REL_OF_DP + j], pl.ds((q * 3 + m) * hidden, hidden), :],
                        out_sems.at[((n * 3 + m) * len(batch) + q) * columns + j],
                    )
                    copy.start()
                    stores.append(copy)
    for start in range(0, total_rows, 256):
        rows = slice(start, start + 256)
        db = None
        for n in range(count):
            term = nn(low_scr[n, 0, rows, :], w_scr[n, 0]) + nn(low_scr[n, 1, rows, :], w_scr[n, 1])
            db = term if db is None else db + term
        db_ref[rows, :] = db.astype(BF)
    wait_all(stores)


def mlp_backward(meta, dy, b, saved, weights, batches, row, dp_blocks, deps):
    rows, width = b.shape
    count = len(batches)
    size = saved[0].shape[1]
    operands, places = unique(weights)
    copies = sum(12 * len(batch) + 2 for batch in batches)
    return call(
        functools.partial(mlp_back_kernel, batches, weights, places, row),
        deps,
        [meta, dy, b, *saved, *operands],
        out_shape=(sds((dp_blocks, 3 * size, width // dp_blocks), BF),) * count + (sds((rows, width), BF),),
        in_specs=[smem_spec()] + [any_spec()] * (2 + 2 * count + len(operands)),
        out_specs=(any_spec(),) * count + (vmem_spec(),),
        scratch_shapes=[
            pltpu.VMEM((rows, width), BF),
            pltpu.VMEM((rows, width), BF),
            pltpu.VMEM((count, rows, size), BF),
            pltpu.VMEM((count, rows, size), BF),
            pltpu.VMEM((count, 3, size, width), BF),
            pltpu.VMEM((count, 3, rows, size), BF),
            pltpu.VMEM((count, 3, size, width), BF),
            pltpu.SemaphoreType.DMA((2 + copies,)),
            pltpu.SemaphoreType.DMA((3 * dp_blocks * sum(len(batch) for batch in batches),)),
        ],
        compiler_params=params(),
        cost_estimate=cost(28),
        name="mlp_back",
    )


def norm_back(values, gain, grads):
    inverse = lax.rsqrt(jnp.mean(values * values, axis=1, keepdims=True) + EPS)
    normed = values * inverse
    scaled = grads * gain
    gain_grad = jnp.sum(grads * normed, axis=0, keepdims=True)
    return inverse * (scaled - normed * jnp.mean(scaled * normed, axis=1, keepdims=True)), gain_grad


def middle_kernel(o_blocks, weights, places, meta, dy_ref, db_ref, other_ref, h_ref, gain_ref, *refs):
    o_refs, refs = refs[: len(o_blocks.arrays)], refs[len(o_blocks.arrays) :]
    number = len({n for place in places for n in place})
    w_refs, refs = refs[:number], refs[number:]
    dh_ref, gain_out, do_ref, grad_ref, w_scr, o_scr, low_scr, grad_scr, sems, out_sems = refs
    count = len(o_blocks.places)
    length = o_scr.shape[1] // 2
    step, steps = pl.program_id(0), pl.num_programs(0)

    def loads():
        found = o_blocks.copies(meta, o_refs, lambda i: o_scr.at[i // 2, pl.ds(i % 2 * length, length)], sems, 0)
        return found + place_output(weights, places, meta, w_refs, w_scr, sems, count)

    @pl.when(step == 0)
    def _():
        start_all(loads())
        gain_out[...] = jnp.zeros_like(gain_out)

    gain = gain_ref[...]
    block = dy_ref.shape[0]
    first = pl.multiple_of(step * block, block)
    total = None
    for start in range(0, block, CHUNK):
        rows = slice(start, start + CHUNK)
        db = db_ref[rows, :].astype(F32) + other_ref[rows, :].astype(F32)
        part, gain_grad = norm_back(h_ref[rows, :], gain, db)
        dh = dy_ref[rows, :].astype(F32) + part
        dh_ref[rows, :] = dh
        low_scr[pl.ds(first + start, CHUNK), :] = dh.astype(BF)
        total = gain_grad if total is None else total + gain_grad
    gain_out[...] += total

    @pl.when(step == 0)
    def _():
        wait_all(loads())

    low = low_scr[pl.ds(first, block), :]
    for n in range(count // 2):
        do_ref[n] = nt(low, w_scr[n]).astype(BF)

    @pl.when(step == steps - 1)
    def _():
        for n in range(count // 2):
            grad_scr[n] = tn(o_scr[n], low_scr[...]).astype(BF)
        stores = []
        columns = grad_ref.shape[0]
        size = grad_ref.shape[2]
        rows = o_scr.shape[2] // 2
        for k in range(count):
            side = pl.multiple_of(meta[SIDE_OF_RING + k] * rows, rows)
            for j in range(columns):
                stores.append(
                    pltpu.make_async_copy(
                        grad_scr.at[meta[CHIP_OF_RING + k], pl.ds(side, rows), pl.ds(j * size, size)],
                        grad_ref.at[meta[REL_OF_DP + j], pl.ds(k * rows, rows), :],
                        out_sems.at[k * columns + j],
                    )
                )
        wait_all(start_all(stores))


def middle(meta, dy, db, other, h, gain, o_blocks, weights, dp_blocks, deps):
    count = len(o_blocks.places)
    _, length, cols = o_blocks.arrays[0].shape
    width = h.shape[1]
    operands, places = unique(weights)
    block = 256
    by_rows = pl.BlockSpec((block, width), lambda i: (i, 0))
    fixed = pl.BlockSpec((1, width), lambda i: (0, 0))
    return call(
        functools.partial(middle_kernel, o_blocks, weights, places),
        deps,
        [meta, dy, db, other, h, gain, *o_blocks.arrays, *operands],
        grid=(2 * length // block,),
        out_shape=(
            sds((2 * length, width), F32),
            sds((1, width), F32),
            sds((count // 2, 2 * length, cols), BF),
            sds((dp_blocks, count * cols // 2, width // dp_blocks), BF),
        ),
        in_specs=[smem_spec()]
        + [by_rows] * 4
        + [fixed]
        + [any_spec()] * (len(o_blocks.arrays) + len(operands)),
        out_specs=(by_rows, fixed, pl.BlockSpec((count // 2, block, cols), lambda i: (0, i, 0)), any_spec()),
        scratch_shapes=[
            pltpu.VMEM((count // 2, cols, width), BF),
            pltpu.VMEM((count // 2, 2 * length, cols), BF),
            pltpu.VMEM((2 * length, width), BF),
            pltpu.VMEM((count // 2, cols, width), BF),
            pltpu.SemaphoreType.DMA((5 * count,)),
            pltpu.SemaphoreType.DMA((count * dp_blocks,)),
        ],
        compiler_params=params(),
        cost_estimate=cost(13),
        name="middle",
    )


def add_low(*terms):
    total = terms[0].astype(F32)
    for term in terms[1:]:
        total = total + term.astype(F32)
    return total.astype(BF)


def hold(x, *after):
    return lax.optimization_barrier((x, *after))[0] if after else x


class Links:
    def __init__(self):
        self.T = lax.axis_size("tensor")
        self.DP = lax.axis_size("dp")
        self.G = self.T // 2
        self.s = lax.axis_index("section")
        self.d = lax.axis_index("dp")
        self.z = lax.axis_index("tensor")
        self.r = self.z // self.G
        self.home = self.s == self.r
        self.planar = self.DP == 4 and self.T == 4
        self.order = [0] + list(range(1, self.T, 2)) + list(range(self.T - 2, 0, -2))

    def sibling(self, x):
        return lax.ppermute(x, "section", [(0, 1), (1, 0)])

    def ring(self, x):
        order = self.order
        return lax.ppermute(x, "tensor", [(order[i], order[(i + 1) % self.T]) for i in range(self.T)])

    def back(self, x, k):
        order = self.order
        return lax.ppermute(x, "tensor", [(order[i], order[(i - k) % self.T]) for i in range(self.T)])

    def along(self, x, bit):
        return lax.ppermute(x, "dp", [(i, i ^ bit) for i in range(self.DP)])

    def across(self, x):
        return lax.ppermute(x, "tensor", [(z, (z + self.G) % self.T) for z in range(self.T)])

    def shift(self, x, k):
        pairs = [(z, z // self.G * self.G + (z + k) % self.G) for z in range(self.T)]
        return lax.ppermute(x, "tensor", pairs)

    def swap_blocks(self, x, *after):
        pairs = []
        for s in range(2):
            z0 = s * self.G
            for z in range(z0, z0 + self.G):
                pairs.append((s * self.T + z, s * self.T + (z + self.G) % self.T))
        give = hold(lax.dynamic_index_in_dim(x, 1 - self.r, 0, keepdims=False), *after)
        return lax.ppermute(give, ("section", "tensor"), pairs)

    def swap_end(self, x, got):
        got = jnp.where(self.home, self.sibling(got), got)
        mine = (jnp.arange(2) == self.r)[:, None, None]
        return jnp.where(mine, x, got[None])

    def spread(self, x):
        give = lax.dynamic_index_in_dim(x, self.s, 0)
        arrays, places = [x], [(0, 0), (0, 1)]
        for k in range(1, self.G):
            got = self.shift(give, -k)
            arrays += [got, self.sibling(got)]
            places += [(len(arrays) - 2, 0), (len(arrays) - 1, 0)]
        return Blocks(arrays, places, (0, 1))

    def exchange(self, x, length):
        cols = x.shape[-1]
        arrays, places = [x.reshape(self.T, length, cols)], [(0, 0), (0, 1)] + [None] * (self.T - 2)
        for k in range(1, self.G):
            got = self.shift(x.reshape(self.G, 2 * length, cols)[k], k)
            chip = -k % self.G
            places[2 * chip], places[2 * chip + 1] = (len(arrays), 0), (len(arrays), 1)
            arrays.append(got.reshape(2, length, cols))
        return Blocks(arrays, places)

    def combine(self, near, far):
        got = self.sibling(far)
        terms, sent = [near[0], got[0]], []
        for k in range(1, self.G):
            sent.append(add_low(near[k], got[k]))
            terms.append(self.shift(sent[-1], k))
        mine = add_low(*terms)
        both = (jnp.arange(2) == self.s)[:, None, None]
        return jnp.where(both, mine[None], self.sibling(mine)[None]), sent[0], mine

    def table(self):
        T, G, DP, order = self.T, self.G, self.DP, self.order
        table = np.zeros((2, DP, T, PLACES), np.int32)
        for s in range(2):
            for d in range(DP):
                for z in range(T):
                    out, c, r, position = table[s, d, z], z % G, z // G, order.index(z)
                    for rel in range(4):
                        out[COL_OF_REL + rel] = d ^ rel if self.planar else rel
                    for i in range(T):
                        quarter = order[(position - i) % T]
                        out[ABS_OF_REL + i] = (c + i // 2) % G + G * (s ^ (i % 2))
                        out[OUT_OF_ABS + i] = 2 * ((i % G - c) % G) + i // G
                        out[ABS_OF_OUT + i] = (c + i // 2) % G + G * (i % 2)
                        out[CHIP_OF_RING + i] = (quarter % G - c) % G
                        out[SIDE_OF_RING + i] = (quarter // G) ^ r
                    for i in range(DP):
                        out[REL_OF_DP + i] = (d ^ i) if self.planar else i
                    out[SECTION] = s
        index = (self.s * DP + self.d) * T + self.z
        return lax.dynamic_index_in_dim(jnp.asarray(table.reshape(-1, PLACES)), index, 0, keepdims=False)


class Gather:
    def __init__(self, links, output_weight, gate_weight, up_weight, down_weight):
        s, d = links.s, links.d

        def half(which):
            def cut(x, dim):
                size = x.shape[dim] // 2
                return lax.dynamic_slice_in_dim(x, which * size, size, dim)

            return jnp.concatenate(
                [cut(output_weight, 0), cut(gate_weight, 1).T, cut(up_weight, 1).T, cut(down_weight, 0)]
            )

        mine = half(s)
        got = links.sibling(half(1 - s))
        self.links = links
        whole = [jnp.where(s == layer, mine, got) for layer in range(2)]
        self.weights = [[Weights([item])] for item in whole]
        if links.planar:
            size = output_weight.shape[1] // 4
            whole = [lax.dynamic_slice_in_dim(item, d * size, size, 1) for item in whole]
        self.current = whole

    def step(self, layer, *after):
        ring = self.links.ring(hold(self.current[layer], *after))
        self.current[layer] = ring
        plane = [self.links.along(ring, bit) for bit in (1, 2, 3)] if self.links.planar else []
        self.weights[layer].append(Weights([ring] + plane))
        return [ring], plane

    def two_steps(self, layer):
        once = self.links.ring(self.current[layer])
        self.current[layer] = self.links.ring(once)
        joined = jnp.concatenate([once, self.current[layer]])
        pieces = [joined] + [self.links.along(joined, bit) for bit in (1, 2, 3)]
        self.weights[layer] += [Weights(pieces), Weights(pieces, once.shape[0])]
        return [once, self.current[layer]]


class Projection:
    def __init__(self, links, query_weight, key_weight, value_weight):
        s = links.s
        self.depth, self.cols = query_weight.shape
        side = self.cols // 2

        def half(which):
            return jnp.concatenate(
                [lax.dynamic_slice_in_dim(w, which * side, side, 1) for w in (query_weight, key_weight, value_weight)],
                axis=1,
            )

        mine = half(s)
        got = links.sibling(half(1 - s))
        self.links = links
        self.own = [jnp.where(s == layer, mine, got) for layer in range(2)]

    def layer(self, layer, *after):
        self.early = []
        links, own, depth, side = self.links, self.own[layer], self.depth, self.cols // 2
        if links.planar:
            size = depth // 4
            other = links.across(hold(lax.dynamic_slice_in_dim(own, links.d * size, size, 0), *after))
            self.early.append(other)
            for bit in (1, 2):
                far = links.along(other, bit)
                other = jnp.where(
                    links.d & bit == 0, jnp.concatenate([other, far]), jnp.concatenate([far, other])
                )
        else:
            other = links.across(own)
        if side % 128:
            both = jnp.stack([own.reshape(depth, 3, side), other.reshape(depth, 3, side)], axis=2)
            return both.reshape(depth, 6 * side)
        return jnp.concatenate([own, other], axis=1)


class PlaneSum:
    def __init__(self, links, part):
        self.links, self.part, self.half = links, part, part.shape[1] // 2

    def begin(self, *after):
        part = hold(self.part, *after)
        self.x = self.links.along(part[1::2, : self.half], 1)
        self.y = self.links.along(part[2:4, self.half :], 2)
        return [self.x, self.y]

    def finish(self, *after):
        part = hold(self.part, *after)
        self.x_end = self.links.along(add_low(part[1, self.half :], self.y[1]), 1)
        self.y_end = self.links.along(add_low(part[2, : self.half], self.x[1]), 2)
        return [self.x_end, self.y_end]

    def total(self, first, rows, more, after):
        part = hold(self.part, *after)
        here = slice(first, first + rows)
        if first + rows <= self.half:
            terms = [part[0, here], self.x[0, here], self.y_end[here]]
        else:
            there = slice(first - self.half, first - self.half + rows)
            terms = [part[0, here], self.y[0, there], self.x_end[there]]
        return add_low(*terms, *more)


class StarSum:
    def __init__(self, links, term_of, order):
        self.links, self.term_of, self.order, self.got = links, term_of, order, []

    def step(self, *after):
        n = len(self.got)
        if n < len(self.order) - 1:
            self.got.append(self.links.back(self.term_of(n, [], after), self.order[n]))
            return self.got[-1:]
        self.total = self.term_of(n, self.got, after)
        return [self.total]


class LayerSums:
    def __init__(self, links, parts, out_part, rows, out_rows, order):
        first, second = PlaneSum(links, parts[0]), PlaneSum(links, parts[1])
        out = PlaneSum(links, out_part)
        self.first, self.second, self.out = first, second, out
        self.mlp = StarSum(
            links, lambda n, more, after: (first, second)[n // 2].total(n % 2 * rows, rows, more, after), order
        )
        self.star = StarSum(
            links, lambda n, more, after: out.total(order[n] * out_rows, out_rows, more, after), order
        )

    def proj_total(self, *after):
        size = self.proj.part.shape[1] // 2
        self.proj_sum = jnp.concatenate([self.proj.total(n * size, size, [], after) for n in range(2)])
        return [self.proj_sum]


def both_halves(links, per_layer):
    mine = jnp.where(links.s == 0, per_layer[0], per_layer[1])
    got = links.sibling(jnp.where(links.s == 0, per_layer[1], per_layer[0]))
    return jnp.where(links.s == 0, mine, got), jnp.where(links.s == 0, got, mine)


def sum_everywhere(links, x):
    if links.planar:
        x = sum([x] + [links.along(x, bit) for bit in (1, 2, 3)])
        return sum([x] + [links.back(x, k) for k in (1, 2, 3)])
    return lax.psum(x, ("dp", "tensor"))


def norm_low(x, gain):
    inverse = lax.rsqrt(jnp.mean(x * x, axis=-1, keepdims=True) + EPS)
    return (x * inverse * gain).astype(BF)


def per_device(
    tokens,
    segment_ids,
    cotangent,
    query_weight,
    key_weight,
    value_weight,
    output_weight,
    gate_weight,
    up_weight,
    down_weight,
    attn_gain,
    mlp_gain,
):
    links = Links()
    T, DP, s = links.T, links.DP, links.s
    seq = segment_ids.shape[1]
    length, width = tokens.shape[1:]
    cols = query_weight.shape[2]
    hidden = gate_weight.shape[2] // 2
    meta = links.table()

    half = HEAD // 2
    frequency = np.float32(ROPE_BASE) ** (-np.arange(half, dtype=np.float32) / np.float32(half))
    angles = np.arange(seq, dtype=np.float32)[:, None] * frequency[None, :].astype(np.float32)
    cosine, sine = np.cos(angles), np.sin(angles)
    tables = (
        jnp.asarray(np.concatenate([cosine] * 4, axis=1), F32),
        jnp.asarray(np.concatenate([-sine, sine, -sine, sine], axis=1), F32),
    )
    segments = lax.dynamic_index_in_dim(segment_ids, links.r, 0, keepdims=False)
    lane = jnp.arange(256, dtype=jnp.int32)[None, :]
    place = jnp.where(lane < 128, lane - HEAD, lane - 128)
    same = segments[:, None] == place
    in_seg = (place >= 0) & (place < 4)
    ext_q = jnp.where(in_seg & ~same, -BIG, 0.0).astype(BF)
    ext_k = jnp.where((in_seg & same) | ((place >= 4) & (place < 7)), 1.0, 0.0).astype(BF)

    own_gains = jnp.concatenate([attn_gain, mlp_gain])
    other_gains = links.sibling(own_gains)
    gains = [
        jnp.where(s == layer, own_gains, other_gains) for layer in range(2)
    ]
    def flat(item):
        return item.reshape(2 * length, width)

    def blocked(item):
        return item.reshape(2, length, width)

    planar = links.planar
    order = list(range(1, T)) + [0]
    batches = [order[: T // 2], order[T // 2 :]]
    out_rows = cols // 2
    rows = 3 * hidden

    x = flat(links.swap_end(tokens, links.swap_blocks(tokens)))
    a = norm_low(x.astype(F32), gains[0][0:1])
    gather = Gather(links, output_weight[0], gate_weight[0], up_weight[0], down_weight[0])
    weights = gather.weights
    projection = Projection(links, query_weight[0], key_weight[0], value_weight[0])
    w_proj = [projection.layer(0), None]
    if planar:
        early = projection.early
        w_proj[1] = projection.layer(1)
        first = gather.step(0, x, *early)
        rings = first[0] + gather.step(0)[0] + gather.step(0)[0]
        begun = gather.step(1, x, *early)
        later_rings = gather.two_steps(1)
    kept = []
    first_values = None
    for layer in range(2):
        gain_mlp = gains[layer][1:2]
        a_blocks = links.spread(blocked(a))
        deps = [[], [], [], []]
        if not planar:
            for _ in range(1, T):
                gather.step(layer)
            w_proj[1] = projection.layer(1)
        elif layer == 0:
            deps[1] = rings[:2] + w_proj[1:]
            deps[2] = rings[2:] + first[1]
        else:
            deps[0] = later_rings + begun[1]
        q, k, v = project(meta, a_blocks, w_proj[layer], tables, (ext_q, ext_k), first_values, deps[0])
        o_rel, q = attend(meta, q, k, v, T, deps[1])
        o_blocks = links.exchange(o_rel, length)
        p = output_forward(meta, o_blocks, weights[layer], width, deps[2])
        if layer:
            dy = flat(links.swap_end(cotangent, links.swap_blocks(cotangent)))
            deps[3] = [dy]
        y, h, b, *saved = mlp_forward(
            meta, x, p, links.sibling(p), gain_mlp, weights[layer], batches, hidden, out_rows, deps[3]
        )
        kept.append((x, a_blocks, q, k, v, o_rel, o_blocks, h, b, saved))
        if planar and layer == 0:
            y = hold(y, *begun[0])
        x = (h + (y.astype(F32) + links.sibling(y).astype(F32))).astype(BF)
        if layer == 0:
            a, first_values = norm_low(x.astype(F32), gains[1][0:1]), v
    last = x

    first_grad = None
    mlp_sums, out_sums, proj_sums, gain_sums, sums = [None] * 2, [None] * 2, [None] * 2, [None] * 2, [None] * 2
    for layer in (1, 0):
        gain_attn, gain_mlp = gains[layer][0:1], gains[layer][1:2]
        x, a_blocks, q, k, v, o_rel, o_blocks, h, b, saved = kept[layer]
        dy_low = dy.astype(BF)
        due = {name: [] for name in ("middle", "attend", "project")}
        before = sums[1] if planar and layer == 0 else None
        *parts, db = mlp_backward(meta, dy_low, b, saved, weights[layer], batches, out_rows, DP, [])
        if before:
            due["middle"] = passing
            due["attend"] = before.mlp.step(parts[0]) + before.star.step() + before.star.step() + before.star.step()
            due["attend"].append(activations)
        dh, mlp_gain_grad, do_rel, out_part = middle(
            meta, dy, db, links.sibling(db), h, gain_mlp, o_blocks, weights[layer], DP, due["middle"]
        )
        if planar:
            mine = sums[layer] = LayerSums(links, parts, out_part, rows, out_rows, order)
            begun = mine.first.begin() + mine.second.begin()
            if before:
                do_rel = hold(do_rel, *begun[:2])
        do_blocks = links.exchange(do_rel, length)
        if planar:
            due["attend"] = due["attend"] + begun[:2]
            due["project"] = begun[2:] + mine.first.finish(do_rel)
            if before:
                begun = begun + mine.out.begin()
                due["project"] = due["project"] + before.mlp.step(do_rel) + before.star.step(do_rel)
                due["project"] = due["project"] + before.proj_total(do_rel)
        if layer:
            sent = links.swap_blocks(blocked(last), parts[0])
            due["attend"] = due["attend"] + [sent]
        back = attend_back(meta, q, k, v, o_rel, do_blocks, tables, first_grad, due["attend"])
        if before:
            mine.second.finish(back[0])
            mine.out.finish(back[0])
            mine.mlp.step(back[0])
            mine.mlp.step(back[0])
        if layer == 1:
            first_grad = back[3]
        near, far, dw = project_back(meta, a_blocks, back[:3], w_proj[layer], DP, due["project"])
        da, sending, summed = links.combine(near, far)
        da = flat(da).astype(F32)
        part, attn_gain_grad = norm_back(x.astype(F32), gain_attn, da)
        gain_sums[layer] = jnp.concatenate([attn_gain_grad, mlp_gain_grad])
        dy = dh + part
        if planar:
            mine.proj = PlaneSum(links, dw)
            if before:
                for _ in range(3):
                    mine.star.step(sending)
                mine.proj.begin(sending)
                mine.mlp.step(summed)
                mine.proj.finish(summed)
            else:
                activations = links.swap_end(blocked(last), hold(sent, near))
                passing = mine.second.finish(sending) + mine.out.begin(sending) + mine.proj.begin(sending)
                passing = passing + mine.mlp.step(sending) + mine.mlp.step(sending)
                passing = passing + mine.out.finish(summed) + mine.proj.finish(summed)
        else:
            if layer:
                activations = links.swap_end(blocked(last), sent)
            running = None
            for part in parts:
                for n in range(T // 2):
                    term = part[:, n * rows : (n + 1) * rows]
                    running = term if running is None else add_low(term, links.ring(running))
            mlp_sums[layer] = lax.psum_scatter(running, "dp", scatter_dimension=0, tiled=True)[0]
            running = None
            for n in order:
                term = out_part[:, n * out_rows : (n + 1) * out_rows]
                running = term if running is None else add_low(term, links.ring(running))
            out_sums[layer] = lax.psum_scatter(running, "dp", scatter_dimension=0, tiled=True)[0]
            proj_sums[layer] = lax.psum_scatter(dw, "dp", scatter_dimension=0, tiled=True)[0]
    half_width = width // 2
    mine = lax.dynamic_slice_in_dim(blocked(dy), s * half_width, half_width, 2)
    give = lax.dynamic_index_in_dim(mine, 1 - links.r, 0, keepdims=False).astype(BF)
    got = links.across(give)
    input_grad = jnp.where((jnp.arange(2) == links.r)[:, None, None], mine, got.astype(F32)[None])
    if planar:
        sums[0].star.step(got)
        sums[0].mlp.step(got)
        sums[0].proj_total(got)
        mlp_sums = [item.mlp.total for item in sums]
        out_sums = [item.star.total for item in sums]
        proj_sums = [item.proj_sum for item in sums]
    halves = both_halves(links, [jnp.concatenate([mlp_sums[n], out_sums[n]]) for n in range(2)])
    joined = []
    for item in proj_sums:
        if out_rows % 128:
            item = item.reshape(-1, 3, 2, out_rows)
            sides = [item[:, :, e].reshape(-1, 3 * out_rows) for e in range(2)]
        else:
            sides = [item[:, : 3 * out_rows], item[:, 3 * out_rows :]]
        joined.append(add_low(sides[0], links.across(sides[1])))
    proj = [item.astype(F32) for item in both_halves(links, joined)]
    halves = [item.astype(F32) for item in halves]
    squares = sum(jnp.sum(item * item) for item in halves + proj)
    gain_mine = jnp.where(s == 0, gain_sums[0], gain_sums[1])
    line = jnp.where(jnp.arange(width)[None, :] == 0, squares, 0.0)
    summed = sum_everywhere(links, jnp.concatenate([gain_mine, line]))
    gain_total = summed[0:2]
    grad_norm = jnp.sqrt(summed[2, 0] + jnp.sum(gain_total * gain_total)).reshape(1)
    shard = width // (DP * T)
    gain_out = lax.dynamic_slice_in_dim(gain_total, (links.d * T + links.z) * shard, shard, 1)
    grads = [
        jnp.concatenate([item[m * hidden : (m + 1) * hidden] for item in halves]) for m in range(3)
    ]
    own_out = jnp.concatenate([item[rows:] for item in halves])
    own_proj = [
        jnp.concatenate([item[:, m * out_rows : (m + 1) * out_rows] for item in proj], axis=1) for m in range(3)
    ]
    return (
        activations,
        input_grad,
        own_proj[0][None],
        own_proj[1][None],
        own_proj[2][None],
        own_out[None],
        grads[0].T[None],
        grads[1].T[None],
        grads[2][None],
        gain_out[0:1],
        gain_out[1:2],
        grad_norm,
    )


def solution(mesh):
    return jax.shard_map(
        per_device,
        mesh=mesh,
        in_specs=(
            P("dp", "tensor", None),
            P("dp", None),
            P("dp", "tensor", None),
            P("section", None, "tensor"),
            P("section", None, "tensor"),
            P("section", None, "tensor"),
            P("section", "tensor", None),
            P("section", None, "tensor"),
            P("section", None, "tensor"),
            P("section", "tensor", None),
            P("section", None),
            P("section", None),
        ),
        out_specs=(
            P("dp", "tensor", None),
            P("dp", "tensor", "section"),
            P("section", "dp", "tensor"),
            P("section", "dp", "tensor"),
            P("section", "dp", "tensor"),
            P("section", "tensor", "dp"),
            P("section", "dp", "tensor"),
            P("section", "dp", "tensor"),
            P("section", "tensor", "dp"),
            P("section", ("dp", "tensor")),
            P("section", ("dp", "tensor")),
            P("section"),
        ),
        check_vma=False,
    )
```

```python
import functools
import math

import jax
import jax.numpy as jnp
import numpy as np
from jax import lax
from jax.experimental import pallas as pl
from jax.experimental.pallas import tpu as pltpu
from jax.sharding import PartitionSpec as P

HEAD = 64
EPS = 1e-05
ROPE_BASE = 10000.0
BIG = 1e30
LOG2E = math.log2(math.e)
BF = jnp.bfloat16
F32 = jnp.float32
ALL = ("section", "dp", "tensor")
VMEM_LIMIT = 60 * 1024 * 1024
STEP = 256
CHUNK = 32
STRIP = 256

COL_OF_REL, ABS_OF_REL, OUT_OF_ABS, ABS_OF_OUT, CHIP_OF_RING, SIDE_OF_RING, REL_OF_DP, SECTION = 0, 8, 16, 24, 32, 40, 48, 56
PLACES = 64


def nn(a, b):
    return jnp.dot(a, b, preferred_element_type=F32)


def nt(a, b):
    return lax.dot_general(a, b, (((1,), (1,)), ((), ())), preferred_element_type=F32)


def tn(a, b):
    return lax.dot_general(a, b, (((0,), (0,)), ((), ())), preferred_element_type=F32)


def vmem_spec():
    return pl.BlockSpec(memory_space=pltpu.VMEM)


def any_spec():
    return pl.BlockSpec(memory_space=pl.ANY)


def smem_spec():
    return pl.BlockSpec(memory_space=pltpu.SMEM)


def sds(shape, dtype):
    return jax.ShapeDtypeStruct(shape, dtype)


def cost(micros):
    return pl.CostEstimate(flops=int(micros * 1.15e9), bytes_accessed=0, transcendentals=0)


def params(**more):
    return pltpu.CompilerParams(vmem_limit_bytes=VMEM_LIMIT, **more)


def call(kernel, deps, operands, *, in_specs, **rest):
    count, extra = len(operands), len(deps)

    def body(*refs):
        kernel(*refs[:count], *refs[count + extra :])

    return pl.pallas_call(body, in_specs=in_specs + [any_spec()] * extra, **rest)(*operands, *deps)


class Weights:
    def __init__(self, arrays, offset=0):
        self.arrays, self.offset = arrays, offset

    def copies(self, meta, refs, parts, sems, first):
        found = []
        for n, ref in enumerate(refs):
            for row, rows, target in parts:
                dst = target
                if len(refs) > 1:
                    width = ref.shape[1]
                    dst = target.at[:, pl.ds(pl.multiple_of(meta[COL_OF_REL + n] * width, width), width)]
                src = ref.at[pl.ds(self.offset + row, rows), :]
                found.append(pltpu.make_async_copy(src, dst, sems.at[first + len(found)]))
        return found


class Blocks:
    def __init__(self, arrays, places, by_section=()):
        self.arrays, self.places, self.by_section = arrays, places, by_section

    def copies(self, meta, refs, target, sems, first):
        found = []
        for i, (n, place) in enumerate(self.places):
            place = meta[SECTION] ^ place if i in self.by_section else place
            found.append(pltpu.make_async_copy(refs[n].at[place], target(i), sems.at[first + i]))
        return found


def unique(weights):
    operands, places = [], []
    for item in weights:
        mine = []
        for array in item.arrays:
            for n, other in enumerate(operands):
                if other is array:
                    mine.append(n)
                    break
            else:
                mine.append(len(operands))
                operands.append(array)
        places.append(mine)
    return operands, places


def start_all(copies):
    for copy in copies:
        copy.start()
    return copies


def wait_all(copies):
    for copy in copies:
        copy.wait()


def swap_halves(tile):
    lane = lax.broadcasted_iota(jnp.int32, tile.shape, 1)
    return jnp.where(lane % HEAD < HEAD // 2, pltpu.roll(tile, 128 - HEAD // 2, 1), pltpu.roll(tile, HEAD // 2, 1))


def column_of(part, pair, cols):
    side = cols // 2
    if side % 128:
        return part * cols + pair * 128
    per_side = side // 128
    return (pair // per_side * 3 + part) * side + pair % per_side * 128


def qkv_kernel(a_blocks, later, meta, *refs):
    blocks, held = len(a_blocks.places), len(a_blocks.arrays)
    a_refs = refs[:held]
    w_ref, cos_ref, sin_ref, extq_ref, extk_ref = refs[held : held + 5]
    rest = refs[held + 5 :]
    if later:
        first_ref, rest = rest[0], rest[1:]
    outs, (a_scr, w_scr, q_scr, k_scr, v_scr, cos_scr, sin_scr, extq_scr, extk_scr), rest = rest[:3], rest[3:12], rest[12:]
    if later:
        first_scr, rest = rest[0], rest[1:]
    sems, out_sems = rest
    length = a_scr.shape[1]
    cols = w_ref.shape[1] // 3
    loads = [
        pltpu.make_async_copy(w_ref, w_scr, sems.at[0]),
        pltpu.make_async_copy(cos_ref, cos_scr, sems.at[2]),
        pltpu.make_async_copy(sin_ref, sin_scr, sems.at[3]),
        pltpu.make_async_copy(extq_ref, extq_scr, sems.at[4]),
        pltpu.make_async_copy(extk_ref, extk_scr, sems.at[5]),
    ]
    if later:
        loads.append(pltpu.make_async_copy(first_ref, first_scr, sems.at[6]))
    more = a_blocks.copies(meta, a_refs, lambda i: a_scr.at[i], sems, 7)
    start_all(loads)
    start_all(more)
    lane = lax.broadcasted_iota(jnp.int32, (length, 128), 1)
    low = lane < HEAD
    ones_even = ((lane >= HEAD + 4) & (lane < HEAD + 7)).astype(F32)
    ones_odd = ((lane >= 4) & (lane < 7)).astype(F32)
    stores = []
    for i in range(blocks):
        start = pl.multiple_of(meta[ABS_OF_REL + i] * length, length)
        rows = pl.ds(start, length)
        if i == 0:
            wait_all(loads)
        more[i].wait()
        a = a_scr[i]
        cosine, sine = cos_scr[rows, :], sin_scr[rows, :]
        whole = nn(a, w_scr[...])
        for part, out in ((0, q_scr), (1, k_scr), (2, v_scr)):
            for pair in range(cols // 128):
                column = column_of(part, pair, cols)
                tile = whole[:, column : column + 128]
                if part < 2:
                    tile = tile * cosine + swap_halves(tile) * sine
                    ext = extq_scr if part == 0 else extk_scr
                    if part == 0:
                        tile = tile * (LOG2E * HEAD**-0.5)
                    even_ext = ext[rows, :128].astype(F32)
                    odd_ext = ext[rows, 128:].astype(F32)
                else:
                    if later:
                        first = jnp.where(
                            low,
                            first_scr[2 * pair, rows, :].astype(F32),
                            first_scr[2 * pair + 1, rows, :].astype(F32),
                        )
                        tile = 0.5 * tile + 0.5 * first
                    even_ext, odd_ext = ones_even, ones_odd
                out[i, 2 * pair] = jnp.where(low, tile, even_ext).astype(BF)
                out[i, 2 * pair + 1] = jnp.where(low, odd_ext, tile).astype(BF)
        for n, (scr, out) in enumerate(zip((q_scr, k_scr, v_scr), outs)):
            stores += start_all([pltpu.make_async_copy(scr.at[i], out.at[:, rows, :], out_sems.at[3 * i + n])])
    wait_all(stores)


def project(meta, a_blocks, w, tables, exts, first, deps):
    blocks, (_, length, width) = len(a_blocks.places), a_blocks.arrays[0].shape
    cols = w.shape[1] // 3
    heads = cols // HEAD
    seq = blocks * length
    out = sds((heads, seq, 128), BF)
    later = first is not None
    operands = [meta, *a_blocks.arrays, w, *tables, *exts] + ([first] if later else [])
    block = pltpu.VMEM((blocks, heads, length, 128), BF)
    return call(
        functools.partial(qkv_kernel, a_blocks, later),
        deps,
        operands,
        out_shape=(out, out, out),
        in_specs=[smem_spec()] + [any_spec()] * (len(operands) - 1),
        out_specs=(any_spec(),) * 3,
        scratch_shapes=[
            pltpu.VMEM((blocks, length, width), BF),
            pltpu.VMEM(w.shape, BF),
            block,
            block,
            block,
            pltpu.VMEM((seq, 128), F32),
            pltpu.VMEM((seq, 128), F32),
            pltpu.VMEM((seq, 256), BF),
            pltpu.VMEM((seq, 256), BF),
        ]
        + ([pltpu.VMEM(out.shape, BF)] if later else [])
        + [pltpu.SemaphoreType.DMA((blocks + 7,)), pltpu.SemaphoreType.DMA((3 * blocks,))],
        compiler_params=params(),
        cost_estimate=cost(10),
        name="project",
    )


def project_back_kernel(a_blocks, dp_blocks, meta, *refs):
    blocks, held = len(a_blocks.places), len(a_blocks.arrays)
    a_refs = refs[:held]
    dq_ref, dk_ref, dv_ref, w_ref, near_ref, far_ref, dw_ref = refs[held : held + 7]
    a_scr, d_scr, w_scr, da_scr, dw_scr, sems, out_sems = refs[held + 7 :]
    _, length, width = da_scr.shape
    cols = dq_ref.shape[1]
    loads = [pltpu.make_async_copy(w_ref, w_scr, sems.at[0])]
    for part, ref in enumerate((dq_ref, dk_ref, dv_ref)):
        for pair in range(cols // 128):
            target = d_scr.at[:, pl.ds(column_of(part, pair, cols), 128)]
            source = ref.at[:, pl.ds(pair * 128, 128)]
            loads.append(pltpu.make_async_copy(source, target, sems.at[len(loads)]))

    def place(i):
        start = pl.multiple_of(meta[ABS_OF_REL + i] * length, length)
        return a_scr.at[pl.ds(start, length)]

    more = a_blocks.copies(meta, a_refs, place, sems, len(loads))
    start_all(loads)
    start_all(more)
    wait_all(loads)
    order = list(range(1, blocks, 2)) + list(range(2, blocks, 2)) + [0]
    stores = []
    for i in order:
        start = pl.multiple_of(meta[ABS_OF_REL + i] * length, length)
        da_scr[i] = nt(d_scr[pl.ds(start, length), :], w_scr[...]).astype(BF)
        out = far_ref if i % 2 else near_ref
        stores += start_all([pltpu.make_async_copy(da_scr.at[i], out.at[i // 2], out_sems.at[i])])
    wait_all(more)
    size = width // dp_blocks
    for j in range(dp_blocks):
        dw_scr[meta[REL_OF_DP + j]] = tn(a_scr[:, j * size : (j + 1) * size], d_scr[...]).astype(BF)
    stores += start_all([pltpu.make_async_copy(dw_scr, dw_ref, out_sems.at[blocks])])
    wait_all(stores)


def project_back(meta, a_blocks, grads, w, dp_blocks, deps):
    blocks, (_, length, width) = len(a_blocks.places), a_blocks.arrays[0].shape
    cols = w.shape[1]
    seq = blocks * length
    half = sds((blocks // 2, length, width), BF)
    dw = (dp_blocks, width // dp_blocks, cols)
    return call(
        functools.partial(project_back_kernel, a_blocks, dp_blocks),
        deps,
        [meta, *a_blocks.arrays, *grads, w],
        out_shape=(half, half, sds(dw, BF)),
        in_specs=[smem_spec()] + [any_spec()] * (len(a_blocks.arrays) + 4),
        out_specs=(any_spec(),) * 3,
        scratch_shapes=[
            pltpu.VMEM((seq, width), BF),
            pltpu.VMEM((seq, cols), BF),
            pltpu.VMEM(w.shape, BF),
            pltpu.VMEM((blocks, length, width), BF),
            pltpu.VMEM(dw, BF),
            pltpu.SemaphoreType.DMA((blocks + 1 + cols // 128,)),
            pltpu.SemaphoreType.DMA((blocks + 1,)),
        ],
        compiler_params=params(),
        cost_estimate=cost(12),
        name="project_back",
    )


def three_parts(value):
    high = value.astype(BF).astype(F32)
    middle = (value - high).astype(BF).astype(F32)
    return high, middle, value - high - middle


def with_parts(base, value, odd):
    lane = lax.broadcasted_iota(jnp.int32, base.shape, 1)
    offset = 4 if odd else HEAD + 4
    high, middle, rest = three_parts(value)
    out = jnp.where(lane == offset, high, base)
    out = jnp.where(lane == offset + 1, middle, out)
    return jnp.where(lane == offset + 2, rest, out)


def attend_kernel(block, meta, q_ref, k_ref, v_ref, o_ref, ql_ref, vt_scr, tot_scr, top_scr, s_scr, p_scr):
    seq = q_ref.shape[1]
    length = o_ref.shape[1]
    key_row = lax.broadcasted_iota(jnp.int32, (STEP, block), 0)
    query_col = lax.broadcasted_iota(jnp.int32, (STEP, block), 1)
    for e in range(2):
        vt_scr[e] = v_ref[e].T

    def score(i, e):
        q = q_ref[e, i * block : (i + 1) * block, :]
        best = None
        for lo in range(0, (i + 1) * block, STEP):
            tile = nt(k_ref[e, lo : lo + STEP, :], q)
            if lo >= i * block:
                tile = jnp.where(key_row + (lo - i * block) <= query_col, tile, -BIG)
            s_scr[e, i % 2, lo : lo + STEP, :] = tile
            best = tile if best is None else jnp.maximum(best, tile)
        top_scr[e, :, i * block : (i + 1) * block] = best.max(axis=0, keepdims=True)

    def weigh(i, e):
        cols = slice(i * block, (i + 1) * block)
        top = top_scr[e, :, cols]
        for lo in range(0, (i + 1) * block, STEP):
            p_scr[e, lo : lo + STEP, :] = jnp.exp2(s_scr[e, i % 2, lo : lo + STEP, :] - top).astype(BF)
        tot_scr[e, :, cols] = nn(vt_scr[e, :, : (i + 1) * block], p_scr[e, : (i + 1) * block, :])

    count = seq // block
    for i in range(count + 1):
        for e in range(2):
            if i < count:
                score(i, e)
            if i > 0:
                weigh(i - 1, e)
    low = lax.broadcasted_iota(jnp.int32, (length, 128), 1) < HEAD
    lane = lax.broadcasted_iota(jnp.int32, (length, 128), 1)
    row = lax.broadcasted_iota(jnp.int32, (128, length), 0)
    for i in range(seq // length):
        rows = slice(i * length, (i + 1) * length)
        results = []
        for e in range(2):
            place = 4 if e else HEAD + 4
            total = tot_scr[e, :, rows]
            weight = total[place : place + 1, :]
            total = total * (1.0 / weight)
            for n, value in enumerate(three_parts(-(top_scr[e, :, rows] + jnp.log2(weight)))):
                total = jnp.where(row == place + n, value, total)
            turned = total.T
            results.append(turned)
            parts = (lane >= place) & (lane < place + 3)
            ql_ref[e, rows, :] = jnp.where(parts, turned, q_ref[e, rows, :].astype(F32)).astype(BF)
        o_ref[meta[OUT_OF_ABS + i]] = jnp.where(low, results[0], results[1]).astype(BF)


def attend(meta, q, k, v, blocks, deps):
    heads, seq, _ = q.shape
    pairs = heads // 2
    length = seq // blocks
    head_spec = pl.BlockSpec((2, seq, 128), lambda p: (p, 0, 0))
    return call(
        functools.partial(attend_kernel, min(256, length)),
        deps,
        [meta, q, k, v],
        grid=(pairs,),
        out_shape=(sds((blocks, length, pairs * 128), BF), sds(q.shape, BF)),
        in_specs=[smem_spec(), head_spec, head_spec, head_spec],
        out_specs=(pl.BlockSpec((blocks, length, 128), lambda p: (0, 0, p)), head_spec),
        scratch_shapes=[
            pltpu.VMEM((2, 128, seq), BF),
            pltpu.VMEM((2, 128, seq), F32),
            pltpu.VMEM((2, 1, seq), F32),
            pltpu.VMEM((2, 2, seq, min(256, length)), F32),
            pltpu.VMEM((2, seq, min(256, length)), BF),
        ],
        compiler_params=params(),
        cost_estimate=cost(14.5),
        name="attend",
    )


def attend_back_kernel(block, blocks, later, meta, q_ref, k_ref, v_ref, o_ref, *refs):
    do_refs = refs[:blocks]
    cos_ref, sin_ref = refs[blocks : blocks + 2]
    rest = refs[blocks + 2 :]
    if not later:
        first_ref, rest = rest[0], rest[1:]
    dq_ref, dk_ref, dv_ref = rest[:3]
    rest = rest[3:]
    if later:
        first_out, rest = rest[0], rest[1:]
    do_scr, dq_scr, dk_scr, dv_scr, kt_scr, p_scr, ds_scr = rest
    seq = q_ref.shape[1]
    length = o_ref.shape[1]
    lane = lax.broadcasted_iota(jnp.int32, (length, 128), 1)
    low = lane < HEAD
    for i in range(blocks):
        start = pl.multiple_of(meta[ABS_OF_OUT + i] * length, length)
        rows = pl.ds(start, length)
        do = do_refs[i][...].astype(F32)
        product = do * o_ref[i].astype(F32)
        for e in range(2):
            mine = low if e == 0 else jnp.logical_not(low)
            delta = jnp.sum(jnp.where(mine, product, 0.0), axis=1, keepdims=True)
            do_scr[e, rows, :] = with_parts(jnp.where(mine, do, 0.0), -delta, e == 1).astype(BF)
    key_row = lax.broadcasted_iota(jnp.int32, (STEP, block), 0)
    query_col = lax.broadcasted_iota(jnp.int32, (STEP, block), 1)
    for e in range(2):
        kt_scr[e] = k_ref[e].T
    count = seq // block

    def weigh(i, e):
        cols = slice(i * block, (i + 1) * block)
        q = q_ref[e, cols, :]
        do = do_scr[e, cols, :]
        for lo in range(0, (i + 1) * block, STEP):
            rows = slice(lo, lo + STEP)
            scores = nt(k_ref[e, rows, :], q)
            if lo >= i * block:
                scores = jnp.where(key_row + (lo - i * block) <= query_col, scores, -BIG)
            prob = jnp.exp2(scores)
            p_scr[e, rows, cols] = prob.astype(BF)
            ds_scr[e, rows, cols] = (prob * nt(v_ref[e, rows, :], do)).astype(BF)

    def query_grad(i, e):
        cols = slice(i * block, (i + 1) * block)
        dq_scr[e, :, cols] = nn(kt_scr[e, :, : (i + 1) * block], ds_scr[e, : (i + 1) * block, cols])

    def key_grads(i, e):
        rows, cols = slice(i * block, (i + 1) * block), slice(i * block, seq)
        dv_scr[e, rows, :] = nn(p_scr[e, rows, cols], do_scr[e, cols, :])
        dk_scr[e, rows, :] = nn(ds_scr[e, rows, cols], q_ref[e, cols, :])

    for i in range(count + 1):
        for e in range(2):
            if i < count:
                weigh(i, e)
            if i > 0:
                query_grad(i - 1, e)
    for i in range(count):
        for e in range(2):
            key_grads(i, e)
    for i in range(blocks):
        rows = slice(i * length, (i + 1) * length)
        cosine, sine = cos_ref[rows, :], sin_ref[rows, :]
        dq = jnp.where(low, dq_scr[0, :, rows].T, dq_scr[1, :, rows].T) * (HEAD**-0.5)
        dk = jnp.where(low, dk_scr[0, rows, :], dk_scr[1, rows, :]) * (1.0 / LOG2E)
        dv = jnp.where(low, dv_scr[0, rows, :], dv_scr[1, rows, :])
        dq_ref[rows, :] = (dq * cosine - swap_halves(dq) * sine).astype(BF)
        dk_ref[rows, :] = (dk * cosine - swap_halves(dk) * sine).astype(BF)
        if later:
            dv_ref[rows, :] = (0.5 * dv).astype(BF)
            first_out[rows, :] = 0.5 * dv
        else:
            dv_ref[rows, :] = (dv + first_ref[rows, :]).astype(BF)


def attend_back(meta, q, k, v, o, do_blocks, tables, first, deps):
    heads, seq, _ = q.shape
    pairs = heads // 2
    blocks, length, cols = o.shape
    later = first is None
    head_spec = pl.BlockSpec((2, seq, 128), lambda p: (p, 0, 0))
    col_spec = pl.BlockSpec((seq, 128), lambda p: (0, p))
    table_spec = pl.BlockSpec((seq, 128), lambda p: (0, 0))
    out = sds((seq, cols), BF)
    return call(
        functools.partial(attend_back_kernel, min(256, length), blocks, later),
        deps,
        [meta, q, k, v, o, *[do_blocks.arrays[n] for n, _ in do_blocks.places], *tables, *([] if later else [first])],
        grid=(pairs,),
        out_shape=(out, out, out) + ((sds((seq, cols), F32),) if later else ()),
        in_specs=[smem_spec(), head_spec, head_spec, head_spec]
        + [pl.BlockSpec((blocks, length, 128), lambda p: (0, 0, p))]
        + [pl.BlockSpec((None, length, 128), functools.partial(lambda n, p: (n, 0, p), n)) for _, n in do_blocks.places]
        + [table_spec] * 2
        + ([] if later else [col_spec]),
        out_specs=(col_spec,) * (4 if later else 3),
        scratch_shapes=[
            pltpu.VMEM((2, seq, 128), BF),
            pltpu.VMEM((2, 128, seq), F32),
            pltpu.VMEM((2, seq, 128), F32),
            pltpu.VMEM((2, seq, 128), F32),
            pltpu.VMEM((2, 128, seq), BF),
            pltpu.VMEM((2, seq, seq), BF),
            pltpu.VMEM((2, seq, seq), BF),
        ],
        compiler_params=params(),
        cost_estimate=cost(29.5),
        name="attend_back",
    )


def place_output(weights, places, meta, refs, target, sems, first):
    found = []
    rows = target.shape[1] // 2
    for k, item in enumerate(weights):
        side = pl.multiple_of(meta[SIDE_OF_RING + k] * rows, rows)
        part = (0, rows, target.at[meta[CHIP_OF_RING + k], pl.ds(side, rows)])
        found += item.copies(meta, [refs[n] for n in places[k]], [part], sems, first + 4 * k)
    return found


def output_kernel(o_blocks, weights, places, meta, *refs):
    o_refs, refs = refs[: len(o_blocks.arrays)], refs[len(o_blocks.arrays) :]
    number = len({n for place in places for n in place})
    w_refs, (p_ref, o_scr, w_scr, sems) = refs[:number], refs[number:]
    count = len(o_blocks.places)
    length = o_scr.shape[1] // 2
    loads = o_blocks.copies(meta, o_refs, lambda i: o_scr.at[i // 2, pl.ds(i % 2 * length, length)], sems, 0)
    loads += place_output(weights, places, meta, w_refs, w_scr, sems, count)
    wait_all(start_all(loads))
    for f in range(2):
        rows = slice(f * length, (f + 1) * length)
        total = nn(o_scr[0, rows, :], w_scr[0])
        for n in range(1, count // 2):
            total += nn(o_scr[n, rows, :], w_scr[n])
        p_ref[rows, :] = total.astype(BF)


def output_forward(meta, o_blocks, weights, width, deps):
    count = len(o_blocks.places)
    _, length, cols = o_blocks.arrays[0].shape
    operands, places = unique(weights)
    return call(
        functools.partial(output_kernel, o_blocks, weights, places),
        deps,
        [meta, *o_blocks.arrays, *operands],
        out_shape=sds((2 * length, width), BF),
        in_specs=[smem_spec()] + [any_spec()] * (len(o_blocks.arrays) + len(operands)),
        out_specs=vmem_spec(),
        scratch_shapes=[
            pltpu.VMEM((count // 2, 2 * length, cols), BF),
            pltpu.VMEM((count // 2, cols, width), BF),
            pltpu.SemaphoreType.DMA((5 * count,)),
        ],
        compiler_params=params(),
        cost_estimate=cost(5),
        name="output",
    )


def place_hidden(batch, weights, places, meta, refs, target, sems, first, row):
    hidden = target.shape[1] // len(batch)
    found = []
    for n, k in enumerate(batch):
        parts = [(row + m * hidden, hidden, target.at[m, pl.ds(n * hidden, hidden)]) for m in range(3)]
        found += weights[k].copies(meta, [refs[i] for i in places[k]], parts, sems, first + 12 * n)
    return found


def mlp_kernel(batches, weights, places, row, meta, x_ref, p_ref, other_ref, gain_ref, *refs):
    number = len({n for place in places for n in place})
    w_refs, refs = refs[:number], refs[number:]
    count = len(batches)
    y_ref, h_ref, b_ref = refs[:3]
    g_refs, u_refs, refs = refs[3 : 3 + count], refs[3 + count : 3 + 2 * count], refs[3 + 2 * count :]
    w_scr, sems = refs
    first = [12 * sum(len(other) for other in batches[:n]) for n in range(count)]

    def loads(n):
        return place_hidden(batches[n], weights, places, meta, w_refs, w_scr.at[n], sems, first[n], row)

    @pl.when(pl.program_id(0) == 0)
    def _():
        for n in range(count):
            start_all(loads(n))

    gain = gain_ref[...]
    for start in range(0, x_ref.shape[0], CHUNK):
        rows = slice(start, start + CHUNK)
        h = x_ref[rows, :].astype(F32) + (p_ref[rows, :].astype(F32) + other_ref[rows, :].astype(F32))
        h_ref[rows, :] = h
        inverse = lax.rsqrt(jnp.mean(h * h, axis=1, keepdims=True) + EPS)
        b_ref[rows, :] = (h * inverse * gain).astype(BF)

    @pl.when(pl.program_id(0) == 0)
    def _():
        for n in range(count):
            wait_all(loads(n))

    for start in range(0, x_ref.shape[0], STRIP):
        rows = slice(start, start + STRIP)
        b = b_ref[rows, :]
        total = None
        for n in range(count):
            g = nt(b, w_scr[n, 0])
            u = nt(b, w_scr[n, 1])
            g_refs[n][rows, :] = g.astype(BF)
            u_refs[n][rows, :] = u.astype(BF)
            m = (g * jax.nn.sigmoid(g) * u).astype(BF)
            term = nn(m, w_scr[n, 2])
            total = term if total is None else total + term
        y_ref[rows, :] = total.astype(BF)


def mlp_forward(meta, x, p, other, gain, weights, batches, hidden, row, deps):
    rows, width = x.shape
    operands, places = unique(weights)
    size = [len(batch) * hidden for batch in batches]
    quarters = sum(len(batch) for batch in batches)
    low = sds((rows, width), BF)
    saved = tuple(sds((rows, n), BF) for n in size)
    block = min(256, rows)

    def by_rows(n):
        return pl.BlockSpec((block, n), lambda i: (i, 0))

    return call(
        functools.partial(mlp_kernel, batches, weights, places, row),
        deps,
        [meta, x, p, other, gain, *operands],
        grid=(rows // block,),
        out_shape=(low, sds((rows, width), F32), low) + saved + saved,
        in_specs=[smem_spec()]
        + [by_rows(width)] * 3
        + [pl.BlockSpec((1, width), lambda i: (0, 0))]
        + [any_spec()] * len(operands),
        out_specs=(by_rows(width),) * 3 + tuple(by_rows(n) for n in size) * 2,
        scratch_shapes=[
            pltpu.VMEM((len(batches), 3, size[0], width), BF),
            pltpu.SemaphoreType.DMA((12 * quarters,)),
        ],
        compiler_params=params(),
        cost_estimate=cost(19),
        name="mlp",
    )


def mlp_back_kernel(batches, weights, places, row, meta, dy_ref, b_ref, *refs):
    count = len(batches)
    g_refs, u_refs, refs = refs[:count], refs[count : 2 * count], refs[2 * count :]
    number = len({n for place in places for n in place})
    w_refs, refs = refs[:number], refs[number:]
    out_refs, refs = refs[:count], refs[count:]
    db_ref, dy_scr, b_scr, g_scr, u_scr, w_scr, low_scr, grad_scr, sems, out_sems = refs
    dy_load = pltpu.make_async_copy(dy_ref, dy_scr, sems.at[0])
    b_load = pltpu.make_async_copy(b_ref, b_scr, sems.at[1])
    dy_load.start()
    loads, used = [], 2
    for n, batch in enumerate(batches):
        group = place_hidden(batch, weights, places, meta, w_refs, w_scr.at[n], sems, used, row)
        used += 12 * len(batch)
        for source, target in ((g_refs[n], g_scr.at[n]), (u_refs[n], u_scr.at[n])):
            group.append(pltpu.make_async_copy(source, target, sems.at[used]))
            used += 1
        loads.append(start_all(group))
    b_load.start()
    total_rows, width = dy_scr.shape
    hidden = w_scr.shape[2] // len(batches[0])
    columns, _, size = out_refs[0].shape
    stores = []
    dy_load.wait()
    for n, batch in enumerate(batches):
        wait_all(loads[n])
        for start in range(0, total_rows, STRIP):
            rows = slice(start, start + STRIP)
            dm = nt(dy_scr[rows, :], w_scr[n, 2])
            g = g_scr[n, rows, :].astype(F32)
            u = u_scr[n, rows, :].astype(F32)
            gate = jax.nn.sigmoid(g)
            active = g * gate
            low_scr[n, 0, rows, :] = (dm * u * (gate + active * (1.0 - gate))).astype(BF)
            low_scr[n, 1, rows, :] = (dm * active).astype(BF)
            low_scr[n, 2, rows, :] = (active * u).astype(BF)
    b_load.wait()
    for n, batch in enumerate(batches):
        for m in range(3):
            grad_scr[n, m] = tn(low_scr[n, m], dy_scr[...] if m == 2 else b_scr[...]).astype(BF)
            for q in range(len(batch)):
                for j in range(columns):
                    copy = pltpu.make_async_copy(
                        grad_scr.at[n, m, pl.ds(q * hidden, hidden), pl.ds(j * size, size)],
                        out_refs[n].at[meta[REL_OF_DP + j], pl.ds((q * 3 + m) * hidden, hidden), :],
                        out_sems.at[((n * 3 + m) * len(batch) + q) * columns + j],
                    )
                    copy.start()
                    stores.append(copy)
    for start in range(0, total_rows, 256):
        rows = slice(start, start + 256)
        db = None
        for n in range(count):
            term = nn(low_scr[n, 0, rows, :], w_scr[n, 0]) + nn(low_scr[n, 1, rows, :], w_scr[n, 1])
            db = term if db is None else db + term
        db_ref[rows, :] = db.astype(BF)
    wait_all(stores)


def mlp_backward(meta, dy, b, saved, weights, batches, row, dp_blocks, deps):
    rows, width = b.shape
    count = len(batches)
    size = saved[0].shape[1]
    operands, places = unique(weights)
    copies = sum(12 * len(batch) + 2 for batch in batches)
    return call(
        functools.partial(mlp_back_kernel, batches, weights, places, row),
        deps,
        [meta, dy, b, *saved, *operands],
        out_shape=(sds((dp_blocks, 3 * size, width // dp_blocks), BF),) * count + (sds((rows, width), BF),),
        in_specs=[smem_spec()] + [any_spec()] * (2 + 2 * count + len(operands)),
        out_specs=(any_spec(),) * count + (vmem_spec(),),
        scratch_shapes=[
            pltpu.VMEM((rows, width), BF),
            pltpu.VMEM((rows, width), BF),
            pltpu.VMEM((count, rows, size), BF),
            pltpu.VMEM((count, rows, size), BF),
            pltpu.VMEM((count, 3, size, width), BF),
            pltpu.VMEM((count, 3, rows, size), BF),
            pltpu.VMEM((count, 3, size, width), BF),
            pltpu.SemaphoreType.DMA((2 + copies,)),
            pltpu.SemaphoreType.DMA((3 * dp_blocks * sum(len(batch) for batch in batches),)),
        ],
        compiler_params=params(),
        cost_estimate=cost(28),
        name="mlp_back",
    )


def norm_back(values, gain, grads):
    inverse = lax.rsqrt(jnp.mean(values * values, axis=1, keepdims=True) + EPS)
    normed = values * inverse
    scaled = grads * gain
    gain_grad = jnp.sum(grads * normed, axis=0, keepdims=True)
    return inverse * (scaled - normed * jnp.mean(scaled * normed, axis=1, keepdims=True)), gain_grad


def middle_kernel(o_blocks, weights, places, meta, dy_ref, db_ref, other_ref, h_ref, gain_ref, *refs):
    o_refs, refs = refs[: len(o_blocks.arrays)], refs[len(o_blocks.arrays) :]
    number = len({n for place in places for n in place})
    w_refs, refs = refs[:number], refs[number:]
    dh_ref, gain_out, do_ref, grad_ref, w_scr, o_scr, low_scr, grad_scr, sems, out_sems = refs
    count = len(o_blocks.places)
    length = o_scr.shape[1] // 2
    step, steps = pl.program_id(0), pl.num_programs(0)

    def loads():
        found = o_blocks.copies(meta, o_refs, lambda i: o_scr.at[i // 2, pl.ds(i % 2 * length, length)], sems, 0)
        return found + place_output(weights, places, meta, w_refs, w_scr, sems, count)

    @pl.when(step == 0)
    def _():
        start_all(loads())
        gain_out[...] = jnp.zeros_like(gain_out)

    gain = gain_ref[...]
    block = dy_ref.shape[0]
    first = pl.multiple_of(step * block, block)
    total = None
    for start in range(0, block, CHUNK):
        rows = slice(start, start + CHUNK)
        db = db_ref[rows, :].astype(F32) + other_ref[rows, :].astype(F32)
        part, gain_grad = norm_back(h_ref[rows, :], gain, db)
        dh = dy_ref[rows, :].astype(F32) + part
        dh_ref[rows, :] = dh
        low_scr[pl.ds(first + start, CHUNK), :] = dh.astype(BF)
        total = gain_grad if total is None else total + gain_grad
    gain_out[...] += total

    @pl.when(step == 0)
    def _():
        wait_all(loads())

    low = low_scr[pl.ds(first, block), :]
    for n in range(count // 2):
        do_ref[n] = nt(low, w_scr[n]).astype(BF)

    @pl.when(step == steps - 1)
    def _():
        for n in range(count // 2):
            grad_scr[n] = tn(o_scr[n], low_scr[...]).astype(BF)
        stores = []
        columns = grad_ref.shape[0]
        size = grad_ref.shape[2]
        rows = o_scr.shape[2] // 2
        for k in range(count):
            side = pl.multiple_of(meta[SIDE_OF_RING + k] * rows, rows)
            for j in range(columns):
                stores.append(
                    pltpu.make_async_copy(
                        grad_scr.at[meta[CHIP_OF_RING + k], pl.ds(side, rows), pl.ds(j * size, size)],
                        grad_ref.at[meta[REL_OF_DP + j], pl.ds(k * rows, rows), :],
                        out_sems.at[k * columns + j],
                    )
                )
        wait_all(start_all(stores))


def middle(meta, dy, db, other, h, gain, o_blocks, weights, dp_blocks, deps):
    count = len(o_blocks.places)
    _, length, cols = o_blocks.arrays[0].shape
    width = h.shape[1]
    operands, places = unique(weights)
    block = 256
    by_rows = pl.BlockSpec((block, width), lambda i: (i, 0))
    fixed = pl.BlockSpec((1, width), lambda i: (0, 0))
    return call(
        functools.partial(middle_kernel, o_blocks, weights, places),
        deps,
        [meta, dy, db, other, h, gain, *o_blocks.arrays, *operands],
        grid=(2 * length // block,),
        out_shape=(
            sds((2 * length, width), F32),
            sds((1, width), F32),
            sds((count // 2, 2 * length, cols), BF),
            sds((dp_blocks, count * cols // 2, width // dp_blocks), BF),
        ),
        in_specs=[smem_spec()]
        + [by_rows] * 4
        + [fixed]
        + [any_spec()] * (len(o_blocks.arrays) + len(operands)),
        out_specs=(by_rows, fixed, pl.BlockSpec((count // 2, block, cols), lambda i: (0, i, 0)), any_spec()),
        scratch_shapes=[
            pltpu.VMEM((count // 2, cols, width), BF),
            pltpu.VMEM((count // 2, 2 * length, cols), BF),
            pltpu.VMEM((2 * length, width), BF),
            pltpu.VMEM((count // 2, cols, width), BF),
            pltpu.SemaphoreType.DMA((5 * count,)),
            pltpu.SemaphoreType.DMA((count * dp_blocks,)),
        ],
        compiler_params=params(),
        cost_estimate=cost(13),
        name="middle",
    )


def add_low(*terms):
    total = terms[0].astype(F32)
    for term in terms[1:]:
        total = total + term.astype(F32)
    return total.astype(BF)


def hold(x, *after):
    return lax.optimization_barrier((x, *after))[0] if after else x


class Links:
    def __init__(self):
        self.T = lax.axis_size("tensor")
        self.DP = lax.axis_size("dp")
        self.G = self.T // 2
        self.s = lax.axis_index("section")
        self.d = lax.axis_index("dp")
        self.z = lax.axis_index("tensor")
        self.r = self.z // self.G
        self.home = self.s == self.r
        self.planar = self.DP == 4 and self.T == 4
        self.order = [0] + list(range(1, self.T, 2)) + list(range(self.T - 2, 0, -2))

    def sibling(self, x):
        return lax.ppermute(x, "section", [(0, 1), (1, 0)])

    def ring(self, x):
        order = self.order
        return lax.ppermute(x, "tensor", [(order[i], order[(i + 1) % self.T]) for i in range(self.T)])

    def back(self, x, k):
        order = self.order
        return lax.ppermute(x, "tensor", [(order[i], order[(i - k) % self.T]) for i in range(self.T)])

    def along(self, x, bit):
        return lax.ppermute(x, "dp", [(i, i ^ bit) for i in range(self.DP)])

    def across(self, x):
        return lax.ppermute(x, "tensor", [(z, (z + self.G) % self.T) for z in range(self.T)])

    def shift(self, x, k):
        pairs = [(z, z // self.G * self.G + (z + k) % self.G) for z in range(self.T)]
        return lax.ppermute(x, "tensor", pairs)

    def swap_blocks(self, x, *after):
        pairs = []
        for s in range(2):
            z0 = s * self.G
            for z in range(z0, z0 + self.G):
                pairs.append((s * self.T + z, s * self.T + (z + self.G) % self.T))
        give = hold(lax.dynamic_index_in_dim(x, 1 - self.r, 0, keepdims=False), *after)
        return lax.ppermute(give, ("section", "tensor"), pairs)

    def swap_end(self, x, got):
        got = jnp.where(self.home, self.sibling(got), got)
        mine = (jnp.arange(2) == self.r)[:, None, None]
        return jnp.where(mine, x, got[None])

    def spread(self, x, *also):
        give = lax.dynamic_index_in_dim(x, self.s, 0)
        arrays, places = [x], [(0, 0), (0, 1)]
        for k in range(1, self.G):
            got = hold(self.shift(give, -k), *also)
            arrays += [got, self.sibling(got)]
            places += [(len(arrays) - 2, 0), (len(arrays) - 1, 0)]
        return Blocks(arrays, places, (0, 1))

    def exchange(self, x, length):
        cols = x.shape[-1]
        arrays, places = [x.reshape(self.T, length, cols)], [(0, 0), (0, 1)] + [None] * (self.T - 2)
        for k in range(1, self.G):
            got = self.shift(x.reshape(self.G, 2 * length, cols)[k], k)
            chip = -k % self.G
            places[2 * chip], places[2 * chip + 1] = (len(arrays), 0), (len(arrays), 1)
            arrays.append(got.reshape(2, length, cols))
        return Blocks(arrays, places)

    def combine(self, near, far):
        got = self.sibling(far)
        terms, sent = [near[0], got[0]], []
        for k in range(1, self.G):
            sent.append(add_low(near[k], got[k]))
            terms.append(self.shift(sent[-1], k))
        mine = add_low(*terms)
        both = (jnp.arange(2) == self.s)[:, None, None]
        return jnp.where(both, mine[None], self.sibling(mine)[None]), sent[0], mine

    def table(self):
        T, G, DP, order = self.T, self.G, self.DP, self.order
        table = np.zeros((2, DP, T, PLACES), np.int32)
        for s in range(2):
            for d in range(DP):
                for z in range(T):
                    out, c, r, position = table[s, d, z], z % G, z // G, order.index(z)
                    for rel in range(4):
                        out[COL_OF_REL + rel] = d ^ rel if self.planar else rel
                    for i in range(T):
                        quarter = order[(position - i) % T]
                        out[ABS_OF_REL + i] = (c + i // 2) % G + G * (s ^ (i % 2))
                        out[OUT_OF_ABS + i] = 2 * ((i % G - c) % G) + i // G
                        out[ABS_OF_OUT + i] = (c + i // 2) % G + G * (i % 2)
                        out[CHIP_OF_RING + i] = (quarter % G - c) % G
                        out[SIDE_OF_RING + i] = (quarter // G) ^ r
                    for i in range(DP):
                        out[REL_OF_DP + i] = (d ^ i) if self.planar else i
                    out[SECTION] = s
        index = (self.s * DP + self.d) * T + self.z
        return lax.dynamic_index_in_dim(jnp.asarray(table.reshape(-1, PLACES)), index, 0, keepdims=False)


class Gather:
    def __init__(self, links, output_weight, gate_weight, up_weight, down_weight):
        s, d = links.s, links.d

        def half(which):
            def cut(x, dim):
                size = x.shape[dim] // 2
                return lax.dynamic_slice_in_dim(x, which * size, size, dim)

            return jnp.concatenate(
                [cut(output_weight, 0), cut(gate_weight, 1).T, cut(up_weight, 1).T, cut(down_weight, 0)]
            )

        mine = half(s)
        got = links.sibling(half(1 - s))
        self.links = links
        whole = [jnp.where(s == layer, mine, got) for layer in range(2)]
        self.weights = [[Weights([item])] for item in whole]
        if links.planar:
            size = output_weight.shape[1] // 4
            whole = [lax.dynamic_slice_in_dim(item, d * size, size, 1) for item in whole]
        self.current = whole

    def step(self, layer, *after):
        ring = self.links.ring(hold(self.current[layer], *after))
        self.current[layer] = ring
        plane = [self.links.along(ring, bit) for bit in (1, 2, 3)] if self.links.planar else []
        self.weights[layer].append(Weights([ring] + plane))
        return [ring], plane

    def two_steps(self, layer):
        once = self.links.ring(self.current[layer])
        self.current[layer] = self.links.ring(once)
        joined = jnp.concatenate([once, self.current[layer]])
        pieces = [joined] + [self.links.along(joined, bit) for bit in (1, 2, 3)]
        self.weights[layer] += [Weights(pieces), Weights(pieces, once.shape[0])]
        return [once, self.current[layer]]


class Projection:
    def __init__(self, links, query_weight, key_weight, value_weight):
        s = links.s
        self.depth, self.cols = query_weight.shape
        side = self.cols // 2

        def half(which):
            return jnp.concatenate(
                [lax.dynamic_slice_in_dim(w, which * side, side, 1) for w in (query_weight, key_weight, value_weight)],
                axis=1,
            )

        mine = half(s)
        got = links.sibling(half(1 - s))
        self.links = links
        self.own = [jnp.where(s == layer, mine, got) for layer in range(2)]

    def layer(self, layer, *after):
        self.early = []
        links, own, depth, side = self.links, self.own[layer], self.depth, self.cols // 2
        if links.planar:
            size = depth // 4
            other = links.across(hold(lax.dynamic_slice_in_dim(own, links.d * size, size, 0), *after))
            self.early.append(other)
            for bit in (1, 2):
                far = links.along(other, bit)
                other = jnp.where(
                    links.d & bit == 0, jnp.concatenate([other, far]), jnp.concatenate([far, other])
                )
        else:
            other = links.across(own)
        if side % 128:
            both = jnp.stack([own.reshape(depth, 3, side), other.reshape(depth, 3, side)], axis=2)
            return both.reshape(depth, 6 * side)
        return jnp.concatenate([own, other], axis=1)


class PlaneSum:
    def __init__(self, links, part):
        self.links, self.part, self.half = links, part, part.shape[1] // 2

    def begin(self, *after):
        part = hold(self.part, *after)
        self.x = self.links.along(part[1::2, : self.half], 1)
        self.y = self.links.along(part[2:4, self.half :], 2)
        return [self.x, self.y]

    def finish(self, *after):
        part = hold(self.part, *after)
        self.x_end = self.links.along(add_low(part[1, self.half :], self.y[1]), 1)
        self.y_end = self.links.along(add_low(part[2, : self.half], self.x[1]), 2)
        return [self.x_end, self.y_end]

    def total(self, first, rows, more, after):
        part = hold(self.part, *after)
        here = slice(first, first + rows)
        if first + rows <= self.half:
            terms = [part[0, here], self.x[0, here], self.y_end[here]]
        else:
            there = slice(first - self.half, first - self.half + rows)
            terms = [part[0, here], self.y[0, there], self.x_end[there]]
        return add_low(*terms, *more)


class StarSum:
    def __init__(self, links, term_of, order):
        self.links, self.term_of, self.order, self.got = links, term_of, order, []

    def step(self, *after):
        n = len(self.got)
        if n < len(self.order) - 1:
            self.got.append(self.links.back(self.term_of(n, [], after), self.order[n]))
            return self.got[-1:]
        self.total = self.term_of(n, self.got, after)
        return [self.total]


class LayerSums:
    def __init__(self, links, parts, out_part, rows, out_rows, order):
        first, second = PlaneSum(links, parts[0]), PlaneSum(links, parts[1])
        out = PlaneSum(links, out_part)
        self.first, self.second, self.out = first, second, out
        self.mlp = StarSum(
            links, lambda n, more, after: (first, second)[n // 2].total(n % 2 * rows, rows, more, after), order
        )
        self.star = StarSum(
            links, lambda n, more, after: out.total(order[n] * out_rows, out_rows, more, after), order
        )

    def proj_total(self, *after):
        size = self.proj.part.shape[1] // 2
        self.proj_sum = jnp.concatenate([self.proj.total(n * size, size, [], after) for n in range(2)])
        return [self.proj_sum]


def both_halves(links, per_layer):
    mine = jnp.where(links.s == 0, per_layer[0], per_layer[1])
    got = links.sibling(jnp.where(links.s == 0, per_layer[1], per_layer[0]))
    return jnp.where(links.s == 0, mine, got), jnp.where(links.s == 0, got, mine)


def sum_everywhere(links, x):
    if links.planar:
        x = sum([x] + [links.along(x, bit) for bit in (1, 2, 3)])
        return sum([x] + [links.back(x, k) for k in (1, 2, 3)])
    return lax.psum(x, ("dp", "tensor"))


def norm_low(x, gain):
    inverse = lax.rsqrt(jnp.mean(x * x, axis=-1, keepdims=True) + EPS)
    return (x * inverse * gain).astype(BF)


def per_device(
    tokens,
    segment_ids,
    cotangent,
    query_weight,
    key_weight,
    value_weight,
    output_weight,
    gate_weight,
    up_weight,
    down_weight,
    attn_gain,
    mlp_gain,
):
    links = Links()
    T, DP, s = links.T, links.DP, links.s
    seq = segment_ids.shape[1]
    length, width = tokens.shape[1:]
    cols = query_weight.shape[2]
    hidden = gate_weight.shape[2] // 2
    meta = links.table()

    half = HEAD // 2
    frequency = np.float32(ROPE_BASE) ** (-np.arange(half, dtype=np.float32) / np.float32(half))
    angles = np.arange(seq, dtype=np.float32)[:, None] * frequency[None, :].astype(np.float32)
    cosine, sine = np.cos(angles), np.sin(angles)
    tables = (
        jnp.asarray(np.concatenate([cosine] * 4, axis=1), F32),
        jnp.asarray(np.concatenate([-sine, sine, -sine, sine], axis=1), F32),
    )
    segments = lax.dynamic_index_in_dim(segment_ids, links.r, 0, keepdims=False)
    lane = jnp.arange(256, dtype=jnp.int32)[None, :]
    place = jnp.where(lane < 128, lane - HEAD, lane - 128)
    same = segments[:, None] == place
    in_seg = (place >= 0) & (place < 4)
    ext_q = jnp.where(in_seg & ~same, -BIG, 0.0).astype(BF)
    ext_k = jnp.where((in_seg & same) | ((place >= 4) & (place < 7)), 1.0, 0.0).astype(BF)

    own_gains = jnp.concatenate([attn_gain, mlp_gain])
    other_gains = links.sibling(own_gains)
    gains = [
        jnp.where(s == layer, own_gains, other_gains) for layer in range(2)
    ]
    def flat(item):
        return item.reshape(2 * length, width)

    def blocked(item):
        return item.reshape(2, length, width)

    planar = links.planar
    order = list(range(1, T)) + [0]
    batches = [order[: T // 2], order[T // 2 :]]
    out_rows = cols // 2
    rows = 3 * hidden

    x = flat(links.swap_end(tokens, links.swap_blocks(tokens)))
    a = norm_low(x.astype(F32), gains[0][0:1])
    gather = Gather(links, output_weight[0], gate_weight[0], up_weight[0], down_weight[0])
    weights = gather.weights
    projection = Projection(links, query_weight[0], key_weight[0], value_weight[0])
    w_proj = [projection.layer(0), None]
    if planar:
        early = projection.early
        w_proj[1] = projection.layer(1)
        first = gather.step(0, x, *early)
        rings = first[0] + gather.step(0)[0] + gather.step(0)[0]
        begun = gather.step(1, x, *early)
    kept = []
    first_values = None
    for layer in range(2):
        gain_mlp = gains[layer][1:2]
        a_blocks = links.spread(blocked(a), *(begun[1] if planar and layer else []))
        deps = [[], [], [], []]
        if not planar:
            for _ in range(1, T):
                gather.step(layer)
            w_proj[1] = projection.layer(1)
        elif layer == 0:
            deps[1] = rings[:2] + w_proj[1:]
            deps[2] = rings[2:] + first[1]
        else:
            deps[1] = gather.step(1, a_blocks.arrays[1])[0]
            gather.step(1)
        q, k, v = project(meta, a_blocks, w_proj[layer], tables, (ext_q, ext_k), first_values, deps[0])
        o_rel, q = attend(meta, q, k, v, T, deps[1])
        o_blocks = links.exchange(o_rel, length)
        p = output_forward(meta, o_blocks, weights[layer], width, deps[2])
        if layer:
            dy = flat(links.swap_end(cotangent, links.swap_blocks(cotangent)))
            deps[3] = [dy]
        y, h, b, *saved = mlp_forward(
            meta, x, p, links.sibling(p), gain_mlp, weights[layer], batches, hidden, out_rows, deps[3]
        )
        kept.append((x, a_blocks, q, k, v, o_rel, o_blocks, h, b, saved))
        if planar and layer == 0:
            y = hold(y, *begun[0])
        x = (h + (y.astype(F32) + links.sibling(y).astype(F32))).astype(BF)
        if layer == 0:
            a, first_values = norm_low(x.astype(F32), gains[1][0:1]), v
    last = x

    first_grad = None
    mlp_sums, out_sums, proj_sums, gain_sums, sums = [None] * 2, [None] * 2, [None] * 2, [None] * 2, [None] * 2
    for layer in (1, 0):
        gain_attn, gain_mlp = gains[layer][0:1], gains[layer][1:2]
        x, a_blocks, q, k, v, o_rel, o_blocks, h, b, saved = kept[layer]
        dy_low = dy.astype(BF)
        due = {name: [] for name in ("middle", "attend", "project")}
        before = sums[1] if planar and layer == 0 else None
        *parts, db = mlp_backward(meta, dy_low, b, saved, weights[layer], batches, out_rows, DP, [])
        if before:
            due["middle"] = passing
            due["attend"] = before.mlp.step(parts[0]) + before.star.step() + before.star.step() + before.star.step()
            due["attend"].append(activations)
        dh, mlp_gain_grad, do_rel, out_part = middle(
            meta, dy, db, links.sibling(db), h, gain_mlp, o_blocks, weights[layer], DP, due["middle"]
        )
        if planar:
            mine = sums[layer] = LayerSums(links, parts, out_part, rows, out_rows, order)
            begun = mine.first.begin() + mine.second.begin()
            if before:
                do_rel = hold(do_rel, *begun[:2])
        do_blocks = links.exchange(do_rel, length)
        if planar:
            due["attend"] = due["attend"] + begun[:2]
            due["project"] = begun[2:] + mine.first.finish(do_rel)
            if before:
                begun = begun + mine.out.begin()
                due["project"] = due["project"] + before.mlp.step(do_rel) + before.star.step(do_rel)
                due["project"] = due["project"] + before.proj_total(do_rel)
        if layer:
            sent = links.swap_blocks(blocked(last), parts[0])
            due["attend"] = due["attend"] + [sent]
        back = attend_back(meta, q, k, v, o_rel, do_blocks, tables, first_grad, due["attend"])
        if before:
            mine.second.finish(back[0])
            mine.out.finish(back[0])
            mine.mlp.step(back[0])
            mine.mlp.step(back[0])
        if layer == 1:
            first_grad = back[3]
        near, far, dw = project_back(meta, a_blocks, back[:3], w_proj[layer], DP, due["project"])
        da, sending, summed = links.combine(near, far)
        da = flat(da).astype(F32)
        part, attn_gain_grad = norm_back(x.astype(F32), gain_attn, da)
        gain_sums[layer] = jnp.concatenate([attn_gain_grad, mlp_gain_grad])
        dy = dh + part
        if planar:
            mine.proj = PlaneSum(links, dw)
            if before:
                for _ in range(3):
                    mine.star.step(sending)
                mine.proj.begin(sending)
                mine.mlp.step(summed)
                mine.proj.finish(summed)
            else:
                activations = links.swap_end(blocked(last), hold(sent, near))
                passing = mine.second.finish(sending) + mine.out.begin(sending) + mine.proj.begin(sending)
                passing = passing + mine.mlp.step(sending) + mine.mlp.step(sending)
                passing = passing + mine.out.finish(summed) + mine.proj.finish(summed)
        else:
            if layer:
                activations = links.swap_end(blocked(last), sent)
            running = None
            for part in parts:
                for n in range(T // 2):
                    term = part[:, n * rows : (n + 1) * rows]
                    running = term if running is None else add_low(term, links.ring(running))
            mlp_sums[layer] = lax.psum_scatter(running, "dp", scatter_dimension=0, tiled=True)[0]
            running = None
            for n in order:
                term = out_part[:, n * out_rows : (n + 1) * out_rows]
                running = term if running is None else add_low(term, links.ring(running))
            out_sums[layer] = lax.psum_scatter(running, "dp", scatter_dimension=0, tiled=True)[0]
            proj_sums[layer] = lax.psum_scatter(dw, "dp", scatter_dimension=0, tiled=True)[0]
    half_width = width // 2
    mine = lax.dynamic_slice_in_dim(blocked(dy), s * half_width, half_width, 2)
    give = lax.dynamic_index_in_dim(mine, 1 - links.r, 0, keepdims=False).astype(BF)
    got = links.across(give)
    input_grad = jnp.where((jnp.arange(2) == links.r)[:, None, None], mine, got.astype(F32)[None])
    if planar:
        sums[0].star.step(got)
        sums[0].mlp.step(got)
        sums[0].proj_total(got)
        mlp_sums = [item.mlp.total for item in sums]
        out_sums = [item.star.total for item in sums]
        proj_sums = [item.proj_sum for item in sums]
    halves = both_halves(links, [jnp.concatenate([mlp_sums[n], out_sums[n]]) for n in range(2)])
    joined = []
    for item in proj_sums:
        if out_rows % 128:
            item = item.reshape(-1, 3, 2, out_rows)
            sides = [item[:, :, e].reshape(-1, 3 * out_rows) for e in range(2)]
        else:
            sides = [item[:, : 3 * out_rows], item[:, 3 * out_rows :]]
        joined.append(add_low(sides[0], links.across(sides[1])))
    proj = [item.astype(F32) for item in both_halves(links, joined)]
    halves = [item.astype(F32) for item in halves]
    squares = sum(jnp.sum(item * item) for item in halves + proj)
    gain_mine = jnp.where(s == 0, gain_sums[0], gain_sums[1])
    line = jnp.where(jnp.arange(width)[None, :] == 0, squares, 0.0)
    summed = sum_everywhere(links, jnp.concatenate([gain_mine, line]))
    gain_total = summed[0:2]
    grad_norm = jnp.sqrt(summed[2, 0] + jnp.sum(gain_total * gain_total)).reshape(1)
    shard = width // (DP * T)
    gain_out = lax.dynamic_slice_in_dim(gain_total, (links.d * T + links.z) * shard, shard, 1)
    grads = [
        jnp.concatenate([item[m * hidden : (m + 1) * hidden] for item in halves]) for m in range(3)
    ]
    own_out = jnp.concatenate([item[rows:] for item in halves])
    own_proj = [
        jnp.concatenate([item[:, m * out_rows : (m + 1) * out_rows] for item in proj], axis=1) for m in range(3)
    ]
    return (
        activations,
        input_grad,
        own_proj[0][None],
        own_proj[1][None],
        own_proj[2][None],
        own_out[None],
        grads[0].T[None],
        grads[1].T[None],
        grads[2][None],
        gain_out[0:1],
        gain_out[1:2],
        grad_norm,
    )


def solution(mesh):
    return jax.shard_map(
        per_device,
        mesh=mesh,
        in_specs=(
            P("dp", "tensor", None),
            P("dp", None),
            P("dp", "tensor", None),
            P("section", None, "tensor"),
            P("section", None, "tensor"),
            P("section", None, "tensor"),
            P("section", "tensor", None),
            P("section", None, "tensor"),
            P("section", None, "tensor"),
            P("section", "tensor", None),
            P("section", None),
            P("section", None),
        ),
        out_specs=(
            P("dp", "tensor", None),
            P("dp", "tensor", "section"),
            P("section", "dp", "tensor"),
            P("section", "dp", "tensor"),
            P("section", "dp", "tensor"),
            P("section", "tensor", "dp"),
            P("section", "dp", "tensor"),
            P("section", "dp", "tensor"),
            P("section", "tensor", "dp"),
            P("section", ("dp", "tensor")),
            P("section", ("dp", "tensor")),
            P("section"),
        ),
        check_vma=False,
    )
```

```python
import functools
import math

import jax
import jax.numpy as jnp
import numpy as np
from jax import lax
from jax.experimental import pallas as pl
from jax.experimental.pallas import tpu as pltpu
from jax.sharding import PartitionSpec as P

HEAD = 64
EPS = 1e-05
ROPE_BASE = 10000.0
BIG = 1e30
LOG2E = math.log2(math.e)
BF = jnp.bfloat16
F32 = jnp.float32
ALL = ("section", "dp", "tensor")
VMEM_LIMIT = 60 * 1024 * 1024
STEP = 256
CHUNK = 32
STRIP = 256

COL_OF_REL, ABS_OF_REL, OUT_OF_ABS, ABS_OF_OUT, CHIP_OF_RING, SIDE_OF_RING, REL_OF_DP, SECTION = 0, 8, 16, 24, 32, 40, 48, 56
PLACES = 64


def nn(a, b):
    return jnp.dot(a, b, preferred_element_type=F32)


def nt(a, b):
    return lax.dot_general(a, b, (((1,), (1,)), ((), ())), preferred_element_type=F32)


def tn(a, b):
    return lax.dot_general(a, b, (((0,), (0,)), ((), ())), preferred_element_type=F32)


def vmem_spec():
    return pl.BlockSpec(memory_space=pltpu.VMEM)


def any_spec():
    return pl.BlockSpec(memory_space=pl.ANY)


def smem_spec():
    return pl.BlockSpec(memory_space=pltpu.SMEM)


def sds(shape, dtype):
    return jax.ShapeDtypeStruct(shape, dtype)


def cost(micros):
    return pl.CostEstimate(flops=int(micros * 1.15e9), bytes_accessed=0, transcendentals=0)


def params(**more):
    return pltpu.CompilerParams(vmem_limit_bytes=VMEM_LIMIT, **more)


def call(kernel, deps, operands, *, in_specs, **rest):
    count, extra = len(operands), len(deps)

    def body(*refs):
        kernel(*refs[:count], *refs[count + extra :])

    return pl.pallas_call(body, in_specs=in_specs + [any_spec()] * extra, **rest)(*operands, *deps)


class Weights:
    def __init__(self, arrays, offset=0):
        self.arrays, self.offset = arrays, offset

    def copies(self, meta, refs, parts, sems, first):
        found = []
        for n, ref in enumerate(refs):
            for row, rows, target in parts:
                dst = target
                if len(refs) > 1:
                    width = ref.shape[1]
                    dst = target.at[:, pl.ds(pl.multiple_of(meta[COL_OF_REL + n] * width, width), width)]
                src = ref.at[pl.ds(self.offset + row, rows), :]
                found.append(pltpu.make_async_copy(src, dst, sems.at[first + len(found)]))
        return found


class Blocks:
    def __init__(self, arrays, places, by_section=()):
        self.arrays, self.places, self.by_section = arrays, places, by_section

    def copies(self, meta, refs, target, sems, first):
        found = []
        for i, (n, place) in enumerate(self.places):
            place = meta[SECTION] ^ place if i in self.by_section else place
            found.append(pltpu.make_async_copy(refs[n].at[place], target(i), sems.at[first + i]))
        return found


def unique(weights):
    operands, places = [], []
    for item in weights:
        mine = []
        for array in item.arrays:
            for n, other in enumerate(operands):
                if other is array:
                    mine.append(n)
                    break
            else:
                mine.append(len(operands))
                operands.append(array)
        places.append(mine)
    return operands, places


def start_all(copies):
    for copy in copies:
        copy.start()
    return copies


def wait_all(copies):
    for copy in copies:
        copy.wait()


def swap_halves(tile):
    lane = lax.broadcasted_iota(jnp.int32, tile.shape, 1)
    return jnp.where(lane % HEAD < HEAD // 2, pltpu.roll(tile, 128 - HEAD // 2, 1), pltpu.roll(tile, HEAD // 2, 1))


def column_of(part, pair, cols):
    side = cols // 2
    if side % 128:
        return part * cols + pair * 128
    per_side = side // 128
    return (pair // per_side * 3 + part) * side + pair % per_side * 128


def qkv_kernel(a_blocks, later, meta, *refs):
    blocks, held = len(a_blocks.places), len(a_blocks.arrays)
    a_refs = refs[:held]
    w_ref, cos_ref, sin_ref, extq_ref, extk_ref = refs[held : held + 5]
    rest = refs[held + 5 :]
    if later:
        first_ref, rest = rest[0], rest[1:]
    outs, (a_scr, w_scr, q_scr, k_scr, v_scr, cos_scr, sin_scr, extq_scr, extk_scr), rest = rest[:3], rest[3:12], rest[12:]
    if later:
        first_scr, rest = rest[0], rest[1:]
    sems, out_sems = rest
    length = a_scr.shape[1]
    cols = w_ref.shape[1] // 3
    loads = [
        pltpu.make_async_copy(w_ref, w_scr, sems.at[0]),
        pltpu.make_async_copy(cos_ref, cos_scr, sems.at[2]),
        pltpu.make_async_copy(sin_ref, sin_scr, sems.at[3]),
        pltpu.make_async_copy(extq_ref, extq_scr, sems.at[4]),
        pltpu.make_async_copy(extk_ref, extk_scr, sems.at[5]),
    ]
    if later:
        loads.append(pltpu.make_async_copy(first_ref, first_scr, sems.at[6]))
    more = a_blocks.copies(meta, a_refs, lambda i: a_scr.at[i], sems, 7)
    start_all(loads)
    start_all(more)
    lane = lax.broadcasted_iota(jnp.int32, (length, 128), 1)
    low = lane < HEAD
    ones_even = ((lane >= HEAD + 4) & (lane < HEAD + 7)).astype(F32)
    ones_odd = ((lane >= 4) & (lane < 7)).astype(F32)
    stores = []
    for i in range(blocks):
        start = pl.multiple_of(meta[ABS_OF_REL + i] * length, length)
        rows = pl.ds(start, length)
        if i == 0:
            wait_all(loads)
        more[i].wait()
        a = a_scr[i]
        cosine, sine = cos_scr[rows, :], sin_scr[rows, :]
        whole = nn(a, w_scr[...])
        for part, out in ((0, q_scr), (1, k_scr), (2, v_scr)):
            for pair in range(cols // 128):
                column = column_of(part, pair, cols)
                tile = whole[:, column : column + 128]
                if part < 2:
                    tile = tile * cosine + swap_halves(tile) * sine
                    ext = extq_scr if part == 0 else extk_scr
                    if part == 0:
                        tile = tile * (LOG2E * HEAD**-0.5)
                    even_ext = ext[rows, :128].astype(F32)
                    odd_ext = ext[rows, 128:].astype(F32)
                else:
                    if later:
                        first = jnp.where(
                            low,
                            first_scr[2 * pair, rows, :].astype(F32),
                            first_scr[2 * pair + 1, rows, :].astype(F32),
                        )
                        tile = 0.5 * tile + 0.5 * first
                    even_ext, odd_ext = ones_even, ones_odd
                out[i, 2 * pair] = jnp.where(low, tile, even_ext).astype(BF)
                out[i, 2 * pair + 1] = jnp.where(low, odd_ext, tile).astype(BF)
        for n, (scr, out) in enumerate(zip((q_scr, k_scr, v_scr), outs)):
            stores += start_all([pltpu.make_async_copy(scr.at[i], out.at[:, rows, :], out_sems.at[3 * i + n])])
    wait_all(stores)


def project(meta, a_blocks, w, tables, exts, first, deps):
    blocks, (_, length, width) = len(a_blocks.places), a_blocks.arrays[0].shape
    cols = w.shape[1] // 3
    heads = cols // HEAD
    seq = blocks * length
    out = sds((heads, seq, 128), BF)
    later = first is not None
    operands = [meta, *a_blocks.arrays, w, *tables, *exts] + ([first] if later else [])
    block = pltpu.VMEM((blocks, heads, length, 128), BF)
    return call(
        functools.partial(qkv_kernel, a_blocks, later),
        deps,
        operands,
        out_shape=(out, out, out),
        in_specs=[smem_spec()] + [any_spec()] * (len(operands) - 1),
        out_specs=(any_spec(),) * 3,
        scratch_shapes=[
            pltpu.VMEM((blocks, length, width), BF),
            pltpu.VMEM(w.shape, BF),
            block,
            block,
            block,
            pltpu.VMEM((seq, 128), F32),
            pltpu.VMEM((seq, 128), F32),
            pltpu.VMEM((seq, 256), BF),
            pltpu.VMEM((seq, 256), BF),
        ]
        + ([pltpu.VMEM(out.shape, BF)] if later else [])
        + [pltpu.SemaphoreType.DMA((blocks + 7,)), pltpu.SemaphoreType.DMA((3 * blocks,))],
        compiler_params=params(),
        cost_estimate=cost(10),
        name="project",
    )


def project_back_kernel(a_blocks, dp_blocks, meta, *refs):
    blocks, held = len(a_blocks.places), len(a_blocks.arrays)
    a_refs = refs[:held]
    dq_ref, dk_ref, dv_ref, w_ref, near_ref, far_ref, dw_ref = refs[held : held + 7]
    a_scr, d_scr, w_scr, da_scr, dw_scr, sems, out_sems = refs[held + 7 :]
    _, length, width = da_scr.shape
    cols = dq_ref.shape[1]
    loads = [pltpu.make_async_copy(w_ref, w_scr, sems.at[0])]
    for part, ref in enumerate((dq_ref, dk_ref, dv_ref)):
        for pair in range(cols // 128):
            target = d_scr.at[:, pl.ds(column_of(part, pair, cols), 128)]
            source = ref.at[:, pl.ds(pair * 128, 128)]
            loads.append(pltpu.make_async_copy(source, target, sems.at[len(loads)]))

    def place(i):
        start = pl.multiple_of(meta[ABS_OF_REL + i] * length, length)
        return a_scr.at[pl.ds(start, length)]

    more = a_blocks.copies(meta, a_refs, place, sems, len(loads))
    start_all(loads)
    start_all(more)
    wait_all(loads)
    order = list(range(1, blocks, 2)) + list(range(2, blocks, 2)) + [0]
    stores = []
    for i in order:
        start = pl.multiple_of(meta[ABS_OF_REL + i] * length, length)
        da_scr[i] = nt(d_scr[pl.ds(start, length), :], w_scr[...]).astype(BF)
        out = far_ref if i % 2 else near_ref
        stores += start_all([pltpu.make_async_copy(da_scr.at[i], out.at[i // 2], out_sems.at[i])])
    wait_all(more)
    size = width // dp_blocks
    for j in range(dp_blocks):
        dw_scr[meta[REL_OF_DP + j]] = tn(a_scr[:, j * size : (j + 1) * size], d_scr[...]).astype(BF)
    stores += start_all([pltpu.make_async_copy(dw_scr, dw_ref, out_sems.at[blocks])])
    wait_all(stores)


def project_back(meta, a_blocks, grads, w, dp_blocks, deps):
    blocks, (_, length, width) = len(a_blocks.places), a_blocks.arrays[0].shape
    cols = w.shape[1]
    seq = blocks * length
    half = sds((blocks // 2, length, width), BF)
    dw = (dp_blocks, width // dp_blocks, cols)
    return call(
        functools.partial(project_back_kernel, a_blocks, dp_blocks),
        deps,
        [meta, *a_blocks.arrays, *grads, w],
        out_shape=(half, half, sds(dw, BF)),
        in_specs=[smem_spec()] + [any_spec()] * (len(a_blocks.arrays) + 4),
        out_specs=(any_spec(),) * 3,
        scratch_shapes=[
            pltpu.VMEM((seq, width), BF),
            pltpu.VMEM((seq, cols), BF),
            pltpu.VMEM(w.shape, BF),
            pltpu.VMEM((blocks, length, width), BF),
            pltpu.VMEM(dw, BF),
            pltpu.SemaphoreType.DMA((blocks + 1 + cols // 128,)),
            pltpu.SemaphoreType.DMA((blocks + 1,)),
        ],
        compiler_params=params(),
        cost_estimate=cost(12),
        name="project_back",
    )


def three_parts(value):
    high = value.astype(BF).astype(F32)
    middle = (value - high).astype(BF).astype(F32)
    return high, middle, value - high - middle


def with_parts(base, value, odd):
    lane = lax.broadcasted_iota(jnp.int32, base.shape, 1)
    offset = 4 if odd else HEAD + 4
    high, middle, rest = three_parts(value)
    out = jnp.where(lane == offset, high, base)
    out = jnp.where(lane == offset + 1, middle, out)
    return jnp.where(lane == offset + 2, rest, out)


def attend_kernel(block, meta, q_ref, k_ref, v_ref, o_ref, ql_ref, vt_scr, tot_scr, top_scr, s_scr, p_scr):
    seq = q_ref.shape[1]
    length = o_ref.shape[1]
    key_row = lax.broadcasted_iota(jnp.int32, (STEP, block), 0)
    query_col = lax.broadcasted_iota(jnp.int32, (STEP, block), 1)
    for e in range(2):
        vt_scr[e] = v_ref[e].T

    def score(i, e):
        q = q_ref[e, i * block : (i + 1) * block, :]
        best = None
        for lo in range(0, (i + 1) * block, STEP):
            tile = nt(k_ref[e, lo : lo + STEP, :], q)
            if lo >= i * block:
                tile = jnp.where(key_row + (lo - i * block) <= query_col, tile, -BIG)
            s_scr[e, i % 2, lo : lo + STEP, :] = tile
            best = tile if best is None else jnp.maximum(best, tile)
        top_scr[e, :, i * block : (i + 1) * block] = best.max(axis=0, keepdims=True)

    def weigh(i, e):
        cols = slice(i * block, (i + 1) * block)
        top = top_scr[e, :, cols]
        for lo in range(0, (i + 1) * block, STEP):
            p_scr[e, lo : lo + STEP, :] = jnp.exp2(s_scr[e, i % 2, lo : lo + STEP, :] - top).astype(BF)
        tot_scr[e, :, cols] = nn(vt_scr[e, :, : (i + 1) * block], p_scr[e, : (i + 1) * block, :])

    count = seq // block
    for i in range(count + 1):
        for e in range(2):
            if i < count:
                score(i, e)
            if i > 0:
                weigh(i - 1, e)
    low = lax.broadcasted_iota(jnp.int32, (length, 128), 1) < HEAD
    lane = lax.broadcasted_iota(jnp.int32, (length, 128), 1)
    row = lax.broadcasted_iota(jnp.int32, (128, length), 0)
    for i in range(seq // length):
        rows = slice(i * length, (i + 1) * length)
        results = []
        for e in range(2):
            place = 4 if e else HEAD + 4
            total = tot_scr[e, :, rows]
            weight = total[place : place + 1, :]
            total = total * (1.0 / weight)
            for n, value in enumerate(three_parts(-(top_scr[e, :, rows] + jnp.log2(weight)))):
                total = jnp.where(row == place + n, value, total)
            turned = total.T
            results.append(turned)
            parts = (lane >= place) & (lane < place + 3)
            ql_ref[e, rows, :] = jnp.where(parts, turned, q_ref[e, rows, :].astype(F32)).astype(BF)
        o_ref[meta[OUT_OF_ABS + i]] = jnp.where(low, results[0], results[1]).astype(BF)


def attend(meta, q, k, v, blocks, deps):
    heads, seq, _ = q.shape
    pairs = heads // 2
    length = seq // blocks
    head_spec = pl.BlockSpec((2, seq, 128), lambda p: (p, 0, 0))
    return call(
        functools.partial(attend_kernel, min(256, length)),
        deps,
        [meta, q, k, v],
        grid=(pairs,),
        out_shape=(sds((blocks, length, pairs * 128), BF), sds(q.shape, BF)),
        in_specs=[smem_spec(), head_spec, head_spec, head_spec],
        out_specs=(pl.BlockSpec((blocks, length, 128), lambda p: (0, 0, p)), head_spec),
        scratch_shapes=[
            pltpu.VMEM((2, 128, seq), BF),
            pltpu.VMEM((2, 128, seq), F32),
            pltpu.VMEM((2, 1, seq), F32),
            pltpu.VMEM((2, 2, seq, min(256, length)), F32),
            pltpu.VMEM((2, seq, min(256, length)), BF),
        ],
        compiler_params=params(),
        cost_estimate=cost(14.5),
        name="attend",
    )


def attend_back_kernel(block, blocks, later, meta, q_ref, k_ref, v_ref, o_ref, *refs):
    do_refs = refs[:blocks]
    cos_ref, sin_ref = refs[blocks : blocks + 2]
    rest = refs[blocks + 2 :]
    if not later:
        first_ref, rest = rest[0], rest[1:]
    dq_ref, dk_ref, dv_ref = rest[:3]
    rest = rest[3:]
    if later:
        first_out, rest = rest[0], rest[1:]
    do_scr, dq_scr, dk_scr, dv_scr, kt_scr, p_scr, ds_scr = rest
    seq = q_ref.shape[1]
    length = o_ref.shape[1]
    lane = lax.broadcasted_iota(jnp.int32, (length, 128), 1)
    low = lane < HEAD
    for i in range(blocks):
        start = pl.multiple_of(meta[ABS_OF_OUT + i] * length, length)
        rows = pl.ds(start, length)
        do = do_refs[i][...].astype(F32)
        product = do * o_ref[i].astype(F32)
        for e in range(2):
            mine = low if e == 0 else jnp.logical_not(low)
            delta = jnp.sum(jnp.where(mine, product, 0.0), axis=1, keepdims=True)
            do_scr[e, rows, :] = with_parts(jnp.where(mine, do, 0.0), -delta, e == 1).astype(BF)
    key_row = lax.broadcasted_iota(jnp.int32, (STEP, block), 0)
    query_col = lax.broadcasted_iota(jnp.int32, (STEP, block), 1)
    for e in range(2):
        kt_scr[e] = k_ref[e].T
    count = seq // block

    def weigh(i, e):
        cols = slice(i * block, (i + 1) * block)
        q = q_ref[e, cols, :]
        do = do_scr[e, cols, :]
        for lo in range(0, (i + 1) * block, STEP):
            rows = slice(lo, lo + STEP)
            scores = nt(k_ref[e, rows, :], q)
            if lo >= i * block:
                scores = jnp.where(key_row + (lo - i * block) <= query_col, scores, -BIG)
            prob = jnp.exp2(scores)
            p_scr[e, rows, cols] = prob.astype(BF)
            ds_scr[e, rows, cols] = (prob * nt(v_ref[e, rows, :], do)).astype(BF)

    def query_grad(i, e):
        cols = slice(i * block, (i + 1) * block)
        dq_scr[e, :, cols] = nn(kt_scr[e, :, : (i + 1) * block], ds_scr[e, : (i + 1) * block, cols])

    def key_grads(i, e):
        rows, cols = slice(i * block, (i + 1) * block), slice(i * block, seq)
        dv_scr[e, rows, :] = nn(p_scr[e, rows, cols], do_scr[e, cols, :])
        dk_scr[e, rows, :] = nn(ds_scr[e, rows, cols], q_ref[e, cols, :])

    for i in range(count + 1):
        for e in range(2):
            if i < count:
                weigh(i, e)
            if i > 0:
                query_grad(i - 1, e)
    for i in range(count):
        for e in range(2):
            key_grads(i, e)
    for i in range(blocks):
        rows = slice(i * length, (i + 1) * length)
        cosine, sine = cos_ref[rows, :], sin_ref[rows, :]
        dq = jnp.where(low, dq_scr[0, :, rows].T, dq_scr[1, :, rows].T) * (HEAD**-0.5)
        dk = jnp.where(low, dk_scr[0, rows, :], dk_scr[1, rows, :]) * (1.0 / LOG2E)
        dv = jnp.where(low, dv_scr[0, rows, :], dv_scr[1, rows, :])
        dq_ref[rows, :] = (dq * cosine - swap_halves(dq) * sine).astype(BF)
        dk_ref[rows, :] = (dk * cosine - swap_halves(dk) * sine).astype(BF)
        if later:
            dv_ref[rows, :] = (0.5 * dv).astype(BF)
            first_out[rows, :] = 0.5 * dv
        else:
            dv_ref[rows, :] = (dv + first_ref[rows, :]).astype(BF)


def attend_back(meta, q, k, v, o, do_blocks, tables, first, deps):
    heads, seq, _ = q.shape
    pairs = heads // 2
    blocks, length, cols = o.shape
    later = first is None
    head_spec = pl.BlockSpec((2, seq, 128), lambda p: (p, 0, 0))
    col_spec = pl.BlockSpec((seq, 128), lambda p: (0, p))
    table_spec = pl.BlockSpec((seq, 128), lambda p: (0, 0))
    out = sds((seq, cols), BF)
    return call(
        functools.partial(attend_back_kernel, min(256, length), blocks, later),
        deps,
        [meta, q, k, v, o, *[do_blocks.arrays[n] for n, _ in do_blocks.places], *tables, *([] if later else [first])],
        grid=(pairs,),
        out_shape=(out, out, out) + ((sds((seq, cols), F32),) if later else ()),
        in_specs=[smem_spec(), head_spec, head_spec, head_spec]
        + [pl.BlockSpec((blocks, length, 128), lambda p: (0, 0, p))]
        + [pl.BlockSpec((None, length, 128), functools.partial(lambda n, p: (n, 0, p), n)) for _, n in do_blocks.places]
        + [table_spec] * 2
        + ([] if later else [col_spec]),
        out_specs=(col_spec,) * (4 if later else 3),
        scratch_shapes=[
            pltpu.VMEM((2, seq, 128), BF),
            pltpu.VMEM((2, 128, seq), F32),
            pltpu.VMEM((2, seq, 128), F32),
            pltpu.VMEM((2, seq, 128), F32),
            pltpu.VMEM((2, 128, seq), BF),
            pltpu.VMEM((2, seq, seq), BF),
            pltpu.VMEM((2, seq, seq), BF),
        ],
        compiler_params=params(),
        cost_estimate=cost(29.5),
        name="attend_back",
    )


def place_output(weights, places, meta, refs, target, sems, first):
    found = []
    rows = target.shape[1] // 2
    for k, item in enumerate(weights):
        side = pl.multiple_of(meta[SIDE_OF_RING + k] * rows, rows)
        part = (0, rows, target.at[meta[CHIP_OF_RING + k], pl.ds(side, rows)])
        found += item.copies(meta, [refs[n] for n in places[k]], [part], sems, first + 4 * k)
    return found


def output_kernel(o_blocks, weights, places, meta, *refs):
    o_refs, refs = refs[: len(o_blocks.arrays)], refs[len(o_blocks.arrays) :]
    number = len({n for place in places for n in place})
    w_refs, (p_ref, o_scr, w_scr, sems) = refs[:number], refs[number:]
    count = len(o_blocks.places)
    length = o_scr.shape[1] // 2
    loads = o_blocks.copies(meta, o_refs, lambda i: o_scr.at[i // 2, pl.ds(i % 2 * length, length)], sems, 0)
    loads += place_output(weights, places, meta, w_refs, w_scr, sems, count)
    wait_all(start_all(loads))
    for f in range(2):
        rows = slice(f * length, (f + 1) * length)
        total = nn(o_scr[0, rows, :], w_scr[0])
        for n in range(1, count // 2):
            total += nn(o_scr[n, rows, :], w_scr[n])
        p_ref[rows, :] = total.astype(BF)


def output_forward(meta, o_blocks, weights, width, deps):
    count = len(o_blocks.places)
    _, length, cols = o_blocks.arrays[0].shape
    operands, places = unique(weights)
    return call(
        functools.partial(output_kernel, o_blocks, weights, places),
        deps,
        [meta, *o_blocks.arrays, *operands],
        out_shape=sds((2 * length, width), BF),
        in_specs=[smem_spec()] + [any_spec()] * (len(o_blocks.arrays) + len(operands)),
        out_specs=vmem_spec(),
        scratch_shapes=[
            pltpu.VMEM((count // 2, 2 * length, cols), BF),
            pltpu.VMEM((count // 2, cols, width), BF),
            pltpu.SemaphoreType.DMA((5 * count,)),
        ],
        compiler_params=params(),
        cost_estimate=cost(5),
        name="output",
    )


def place_hidden(batch, weights, places, meta, refs, target, sems, first, row):
    hidden = target.shape[1] // len(batch)
    found = []
    for n, k in enumerate(batch):
        parts = [(row + m * hidden, hidden, target.at[m, pl.ds(n * hidden, hidden)]) for m in range(3)]
        found += weights[k].copies(meta, [refs[i] for i in places[k]], parts, sems, first + 12 * n)
    return found


def mlp_kernel(batches, weights, places, row, meta, x_ref, p_ref, other_ref, gain_ref, *refs):
    number = len({n for place in places for n in place})
    w_refs, refs = refs[:number], refs[number:]
    count = len(batches)
    y_ref, h_ref, b_ref = refs[:3]
    g_refs, u_refs, refs = refs[3 : 3 + count], refs[3 + count : 3 + 2 * count], refs[3 + 2 * count :]
    w_scr, sems = refs
    first = [12 * sum(len(other) for other in batches[:n]) for n in range(count)]

    def loads(n):
        return place_hidden(batches[n], weights, places, meta, w_refs, w_scr.at[n], sems, first[n], row)

    @pl.when(pl.program_id(0) == 0)
    def _():
        for n in range(count):
            start_all(loads(n))

    gain = gain_ref[...]
    for start in range(0, x_ref.shape[0], CHUNK):
        rows = slice(start, start + CHUNK)
        h = x_ref[rows, :].astype(F32) + (p_ref[rows, :].astype(F32) + other_ref[rows, :].astype(F32))
        h_ref[rows, :] = h
        inverse = lax.rsqrt(jnp.mean(h * h, axis=1, keepdims=True) + EPS)
        b_ref[rows, :] = (h * inverse * gain).astype(BF)

    @pl.when(pl.program_id(0) == 0)
    def _():
        for n in range(count):
            wait_all(loads(n))

    for start in range(0, x_ref.shape[0], STRIP):
        rows = slice(start, start + STRIP)
        b = b_ref[rows, :]
        total = None
        for n in range(count):
            g = nt(b, w_scr[n, 0])
            u = nt(b, w_scr[n, 1])
            g_refs[n][rows, :] = g.astype(BF)
            u_refs[n][rows, :] = u.astype(BF)
            m = (g * jax.nn.sigmoid(g) * u).astype(BF)
            term = nn(m, w_scr[n, 2])
            total = term if total is None else total + term
        y_ref[rows, :] = total.astype(BF)


def mlp_forward(meta, x, p, other, gain, weights, batches, hidden, row, deps):
    rows, width = x.shape
    operands, places = unique(weights)
    size = [len(batch) * hidden for batch in batches]
    quarters = sum(len(batch) for batch in batches)
    low = sds((rows, width), BF)
    saved = tuple(sds((rows, n), BF) for n in size)
    block = min(256, rows)

    def by_rows(n):
        return pl.BlockSpec((block, n), lambda i: (i, 0))

    return call(
        functools.partial(mlp_kernel, batches, weights, places, row),
        deps,
        [meta, x, p, other, gain, *operands],
        grid=(rows // block,),
        out_shape=(low, sds((rows, width), F32), low) + saved + saved,
        in_specs=[smem_spec()]
        + [by_rows(width)] * 3
        + [pl.BlockSpec((1, width), lambda i: (0, 0))]
        + [any_spec()] * len(operands),
        out_specs=(by_rows(width),) * 3 + tuple(by_rows(n) for n in size) * 2,
        scratch_shapes=[
            pltpu.VMEM((len(batches), 3, size[0], width), BF),
            pltpu.SemaphoreType.DMA((12 * quarters,)),
        ],
        compiler_params=params(),
        cost_estimate=cost(19),
        name="mlp",
    )


def mlp_back_kernel(batches, weights, places, row, meta, dy_ref, b_ref, *refs):
    count = len(batches)
    g_refs, u_refs, refs = refs[:count], refs[count : 2 * count], refs[2 * count :]
    number = len({n for place in places for n in place})
    w_refs, refs = refs[:number], refs[number:]
    out_refs, refs = refs[:count], refs[count:]
    db_ref, dy_scr, b_scr, g_scr, u_scr, w_scr, low_scr, grad_scr, sems, out_sems = refs
    dy_load = pltpu.make_async_copy(dy_ref, dy_scr, sems.at[0])
    b_load = pltpu.make_async_copy(b_ref, b_scr, sems.at[1])
    dy_load.start()
    loads, used = [], 2
    for n, batch in enumerate(batches):
        group = place_hidden(batch, weights, places, meta, w_refs, w_scr.at[n], sems, used, row)
        used += 12 * len(batch)
        for source, target in ((g_refs[n], g_scr.at[n]), (u_refs[n], u_scr.at[n])):
            group.append(pltpu.make_async_copy(source, target, sems.at[used]))
            used += 1
        loads.append(start_all(group))
    b_load.start()
    total_rows, width = dy_scr.shape
    hidden = w_scr.shape[2] // len(batches[0])
    columns, _, size = out_refs[0].shape
    stores = []
    dy_load.wait()
    for n, batch in enumerate(batches):
        wait_all(loads[n])
        for start in range(0, total_rows, STRIP):
            rows = slice(start, start + STRIP)
            dm = nt(dy_scr[rows, :], w_scr[n, 2])
            g = g_scr[n, rows, :].astype(F32)
            u = u_scr[n, rows, :].astype(F32)
            gate = jax.nn.sigmoid(g)
            active = g * gate
            low_scr[n, 0, rows, :] = (dm * u * (gate + active * (1.0 - gate))).astype(BF)
            low_scr[n, 1, rows, :] = (dm * active).astype(BF)
            low_scr[n, 2, rows, :] = (active * u).astype(BF)
    b_load.wait()
    for n, batch in enumerate(batches):
        for m in range(3):
            grad_scr[n, m] = tn(low_scr[n, m], dy_scr[...] if m == 2 else b_scr[...]).astype(BF)
            for q in range(len(batch)):
                for j in range(columns):
                    copy = pltpu.make_async_copy(
                        grad_scr.at[n, m, pl.ds(q * hidden, hidden), pl.ds(j * size, size)],
                        out_refs[n].at[meta[REL_OF_DP + j], pl.ds((q * 3 + m) * hidden, hidden), :],
                        out_sems.at[((n * 3 + m) * len(batch) + q) * columns + j],
                    )
                    copy.start()
                    stores.append(copy)
    for start in range(0, total_rows, 256):
        rows = slice(start, start + 256)
        db = None
        for n in range(count):
            term = nn(low_scr[n, 0, rows, :], w_scr[n, 0]) + nn(low_scr[n, 1, rows, :], w_scr[n, 1])
            db = term if db is None else db + term
        db_ref[rows, :] = db.astype(BF)
    wait_all(stores)


def mlp_backward(meta, dy, b, saved, weights, batches, row, dp_blocks, deps):
    rows, width = b.shape
    count = len(batches)
    size = saved[0].shape[1]
    operands, places = unique(weights)
    copies = sum(12 * len(batch) + 2 for batch in batches)
    return call(
        functools.partial(mlp_back_kernel, batches, weights, places, row),
        deps,
        [meta, dy, b, *saved, *operands],
        out_shape=(sds((dp_blocks, 3 * size, width // dp_blocks), BF),) * count + (sds((rows, width), BF),),
        in_specs=[smem_spec()] + [any_spec()] * (2 + 2 * count + len(operands)),
        out_specs=(any_spec(),) * count + (vmem_spec(),),
        scratch_shapes=[
            pltpu.VMEM((rows, width), BF),
            pltpu.VMEM((rows, width), BF),
            pltpu.VMEM((count, rows, size), BF),
            pltpu.VMEM((count, rows, size), BF),
            pltpu.VMEM((count, 3, size, width), BF),
            pltpu.VMEM((count, 3, rows, size), BF),
            pltpu.VMEM((count, 3, size, width), BF),
            pltpu.SemaphoreType.DMA((2 + copies,)),
            pltpu.SemaphoreType.DMA((3 * dp_blocks * sum(len(batch) for batch in batches),)),
        ],
        compiler_params=params(),
        cost_estimate=cost(28),
        name="mlp_back",
    )


def norm_back(values, gain, grads):
    inverse = lax.rsqrt(jnp.mean(values * values, axis=1, keepdims=True) + EPS)
    normed = values * inverse
    scaled = grads * gain
    gain_grad = jnp.sum(grads * normed, axis=0, keepdims=True)
    return inverse * (scaled - normed * jnp.mean(scaled * normed, axis=1, keepdims=True)), gain_grad


def middle_kernel(o_blocks, weights, places, meta, dy_ref, db_ref, other_ref, h_ref, gain_ref, *refs):
    o_refs, refs = refs[: len(o_blocks.arrays)], refs[len(o_blocks.arrays) :]
    number = len({n for place in places for n in place})
    w_refs, refs = refs[:number], refs[number:]
    dh_ref, gain_out, do_ref, grad_ref, w_scr, o_scr, low_scr, grad_scr, sems, out_sems = refs
    count = len(o_blocks.places)
    length = o_scr.shape[1] // 2
    step, steps = pl.program_id(0), pl.num_programs(0)

    def loads():
        found = o_blocks.copies(meta, o_refs, lambda i: o_scr.at[i // 2, pl.ds(i % 2 * length, length)], sems, 0)
        return found + place_output(weights, places, meta, w_refs, w_scr, sems, count)

    @pl.when(step == 0)
    def _():
        start_all(loads())
        gain_out[...] = jnp.zeros_like(gain_out)

    gain = gain_ref[...]
    block = dy_ref.shape[0]
    first = pl.multiple_of(step * block, block)
    total = None
    for start in range(0, block, CHUNK):
        rows = slice(start, start + CHUNK)
        db = db_ref[rows, :].astype(F32) + other_ref[rows, :].astype(F32)
        part, gain_grad = norm_back(h_ref[rows, :], gain, db)
        dh = dy_ref[rows, :].astype(F32) + part
        dh_ref[rows, :] = dh
        low_scr[pl.ds(first + start, CHUNK), :] = dh.astype(BF)
        total = gain_grad if total is None else total + gain_grad
    gain_out[...] += total

    @pl.when(step == 0)
    def _():
        wait_all(loads())

    low = low_scr[pl.ds(first, block), :]
    for n in range(count // 2):
        do_ref[n] = nt(low, w_scr[n]).astype(BF)

    @pl.when(step == steps - 1)
    def _():
        for n in range(count // 2):
            grad_scr[n] = tn(o_scr[n], low_scr[...]).astype(BF)
        stores = []
        columns = grad_ref.shape[0]
        size = grad_ref.shape[2]
        rows = o_scr.shape[2] // 2
        for k in range(count):
            side = pl.multiple_of(meta[SIDE_OF_RING + k] * rows, rows)
            for j in range(columns):
                stores.append(
                    pltpu.make_async_copy(
                        grad_scr.at[meta[CHIP_OF_RING + k], pl.ds(side, rows), pl.ds(j * size, size)],
                        grad_ref.at[meta[REL_OF_DP + j], pl.ds(k * rows, rows), :],
                        out_sems.at[k * columns + j],
                    )
                )
        wait_all(start_all(stores))


def middle(meta, dy, db, other, h, gain, o_blocks, weights, dp_blocks, deps):
    count = len(o_blocks.places)
    _, length, cols = o_blocks.arrays[0].shape
    width = h.shape[1]
    operands, places = unique(weights)
    block = 256
    by_rows = pl.BlockSpec((block, width), lambda i: (i, 0))
    fixed = pl.BlockSpec((1, width), lambda i: (0, 0))
    return call(
        functools.partial(middle_kernel, o_blocks, weights, places),
        deps,
        [meta, dy, db, other, h, gain, *o_blocks.arrays, *operands],
        grid=(2 * length // block,),
        out_shape=(
            sds((2 * length, width), F32),
            sds((1, width), F32),
            sds((count // 2, 2 * length, cols), BF),
            sds((dp_blocks, count * cols // 2, width // dp_blocks), BF),
        ),
        in_specs=[smem_spec()]
        + [by_rows] * 4
        + [fixed]
        + [any_spec()] * (len(o_blocks.arrays) + len(operands)),
        out_specs=(by_rows, fixed, pl.BlockSpec((count // 2, block, cols), lambda i: (0, i, 0)), any_spec()),
        scratch_shapes=[
            pltpu.VMEM((count // 2, cols, width), BF),
            pltpu.VMEM((count // 2, 2 * length, cols), BF),
            pltpu.VMEM((2 * length, width), BF),
            pltpu.VMEM((count // 2, cols, width), BF),
            pltpu.SemaphoreType.DMA((5 * count,)),
            pltpu.SemaphoreType.DMA((count * dp_blocks,)),
        ],
        compiler_params=params(),
        cost_estimate=cost(13),
        name="middle",
    )


def add_low(*terms):
    total = terms[0].astype(F32)
    for term in terms[1:]:
        total = total + term.astype(F32)
    return total.astype(BF)


def hold(x, *after):
    return lax.optimization_barrier((x, *after))[0] if after else x


class Links:
    def __init__(self):
        self.T = lax.axis_size("tensor")
        self.DP = lax.axis_size("dp")
        self.G = self.T // 2
        self.s = lax.axis_index("section")
        self.d = lax.axis_index("dp")
        self.z = lax.axis_index("tensor")
        self.r = self.z // self.G
        self.home = self.s == self.r
        self.planar = self.DP == 4 and self.T == 4
        self.order = [0] + list(range(1, self.T, 2)) + list(range(self.T - 2, 0, -2))

    def sibling(self, x):
        return lax.ppermute(x, "section", [(0, 1), (1, 0)])

    def ring(self, x):
        order = self.order
        return lax.ppermute(x, "tensor", [(order[i], order[(i + 1) % self.T]) for i in range(self.T)])

    def back(self, x, k):
        order = self.order
        return lax.ppermute(x, "tensor", [(order[i], order[(i - k) % self.T]) for i in range(self.T)])

    def along(self, x, bit):
        return lax.ppermute(x, "dp", [(i, i ^ bit) for i in range(self.DP)])

    def across(self, x):
        return lax.ppermute(x, "tensor", [(z, (z + self.G) % self.T) for z in range(self.T)])

    def shift(self, x, k):
        pairs = [(z, z // self.G * self.G + (z + k) % self.G) for z in range(self.T)]
        return lax.ppermute(x, "tensor", pairs)

    def swap_blocks(self, x, *after):
        pairs = []
        for s in range(2):
            z0 = s * self.G
            for z in range(z0, z0 + self.G):
                pairs.append((s * self.T + z, s * self.T + (z + self.G) % self.T))
        give = hold(lax.dynamic_index_in_dim(x, 1 - self.r, 0, keepdims=False), *after)
        return lax.ppermute(give, ("section", "tensor"), pairs)

    def swap_end(self, x, got):
        got = jnp.where(self.home, self.sibling(got), got)
        mine = (jnp.arange(2) == self.r)[:, None, None]
        return jnp.where(mine, x, got[None])

    def spread(self, x, *also):
        give = lax.dynamic_index_in_dim(x, self.s, 0)
        arrays, places = [x], [(0, 0), (0, 1)]
        for k in range(1, self.G):
            got = hold(self.shift(give, -k), *also)
            arrays += [got, self.sibling(got)]
            places += [(len(arrays) - 2, 0), (len(arrays) - 1, 0)]
        return Blocks(arrays, places, (0, 1))

    def exchange(self, x, length):
        cols = x.shape[-1]
        arrays, places = [x.reshape(self.T, length, cols)], [(0, 0), (0, 1)] + [None] * (self.T - 2)
        for k in range(1, self.G):
            got = self.shift(x.reshape(self.G, 2 * length, cols)[k], k)
            chip = -k % self.G
            places[2 * chip], places[2 * chip + 1] = (len(arrays), 0), (len(arrays), 1)
            arrays.append(got.reshape(2, length, cols))
        return Blocks(arrays, places)

    def combine(self, near, far):
        got = self.sibling(far)
        terms, sent = [near[0], got[0]], []
        for k in range(1, self.G):
            sent.append(add_low(near[k], got[k]))
            terms.append(self.shift(sent[-1], k))
        mine = add_low(*terms)
        both = (jnp.arange(2) == self.s)[:, None, None]
        return jnp.where(both, mine[None], self.sibling(mine)[None]), sent[0], mine

    def table(self):
        T, G, DP, order = self.T, self.G, self.DP, self.order
        table = np.zeros((2, DP, T, PLACES), np.int32)
        for s in range(2):
            for d in range(DP):
                for z in range(T):
                    out, c, r, position = table[s, d, z], z % G, z // G, order.index(z)
                    for rel in range(4):
                        out[COL_OF_REL + rel] = d ^ rel if self.planar else rel
                    for i in range(T):
                        quarter = order[(position - i) % T]
                        out[ABS_OF_REL + i] = (c + i // 2) % G + G * (s ^ (i % 2))
                        out[OUT_OF_ABS + i] = 2 * ((i % G - c) % G) + i // G
                        out[ABS_OF_OUT + i] = (c + i // 2) % G + G * (i % 2)
                        out[CHIP_OF_RING + i] = (quarter % G - c) % G
                        out[SIDE_OF_RING + i] = (quarter // G) ^ r
                    for i in range(DP):
                        out[REL_OF_DP + i] = (d ^ i) if self.planar else i
                    out[SECTION] = s
        index = (self.s * DP + self.d) * T + self.z
        return lax.dynamic_index_in_dim(jnp.asarray(table.reshape(-1, PLACES)), index, 0, keepdims=False)


class Gather:
    def __init__(self, links, output_weight, gate_weight, up_weight, down_weight):
        s, d = links.s, links.d

        def half(which):
            def cut(x, dim):
                size = x.shape[dim] // 2
                return lax.dynamic_slice_in_dim(x, which * size, size, dim)

            return jnp.concatenate(
                [cut(output_weight, 0), cut(gate_weight, 1).T, cut(up_weight, 1).T, cut(down_weight, 0)]
            )

        mine = half(s)
        got = links.sibling(half(1 - s))
        self.links = links
        whole = [jnp.where(s == layer, mine, got) for layer in range(2)]
        self.weights = [[Weights([item])] for item in whole]
        if links.planar:
            size = output_weight.shape[1] // 4
            whole = [lax.dynamic_slice_in_dim(item, d * size, size, 1) for item in whole]
        self.current = whole

    def step(self, layer, *after):
        ring = self.links.ring(hold(self.current[layer], *after))
        self.current[layer] = ring
        plane = [self.links.along(ring, bit) for bit in (1, 2, 3)] if self.links.planar else []
        self.weights[layer].append(Weights([ring] + plane))
        return [ring], plane

    def two_steps(self, layer):
        once = self.links.ring(self.current[layer])
        self.current[layer] = self.links.ring(once)
        joined = jnp.concatenate([once, self.current[layer]])
        pieces = [joined] + [self.links.along(joined, bit) for bit in (1, 2, 3)]
        self.weights[layer] += [Weights(pieces), Weights(pieces, once.shape[0])]
        return [once, self.current[layer]]


class Projection:
    def __init__(self, links, query_weight, key_weight, value_weight):
        s = links.s
        self.depth, self.cols = query_weight.shape
        side = self.cols // 2

        def half(which):
            return jnp.concatenate(
                [lax.dynamic_slice_in_dim(w, which * side, side, 1) for w in (query_weight, key_weight, value_weight)],
                axis=1,
            )

        mine = half(s)
        got = links.sibling(half(1 - s))
        self.links = links
        self.own = [jnp.where(s == layer, mine, got) for layer in range(2)]

    def layer(self, layer, *after):
        self.early = []
        links, own, depth, side = self.links, self.own[layer], self.depth, self.cols // 2
        if links.planar:
            size = depth // 4
            other = links.across(hold(lax.dynamic_slice_in_dim(own, links.d * size, size, 0), *after))
            self.early.append(other)
            for bit in (1, 2):
                far = links.along(other, bit)
                other = jnp.where(
                    links.d & bit == 0, jnp.concatenate([other, far]), jnp.concatenate([far, other])
                )
        else:
            other = links.across(own)
        if side % 128:
            both = jnp.stack([own.reshape(depth, 3, side), other.reshape(depth, 3, side)], axis=2)
            return both.reshape(depth, 6 * side)
        return jnp.concatenate([own, other], axis=1)


class PlaneSum:
    def __init__(self, links, part):
        self.links, self.part, self.half = links, part, part.shape[1] // 2

    def begin(self, *after):
        part = hold(self.part, *after)
        self.x = self.links.along(part[1::2, : self.half], 1)
        self.y = self.links.along(part[2:4, self.half :], 2)
        return [self.x, self.y]

    def finish(self, *after):
        part = hold(self.part, *after)
        self.x_end = self.links.along(add_low(part[1, self.half :], self.y[1]), 1)
        self.y_end = self.links.along(add_low(part[2, : self.half], self.x[1]), 2)
        return [self.x_end, self.y_end]

    def total(self, first, rows, more, after):
        part = hold(self.part, *after)
        here = slice(first, first + rows)
        if first + rows <= self.half:
            terms = [part[0, here], self.x[0, here], self.y_end[here]]
        else:
            there = slice(first - self.half, first - self.half + rows)
            terms = [part[0, here], self.y[0, there], self.x_end[there]]
        return add_low(*terms, *more)


class StarSum:
    def __init__(self, links, term_of, order):
        self.links, self.term_of, self.order, self.got = links, term_of, order, []

    def step(self, *after):
        n = len(self.got)
        if n < len(self.order) - 1:
            self.got.append(self.links.back(self.term_of(n, [], after), self.order[n]))
            return self.got[-1:]
        self.total = self.term_of(n, self.got, after)
        return [self.total]


class LayerSums:
    def __init__(self, links, parts, out_part, rows, out_rows, order):
        first, second = PlaneSum(links, parts[0]), PlaneSum(links, parts[1])
        out = PlaneSum(links, out_part)
        self.first, self.second, self.out = first, second, out
        self.mlp = StarSum(
            links, lambda n, more, after: (first, second)[n // 2].total(n % 2 * rows, rows, more, after), order
        )
        self.star = StarSum(
            links, lambda n, more, after: out.total(order[n] * out_rows, out_rows, more, after), order
        )

    def proj_total(self, *after):
        size = self.proj.part.shape[1] // 2
        self.proj_sum = jnp.concatenate([self.proj.total(n * size, size, [], after) for n in range(2)])
        return [self.proj_sum]


def both_halves(links, per_layer):
    mine = jnp.where(links.s == 0, per_layer[0], per_layer[1])
    got = links.sibling(jnp.where(links.s == 0, per_layer[1], per_layer[0]))
    return jnp.where(links.s == 0, mine, got), jnp.where(links.s == 0, got, mine)


def sum_everywhere(links, x):
    if links.planar:
        x = sum([x] + [links.along(x, bit) for bit in (1, 2, 3)])
        return sum([x] + [links.back(x, k) for k in (1, 2, 3)])
    return lax.psum(x, ("dp", "tensor"))


def norm_low(x, gain):
    inverse = lax.rsqrt(jnp.mean(x * x, axis=-1, keepdims=True) + EPS)
    return (x * inverse * gain).astype(BF)


def per_device(
    tokens,
    segment_ids,
    cotangent,
    query_weight,
    key_weight,
    value_weight,
    output_weight,
    gate_weight,
    up_weight,
    down_weight,
    attn_gain,
    mlp_gain,
):
    links = Links()
    T, DP, s = links.T, links.DP, links.s
    seq = segment_ids.shape[1]
    length, width = tokens.shape[1:]
    cols = query_weight.shape[2]
    hidden = gate_weight.shape[2] // 2
    meta = links.table()

    half = HEAD // 2
    frequency = np.float32(ROPE_BASE) ** (-np.arange(half, dtype=np.float32) / np.float32(half))
    angles = np.arange(seq, dtype=np.float32)[:, None] * frequency[None, :].astype(np.float32)
    cosine, sine = np.cos(angles), np.sin(angles)
    tables = (
        jnp.asarray(np.concatenate([cosine] * 4, axis=1), F32),
        jnp.asarray(np.concatenate([-sine, sine, -sine, sine], axis=1), F32),
    )
    segments = lax.dynamic_index_in_dim(segment_ids, links.r, 0, keepdims=False)
    lane = jnp.arange(256, dtype=jnp.int32)[None, :]
    place = jnp.where(lane < 128, lane - HEAD, lane - 128)
    same = segments[:, None] == place
    in_seg = (place >= 0) & (place < 4)
    ext_q = jnp.where(in_seg & ~same, -BIG, 0.0).astype(BF)
    ext_k = jnp.where((in_seg & same) | ((place >= 4) & (place < 7)), 1.0, 0.0).astype(BF)

    own_gains = jnp.concatenate([attn_gain, mlp_gain])
    other_gains = links.sibling(own_gains)
    gains = [
        jnp.where(s == layer, own_gains, other_gains) for layer in range(2)
    ]
    def flat(item):
        return item.reshape(2 * length, width)

    def blocked(item):
        return item.reshape(2, length, width)

    planar = links.planar
    order = list(range(1, T)) + [0]
    batches = [order[: T // 2], order[T // 2 :]]
    out_rows = cols // 2
    rows = 3 * hidden

    x = flat(links.swap_end(tokens, links.swap_blocks(tokens)))
    a = norm_low(x.astype(F32), gains[0][0:1])
    gather = Gather(links, output_weight[0], gate_weight[0], up_weight[0], down_weight[0])
    weights = gather.weights
    projection = Projection(links, query_weight[0], key_weight[0], value_weight[0])
    w_proj = [projection.layer(0), None]
    if planar:
        early = projection.early
        w_proj[1] = projection.layer(1)
        first = gather.step(0, x, *early)
        rings = first[0] + gather.step(0)[0] + gather.step(0)[0]
        begun = gather.step(1, x, *early)
    kept = []
    first_values = None
    for layer in range(2):
        gain_mlp = gains[layer][1:2]
        a_blocks = links.spread(blocked(a), *(begun[1] if planar and layer else []))
        deps = [[], [], [], []]
        if not planar:
            for _ in range(1, T):
                gather.step(layer)
            w_proj[1] = projection.layer(1)
        elif layer == 0:
            deps[1] = rings[:2]
            deps[3] = w_proj[1:]
            deps[2] = rings[2:] + first[1]
        else:
            deps[1] = gather.step(1, a_blocks.arrays[1])[0]
            gather.step(1)
        q, k, v = project(meta, a_blocks, w_proj[layer], tables, (ext_q, ext_k), first_values, deps[0])
        o_rel, q = attend(meta, q, k, v, T, deps[1])
        o_blocks = links.exchange(o_rel, length)
        p = output_forward(meta, o_blocks, weights[layer], width, deps[2])
        if layer:
            dy = flat(links.swap_end(cotangent, links.swap_blocks(cotangent)))
            deps[3] = [dy]
        y, h, b, *saved = mlp_forward(
            meta, x, p, links.sibling(p), gain_mlp, weights[layer], batches, hidden, out_rows, deps[3]
        )
        kept.append((x, a_blocks, q, k, v, o_rel, o_blocks, h, b, saved))
        if planar and layer == 0:
            y = hold(y, *begun[0])
        x = (h + (y.astype(F32) + links.sibling(y).astype(F32))).astype(BF)
        if layer == 0:
            a, first_values = norm_low(x.astype(F32), gains[1][0:1]), v
    last = x

    first_grad = None
    mlp_sums, out_sums, proj_sums, gain_sums, sums = [None] * 2, [None] * 2, [None] * 2, [None] * 2, [None] * 2
    for layer in (1, 0):
        gain_attn, gain_mlp = gains[layer][0:1], gains[layer][1:2]
        x, a_blocks, q, k, v, o_rel, o_blocks, h, b, saved = kept[layer]
        dy_low = dy.astype(BF)
        due = {name: [] for name in ("middle", "attend", "project")}
        before = sums[1] if planar and layer == 0 else None
        *parts, db = mlp_backward(meta, dy_low, b, saved, weights[layer], batches, out_rows, DP, [])
        if before:
            due["middle"] = passing
            due["attend"] = before.mlp.step(parts[0]) + before.star.step() + before.star.step() + before.star.step()
            due["attend"].append(activations)
        dh, mlp_gain_grad, do_rel, out_part = middle(
            meta, dy, db, links.sibling(db), h, gain_mlp, o_blocks, weights[layer], DP, due["middle"]
        )
        if planar:
            mine = sums[layer] = LayerSums(links, parts, out_part, rows, out_rows, order)
            begun = mine.first.begin() + mine.second.begin()
            if before:
                do_rel = hold(do_rel, *begun[:2])
        do_blocks = links.exchange(do_rel, length)
        if planar:
            due["attend"] = due["attend"] + begun[:2]
            due["project"] = begun[2:] + mine.first.finish(do_rel)
            if before:
                begun = begun + mine.out.begin()
                due["project"] = due["project"] + before.mlp.step(do_rel) + before.star.step(do_rel)
                due["project"] = due["project"] + before.proj_total(do_rel)
        if layer:
            sent = links.swap_blocks(blocked(last), parts[0])
            due["attend"] = due["attend"] + [sent]
        back = attend_back(meta, q, k, v, o_rel, do_blocks, tables, first_grad, due["attend"])
        if before:
            mine.second.finish(back[0])
            mine.out.finish(back[0])
            mine.mlp.step(back[0])
            mine.mlp.step(back[0])
        if layer == 1:
            first_grad = back[3]
        near, far, dw = project_back(meta, a_blocks, back[:3], w_proj[layer], DP, due["project"])
        da, sending, summed = links.combine(near, far)
        da = flat(da).astype(F32)
        part, attn_gain_grad = norm_back(x.astype(F32), gain_attn, da)
        gain_sums[layer] = jnp.concatenate([attn_gain_grad, mlp_gain_grad])
        dy = dh + part
        if planar:
            mine.proj = PlaneSum(links, dw)
            if before:
                for _ in range(3):
                    mine.star.step(sending)
                mine.proj.begin(sending)
                mine.mlp.step(summed)
                mine.proj.finish(summed)
            else:
                activations = links.swap_end(blocked(last), hold(sent, near))
                passing = mine.second.finish(sending) + mine.out.begin(sending) + mine.proj.begin(sending)
                passing = passing + mine.mlp.step(sending) + mine.mlp.step(sending)
                passing = passing + mine.out.finish(summed) + mine.proj.finish(summed)
        else:
            if layer:
                activations = links.swap_end(blocked(last), sent)
            running = None
            for part in parts:
                for n in range(T // 2):
                    term = part[:, n * rows : (n + 1) * rows]
                    running = term if running is None else add_low(term, links.ring(running))
            mlp_sums[layer] = lax.psum_scatter(running, "dp", scatter_dimension=0, tiled=True)[0]
            running = None
            for n in order:
                term = out_part[:, n * out_rows : (n + 1) * out_rows]
                running = term if running is None else add_low(term, links.ring(running))
            out_sums[layer] = lax.psum_scatter(running, "dp", scatter_dimension=0, tiled=True)[0]
            proj_sums[layer] = lax.psum_scatter(dw, "dp", scatter_dimension=0, tiled=True)[0]
    half_width = width // 2
    mine = lax.dynamic_slice_in_dim(blocked(dy), s * half_width, half_width, 2)
    give = lax.dynamic_index_in_dim(mine, 1 - links.r, 0, keepdims=False).astype(BF)
    got = links.across(give)
    input_grad = jnp.where((jnp.arange(2) == links.r)[:, None, None], mine, got.astype(F32)[None])
    if planar:
        sums[0].star.step(got)
        sums[0].mlp.step(got)
        sums[0].proj_total(got)
        mlp_sums = [item.mlp.total for item in sums]
        out_sums = [item.star.total for item in sums]
        proj_sums = [item.proj_sum for item in sums]
    halves = both_halves(links, [jnp.concatenate([mlp_sums[n], out_sums[n]]) for n in range(2)])
    joined = []
    for item in proj_sums:
        if out_rows % 128:
            item = item.reshape(-1, 3, 2, out_rows)
            sides = [item[:, :, e].reshape(-1, 3 * out_rows) for e in range(2)]
        else:
            sides = [item[:, : 3 * out_rows], item[:, 3 * out_rows :]]
        joined.append(add_low(sides[0], links.across(sides[1])))
    proj = [item.astype(F32) for item in both_halves(links, joined)]
    halves = [item.astype(F32) for item in halves]
    squares = sum(jnp.sum(item * item) for item in halves + proj)
    gain_mine = jnp.where(s == 0, gain_sums[0], gain_sums[1])
    line = jnp.where(jnp.arange(width)[None, :] == 0, squares, 0.0)
    summed = sum_everywhere(links, jnp.concatenate([gain_mine, line]))
    gain_total = summed[0:2]
    grad_norm = jnp.sqrt(summed[2, 0] + jnp.sum(gain_total * gain_total)).reshape(1)
    shard = width // (DP * T)
    gain_out = lax.dynamic_slice_in_dim(gain_total, (links.d * T + links.z) * shard, shard, 1)
    grads = [
        jnp.concatenate([item[m * hidden : (m + 1) * hidden] for item in halves]) for m in range(3)
    ]
    own_out = jnp.concatenate([item[rows:] for item in halves])
    own_proj = [
        jnp.concatenate([item[:, m * out_rows : (m + 1) * out_rows] for item in proj], axis=1) for m in range(3)
    ]
    return (
        activations,
        input_grad,
        own_proj[0][None],
        own_proj[1][None],
        own_proj[2][None],
        own_out[None],
        grads[0].T[None],
        grads[1].T[None],
        grads[2][None],
        gain_out[0:1],
        gain_out[1:2],
        grad_norm,
    )


def solution(mesh):
    return jax.shard_map(
        per_device,
        mesh=mesh,
        in_specs=(
            P("dp", "tensor", None),
            P("dp", None),
            P("dp", "tensor", None),
            P("section", None, "tensor"),
            P("section", None, "tensor"),
            P("section", None, "tensor"),
            P("section", "tensor", None),
            P("section", None, "tensor"),
            P("section", None, "tensor"),
            P("section", "tensor", None),
            P("section", None),
            P("section", None),
        ),
        out_specs=(
            P("dp", "tensor", None),
            P("dp", "tensor", "section"),
            P("section", "dp", "tensor"),
            P("section", "dp", "tensor"),
            P("section", "dp", "tensor"),
            P("section", "tensor", "dp"),
            P("section", "dp", "tensor"),
            P("section", "dp", "tensor"),
            P("section", "tensor", "dp"),
            P("section", ("dp", "tensor")),
            P("section", ("dp", "tensor")),
            P("section"),
        ),
        check_vma=False,
    )
```
